768 devices in a mesh: ctx: 96 (over x, z, y_lo), tp: 8 (over y_hi, core).
Axes of the slice: x: 4, y: 8 (y_hi: 4, y_lo: 2; y = y_hi * 2 + y_lo), z: 12, core: 2. Of those that a mesh axis runs over, the one named last changes fastest.
Arguments:
- queries: bfloat16 [12288, 4096], P('ctx', 'tp'), may hold values from -6 to 6
- keys: bfloat16 [12288, 4096], P('ctx', 'tp'), may hold values from -6 to 6
- values: bfloat16 [12288, 4096], P('ctx', 'tp'), may hold values from -6 to 6
- state_retention_log: float32 [32, 12288], P('tp', 'ctx'), may hold values from -0.1 to 0, as said below
- boundary: int32 [12288], P('ctx'), may hold values 0 or 1
- gain: float32 [4096], P('tp'), may hold values from 0.25 to 1.75
- w_out: bfloat16 [4096, 6144], P('tp'), may hold values from -0.09375 to 0.09375
Outputs:
- attended: bfloat16 [12288, 6144], P('ctx', 'tp')
The draws below stay inside these ranges and needn't reach their ends.
Inputs may be any that keep to these rules, and one draw needn't show every extreme that they name: `state_retention_log`: every entry is negative.
All inputs are finite; a program needn't handle non-finite values. No bound on the sum of `boundary` on one device may be relied on, other than what follows from the above.
Results may differ from the reference program's by a relative error of at most 0.0053.
Values sent between devices are 32-bit elements; how exact they have to be, the bound alone decides.
No kernel may reach another device: no remote copies, remote signals or barrier semaphores. Data moves between devices by JAX's collectives and lax.ppermute only.
A program may use at most 128 MiB of HBM per device.

```python
import math
import jax
import jax.numpy as jnp
from jax import lax

D = 6144
HEADS = 32
HEAD_DIM = 128
TOK_DEV = 128
TOKENS = 12288


reach_low_log = math.log(0.5)


reach_high_log = math.log(2.3)


def draw_state_retention_log(key, part):
    key = jax.random.fold_in(key, 17)
    key_order, key_jitter, key_reach, key_block, key_event = jax.random.split(key, 5)
    fast_count = max(1, HEADS // 4)
    medium_count = max(1, HEADS // 4)
    ranking = jax.random.permutation(key_order, HEADS)
    fast_heads = ranking < fast_count
    medium_heads = jnp.logical_and(ranking >= fast_count, ranking < fast_count + medium_count)
    jitter = jax.random.uniform(key_jitter, (HEADS,), jnp.float32, 0.8, 1.25)
    reach = jnp.exp(jax.random.uniform(key_reach, (HEADS,), jnp.float32, reach_low_log, reach_high_log))
    medium_rate = jnp.minimum(reach / TOK_DEV, 1.0 / 40.0)
    slow_rate = jitter * 0.3 / TOKENS
    head_rate = jnp.where(fast_heads, jitter / 40.0, jnp.where(medium_heads, medium_rate, slow_rate))
    block_count = TOKENS // TOK_DEV
    block_factor = jnp.exp(jax.random.uniform(key_block, (HEADS, block_count), jnp.float32, -0.6931, 0.6931))
    block_factor = jnp.repeat(block_factor, TOK_DEV, axis=1)
    event_factor = jax.random.uniform(key_event, (HEADS, TOKENS), jnp.float32, 0.5, 1.5)
    return (-(head_rate[:, None] * block_factor * event_factor)).astype(jnp.float32)


def touch_ends(entries, own_key, smallest, high):
    spot = [jax.random.randint(jax.random.fold_in(own_key, axis), (), 0, length) for axis, length in enumerate(entries.shape)]
    main_axis = entries.shape.index(max(entries.shape))
    beside = spot[:main_axis] + [(spot[main_axis] + 1) % entries.shape[main_axis]] + spot[main_axis + 1:]
    return entries.at[tuple(spot)].set(smallest).at[tuple(beside)].set(high)


def level_of(stream_key, dims, shards, smallest, high):
    factor_of = 1.0
    for axis_at, blocks in shards:
        steps = jax.random.uniform(jax.random.fold_in(jax.random.fold_in(stream_key, 6), axis_at), (blocks,), jnp.float32, smallest / len(shards), high / len(shards))
        factor_of = factor_of * jnp.repeat(jnp.exp(steps), dims[axis_at] // blocks).reshape((-1,) + (1,) * (len(dims) - 1 - axis_at))
    return factor_of


def bell_draw(stream_key, extent, deviation, most, cuts=(), held_as=jnp.bfloat16):
    entries = deviation * jax.random.normal(stream_key, extent, jnp.float32)
    if cuts:
        entries = entries * level_of(stream_key, extent, cuts, -0.22, 0.18)
    return jnp.clip(entries, -most, most).astype(held_as)


def setup_inputs(seed: int = 0) -> dict:
    key_of = jax.random.split(jax.random.key(seed), 8)
    queries = bell_draw(key_of[0], (TOKENS, HEADS * HEAD_DIM), 1.0, 6.0, ((0, 96), (1, 8)))
    keys = bell_draw(key_of[1], (TOKENS, HEADS * HEAD_DIM), 1.0, 6.0, ((0, 96), (1, 8)))
    values = bell_draw(key_of[2], (TOKENS, HEADS * HEAD_DIM), 1.0, 6.0, ((0, 96), (1, 8)))
    state_retention_log = draw_state_retention_log(jax.random.fold_in(key_of[7], 71), 0)
    boundary = touch_ends((jax.random.randint(key_of[4], (TOKENS,), 0, TOKENS // 3) < 1).astype(jnp.int32), jax.random.fold_in(key_of[4], 1), 0, 1)
    gain = jnp.clip(1.0 + 0.15 * jax.random.normal(key_of[5], (HEADS * HEAD_DIM,), jnp.float32), 0.25, 1.75)
    w_out = bell_draw(key_of[6], (HEADS * HEAD_DIM, D), (HEADS * HEAD_DIM) ** -0.5, 0.09375, ((0, 8),))
    return dict(queries=queries, keys=keys, values=values, state_retention_log=state_retention_log, boundary=boundary, gain=gain, w_out=w_out)


surge_log_factor = math.log(0.6)
highest = lax.Precision.HIGHEST

def reference(queries, keys, values, state_retention_log, boundary, gain, w_out):
    blocks = TOKENS // TOK_DEV
    retained_log_share = state_retention_log + surge_log_factor * boundary.astype(jnp.float32)[None, :]
    local_cum = jnp.cumsum(retained_log_share.reshape(HEADS, blocks, TOK_DEV), axis=2).transpose(1, 0, 2)
    block_end = local_cum[:, :, -1]

    def split_heads(array):
        return array.reshape(blocks, TOK_DEV, HEADS, HEAD_DIM)
    query_heads = split_heads(queries)
    key_heads = split_heads(keys)
    value_heads = split_heads(values)

    def block_states(inputs):
        key_block, value_block, cum_block, end_block = inputs
        key_wide = key_block.astype(jnp.float32)
        value_wide = value_block.astype(jnp.float32)
        toward_end = jnp.exp(end_block[None, :] - cum_block.T)[:, :, None]
        prefix_decay_factor = jnp.exp(cum_block.T)[:, :, None]
        forward_term = jnp.einsum('bhd,bhe->hde', key_wide * toward_end, value_wide, precision=highest)
        backward_term = jnp.einsum('bhd,bhe->hde', key_wide * prefix_decay_factor, value_wide, precision=highest)
        return (forward_term, backward_term)
    forward_terms, backward_terms = lax.map(block_states, (key_heads, value_heads, local_cum, block_end))
    decay = jnp.exp(block_end)

    def carry_step(state, inputs):
        factor, term = inputs
        return (factor[:, None, None] * state + term, state)
    zero_state = jnp.zeros((HEADS, HEAD_DIM, HEAD_DIM), jnp.float32)
    _, forward_states = lax.scan(carry_step, zero_state, (decay, forward_terms))
    _, backward_states = lax.scan(carry_step, zero_state, (decay, backward_terms), reverse=True)
    gain_heads = gain.reshape(HEADS, HEAD_DIM)

    def block_output(inputs):
        query_block, key_block, value_block, cum_block, end_block, state_fwd, state_bwd = inputs
        query_wide = query_block.astype(jnp.float32)
        key_wide = key_block.astype(jnp.float32)
        value_wide = value_block.astype(jnp.float32)
        attention_logits = jnp.einsum('thd,shd->hts', query_wide, key_wide, precision=highest)
        weight = jnp.exp(-jnp.abs(cum_block[:, :, None] - cum_block[:, None, :]))
        probs = lax.optimization_barrier((attention_logits * weight).astype(jnp.bfloat16)).astype(jnp.float32)
        intra = jnp.einsum('hts,shd->thd', probs, value_wide, precision=highest)
        cum_rows = cum_block.T
        ahead = jnp.exp(cum_rows)[:, :, None]
        behind = jnp.exp(end_block[None, :] - cum_rows)[:, :, None]
        inter = jnp.einsum('thd,hde->the', query_wide * ahead, state_fwd, precision=highest)
        inter = inter + jnp.einsum('thd,hde->the', query_wide * behind, state_bwd, precision=highest)
        total = intra + inter
        squared_average = lax.optimization_barrier(jnp.mean(total * total, axis=2, keepdims=True))
        normed = total * lax.rsqrt(squared_average + 1e-06) * gain_heads[None, :, :]
        return normed.astype(jnp.bfloat16).reshape(TOK_DEV, HEADS * HEAD_DIM)
    normed_all = lax.map(block_output, (query_heads, key_heads, value_heads, local_cum, block_end, forward_states, backward_states))
    normed_all = normed_all.reshape(TOKENS, HEADS * HEAD_DIM)
    return jnp.dot(normed_all, w_out, preferred_element_type=jnp.float32).astype(jnp.bfloat16)
```

```python
import functools
import math

import jax
import jax.numpy as jnp
import numpy as np
from jax import lax
from jax.experimental import pallas as pl
from jax.experimental.pallas import tpu as pltpu
from jax.sharding import PartitionSpec as P

HEAD_DIM = 128
EVENTS = 128
HEADS_DEV = 4
D = 6144
COLS = 768
PAIRS = 48
PIECES = PAIRS // HEADS_DEV
ROWS = 11
CHUNK = ROWS + 1
HEAD_ROWS = PIECES * CHUNK
PACKED = PAIRS * CHUNK
HALF = EVENTS // 2

surge_log_factor = math.log(0.6)
F32 = jnp.float32
BF16 = jnp.bfloat16
VMEM_LIMIT = 24 * 1024 * 1024

SIDE_GROUPS = [[2 * pair + side for pair in range(PAIRS)] for side in range(2)]
SIDE_SWAP = [(i, i ^ 1) for i in range(2 * PAIRS)]
CORE_SWAP = [(i, i ^ 1) for i in range(8)]
RING_UP = [(i, (i + 2) % 8) for i in range(8)]
RING_DOWN = [(i, (i - 2) % 8) for i in range(8)]


def piece_rows(piece):
    return min(ROWS, HEAD_DIM - ROWS * piece)


def call(kernel, outs, args, scalars=0, scratch=(), flops=0, moved=0):
    specs = [pl.BlockSpec(memory_space=pltpu.SMEM)] * scalars
    specs += [pl.BlockSpec(memory_space=pltpu.VMEM)] * (len(args) - scalars)
    return pl.pallas_call(
        kernel,
        out_shape=[jax.ShapeDtypeStruct(shape, dtype) for shape, dtype in outs],
        in_specs=specs,
        out_specs=[pl.BlockSpec(memory_space=pltpu.VMEM)] * len(outs),
        scratch_shapes=list(scratch),
        compiler_params=pltpu.CompilerParams(vmem_limit_bytes=VMEM_LIMIT),
        cost_estimate=pl.CostEstimate(flops=flops, bytes_accessed=moved, transcendentals=0),
    )(*args)


def event_sums(log_ref, boundary_ref):
    rate = log_ref[...] + surge_log_factor * boundary_ref[...].astype(F32)
    row = lax.broadcasted_iota(jnp.int32, (EVENTS, EVENTS), 0)
    column = lax.broadcasted_iota(jnp.int32, (EVENTS, EVENTS), 1)
    lower = (column <= row).astype(F32)
    upper = (row <= column).astype(F32)
    columns = lax.dot_general(
        lower, rate, (((1,), (1,)), ((), ())), precision=lax.Precision.HIGHEST, preferred_element_type=F32
    )
    return rate, columns, upper


def factors(side, columns):
    ends = columns[EVENTS - 1 : EVENTS, :]
    toward_end = jnp.exp(ends - columns)
    from_start = jnp.exp(columns)
    sent = jnp.where(side == 0, toward_end, from_start)
    kept = jnp.where(side == 0, from_start, toward_end)
    return ends, sent, kept


def halves(wide):
    high = wide.astype(BF16)
    low = (wide - high.astype(F32)).astype(BF16)
    return high, low


def terms_kernel(side_ref, key_ref, value_ref, log_ref, boundary_ref, sent_ref, kept_ref, decay_ref):
    _, columns, _ = event_sums(log_ref, boundary_ref)
    ends, sent, kept = factors(side_ref[0], columns)
    decay = jnp.exp(ends)
    sent_ref[...] = jnp.zeros_like(sent_ref)
    kept_ref[...] = jnp.zeros_like(kept_ref)
    for head in range(HEADS_DEV):
        lanes = slice(head * HEAD_DIM, (head + 1) * HEAD_DIM)
        value = value_ref[:, lanes].astype(F32)
        sides = halves(value * sent[:, head : head + 1]) + halves(value * kept[:, head : head + 1])
        product = lax.dot_general(
            key_ref[:, lanes],
            jnp.concatenate(sides, axis=1),
            (((0,), (0,)), ((), ())),
            preferred_element_type=F32,
        )
        sent_term = product[:, :128] + product[:, 128:256]
        kept_term = product[:, 256:384] + product[:, 384:]
        whole_row = jnp.broadcast_to(decay[:, head : head + 1], (1, HEAD_DIM))
        decay_ref[head : head + 1, :] = whole_row
        for piece in range(PIECES):
            count, first = piece_rows(piece), head * HEAD_ROWS + piece * CHUNK
            rows = slice(ROWS * piece, ROWS * piece + count)
            sent_ref[first : first + count, :] = sent_term[rows]
            kept_ref[first : first + count, :] = kept_term[rows]
            sent_ref[first + ROWS : first + CHUNK, :] = whole_row


def combine_kernel(kept_ref, got_ref, decay_ref, out_ref):
    for head in range(HEADS_DEV):
        rows = slice(head * HEAD_ROWS, (head + 1) * HEAD_ROWS)
        out_ref[rows, :] = kept_ref[rows, :] + decay_ref[head : head + 1, :] * got_ref[rows, :]


def scan_kernel(side_ref, term_ref, out_ref):
    def run(pairs):
        state = jnp.zeros((CHUNK, HEAD_DIM), F32)
        for pair in pairs:
            rows = slice(pair * CHUNK, (pair + 1) * CHUNK)
            out_ref[rows, :] = state
            term = term_ref[rows, :]
            state = term[ROWS:, :] * state + term

    @pl.when(side_ref[0] == 1)
    def _():
        run(range(PAIRS))

    @pl.when(side_ref[0] == 0)
    def _():
        run(range(PAIRS - 1, -1, -1))


def unpack(packed_ref, head):
    parts = []
    for piece in range(PIECES):
        first = head * HEAD_ROWS + piece * CHUNK
        parts.append(packed_ref[first : first + piece_rows(piece), :])
    return jnp.concatenate(parts, axis=0)


def times_state(query, state):
    product = jnp.dot(query, jnp.concatenate(halves(state), axis=1), preferred_element_type=F32)
    return product[:, :128] + product[:, 128:]


def inner_kernel(
    side_ref, query_ref, key_ref, value_ref, log_ref, boundary_ref, got_ref, own_ref, total_ref, factor_ref
):
    rate, columns, upper = event_sums(log_ref, boundary_ref)
    rows_cum = lax.dot_general(
        rate, upper, (((1,), (0,)), ((), ())), precision=lax.Precision.HIGHEST, preferred_element_type=F32
    )
    _, own, other = factors(side_ref[0], columns)
    for head in range(HEADS_DEV):
        lanes = slice(head * HEAD_DIM, (head + 1) * HEAD_DIM)
        query = query_ref[:, lanes]
        logits = lax.dot_general(
            query, key_ref[:, lanes], (((1,), (1,)), ((), ())), preferred_element_type=F32
        )
        weight = jnp.exp(-jnp.abs(columns[:, head : head + 1] - rows_cum[head : head + 1, :]))
        probs = (logits * weight).astype(BF16)
        intra = jnp.dot(probs, value_ref[:, lanes], preferred_element_type=F32)
        last = head * HEAD_ROWS + ROWS
        state = unpack(got_ref, head) + got_ref[last : last + 1, :] * unpack(own_ref, head)
        total_ref[:, lanes] = intra + own[:, head : head + 1] * times_state(query, state)
        factor_ref[:, lanes] = jnp.broadcast_to(other[:, head : head + 1], (EVENTS, HEAD_DIM))


def first_kernel(
    order_ref, query_ref, total_ref, factor_ref, other_ref, gain_ref, w_ref, normed_ref, send_ref, mine_ref
):
    step = pl.program_id(0)

    @pl.when(step == 0)
    def _():
        for head in range(HEADS_DEV):
            lanes = slice(head * HEAD_DIM, (head + 1) * HEAD_DIM)
            total = total_ref[:, lanes] + factor_ref[:, lanes] * times_state(
                query_ref[:, lanes], unpack(other_ref, head)
            )
            average = jnp.mean(total * total, axis=1, keepdims=True)
            scaled = total * lax.rsqrt(average + 1e-06) * gain_ref[:, lanes]
            normed_ref[:, lanes] = scaled.astype(BF16)
        send_ref[...] = jnp.dot(normed_ref[...], w_ref[...], preferred_element_type=F32)

    @pl.when(step == 1)
    def _():
        mine_ref[...] = jnp.dot(normed_ref[...], w_ref[...], preferred_element_type=F32)


def rest_kernel(order_ref, normed_ref, w_ref, send_ref, mine_ref):
    step = pl.program_id(0)
    product = jnp.dot(normed_ref[...], w_ref[...], preferred_element_type=F32)

    @pl.when(step < 3)
    def _():
        send_ref[0] = product

    @pl.when(step >= 3)
    def _():
        mine_ref[0] = product


def whole(shape):
    return pl.BlockSpec(shape, lambda step, order: (0,) * len(shape))


def project_first(order, query, total, factor, other, gain, w_out):
    spec = pltpu.PrefetchScalarGridSpec(
        num_scalar_prefetch=1,
        grid=(2,),
        in_specs=[
            whole(query.shape),
            whole(total.shape),
            whole(factor.shape),
            whole(other.shape),
            whole(gain.shape),
            pl.BlockSpec((w_out.shape[0], COLS), lambda step, order: (0, order[step])),
        ],
        out_specs=[whole((EVENTS, 512)), whole((EVENTS, COLS)), whole((EVENTS, COLS))],
    )
    return pl.pallas_call(
        first_kernel,
        grid_spec=spec,
        out_shape=[
            jax.ShapeDtypeStruct((EVENTS, 512), BF16),
            jax.ShapeDtypeStruct((EVENTS, COLS), F32),
            jax.ShapeDtypeStruct((EVENTS, COLS), F32),
        ],
        compiler_params=pltpu.CompilerParams(vmem_limit_bytes=VMEM_LIMIT),
        cost_estimate=pl.CostEstimate(flops=230_000_000, bytes_accessed=3_500_000, transcendentals=0),
    )(order, query, total, factor, other, gain, w_out)


def project_rest(order, normed, w_out):
    spec = pltpu.PrefetchScalarGridSpec(
        num_scalar_prefetch=1,
        grid=(6,),
        in_specs=[
            whole(normed.shape),
            pl.BlockSpec((w_out.shape[0], COLS), lambda step, order: (0, order[step])),
        ],
        out_specs=[
            pl.BlockSpec((1, EVENTS, COLS), lambda step, order: (jnp.minimum(step, 2), 0, 0)),
            pl.BlockSpec((1, EVENTS, COLS), lambda step, order: (jnp.maximum(step - 3, 0), 0, 0)),
        ],
    )
    return pl.pallas_call(
        rest_kernel,
        grid_spec=spec,
        out_shape=[
            jax.ShapeDtypeStruct((3, EVENTS, COLS), F32),
            jax.ShapeDtypeStruct((3, EVENTS, COLS), F32),
        ],
        compiler_params=pltpu.CompilerParams(vmem_limit_bytes=VMEM_LIMIT),
        cost_estimate=pl.CostEstimate(flops=604_000_000, bytes_accessed=7_500_000, transcendentals=0),
    )(order, normed, w_out)


def far_kernel(mine_ref, got_ref, top_ref, bottom_ref):
    top_ref[...] = mine_ref[:HALF] + got_ref[:HALF]
    bottom_ref[...] = mine_ref[HALF:] + got_ref[HALF:]


def near_kernel(mine_ref, got_ref, up_bottom_ref, down_top_ref, up_top_ref, down_bottom_ref, own_ref):
    up_bottom_ref[...] = mine_ref[0, HALF:] + got_ref[0, HALF:]
    down_top_ref[...] = mine_ref[1, :HALF] + got_ref[1, :HALF]
    up_top_ref[...] = mine_ref[0, :HALF] + got_ref[0, :HALF]
    down_bottom_ref[...] = mine_ref[1, HALF:] + got_ref[1, HALF:]
    own_ref[...] = mine_ref[2] + got_ref[2]


def relay_kernel(up_top_ref, from_below_ref, down_bottom_ref, from_above_ref, up_ref, down_ref):
    up_ref[...] = up_top_ref[...] + from_below_ref[...]
    down_ref[...] = down_bottom_ref[...] + from_above_ref[...]


def final_kernel(own_ref, top_a_ref, top_b_ref, bottom_a_ref, bottom_b_ref, out_ref):
    out_ref[:HALF] = (own_ref[:HALF] + (top_a_ref[...] + top_b_ref[...])).astype(BF16)
    out_ref[HALF:] = (own_ref[HALF:] + (bottom_a_ref[...] + bottom_b_ref[...])).astype(BF16)


def exchange_pieces(packed):
    pieces = packed.reshape(PAIRS, 3, 4, HEAD_DIM)
    pieces = lax.all_to_all(pieces, "ctx", 0, 0, axis_index_groups=SIDE_GROUPS)
    return pieces.reshape(PACKED, HEAD_DIM)


def body(queries, keys, values, state_retention_log, boundary, gain, w_out):
    side = (lax.axis_index("ctx") % 2).reshape(1)
    place = lax.axis_index("tp")
    ring, core = place // 2, place % 2
    blocks = [2 * ((ring + far) % 4) + c for far, c in ((2, 1 - core), (2, core))]
    first_order = jnp.stack(blocks).astype(jnp.int32)
    blocks = [2 * ((ring + far) % 4) + c for c in (1 - core, core) for far in (1, 3, 0)]
    rest_order = jnp.stack(blocks).astype(jnp.int32)
    boundary = boundary.reshape(1, EVENTS)
    gain = gain.reshape(1, 512)
    packed = ((PACKED, HEAD_DIM), F32)

    sent, kept, decay = call(
        terms_kernel,
        [packed, packed, ((HEADS_DEV, HEAD_DIM), F32)],
        (side, keys, values, state_retention_log, boundary),
        scalars=1,
        flops=70_000_000,
        moved=900_000,
    )
    got = lax.ppermute(sent, "ctx", SIDE_SWAP)
    (pair_terms,) = call(combine_kernel, [packed], (kept, got, decay), flops=200_000, moved=900_000)
    slices = exchange_pieces(pair_terms)
    (states,) = call(scan_kernel, [packed], (side, slices), scalars=1, flops=200_000, moved=600_000)
    own = exchange_pieces(states)
    other = lax.ppermute(own, "ctx", SIDE_SWAP)
    inner = ((EVENTS, 512), F32)
    total, factor = call(
        inner_kernel,
        [inner, inner],
        (side, queries, keys, values, state_retention_log, boundary, got, own),
        scalars=1,
        flops=100_000_000,
        moved=1_500_000,
    )
    normed, send, mine = project_first(first_order, queries, total, factor, other, gain, w_out)
    far_got = lax.ppermute(send, "tp", CORE_SWAP)
    near_send, near_mine = project_rest(rest_order, normed, w_out)
    half = ((HALF, COLS), F32)
    far_top, far_bottom = call(far_kernel, [half, half], (mine, far_got), moved=1_200_000)
    from_below = lax.ppermute(far_top, "tp", RING_UP)
    from_above = lax.ppermute(far_bottom, "tp", RING_DOWN)
    near_got = lax.ppermute(near_send, "tp", CORE_SWAP)
    up_bottom, down_top, up_top, down_bottom, own_sum = call(
        near_kernel, [half] * 4 + [((EVENTS, COLS), F32)], (near_mine, near_got), moved=3_600_000
    )
    bottom_a = lax.ppermute(up_bottom, "tp", RING_UP)
    top_a = lax.ppermute(down_top, "tp", RING_DOWN)
    up, down = call(
        relay_kernel, [half, half], (up_top, from_below, down_bottom, from_above), moved=1_200_000
    )
    top_b = lax.ppermute(up, "tp", RING_UP)
    bottom_b = lax.ppermute(down, "tp", RING_DOWN)
    (out,) = call(
        final_kernel,
        [((EVENTS, COLS), BF16)],
        (own_sum, top_a, top_b, bottom_a, bottom_b),
        moved=1_400_000,
    )
    return out


def solution(mesh):
    in_specs = (
        P("ctx", "tp"),
        P("ctx", "tp"),
        P("ctx", "tp"),
        P("tp", "ctx"),
        P("ctx"),
        P("tp"),
        P("tp", None),
    )
    out_specs = P("ctx", "tp")
    return jax.shard_map(body, mesh=mesh, in_specs=in_specs, out_specs=out_specs, check_vma=False)
```

```python
import math

import jax
import jax.numpy as jnp
from jax import lax
from jax.experimental import pallas as pl
from jax.experimental.pallas import tpu as pltpu
from jax.sharding import PartitionSpec as P

HEAD_DIM = 128
EVENTS = 128
HEADS_DEV = 4
D = 6144
COLS = 768
PAIRS = 48
PIECES = PAIRS // HEADS_DEV
ROWS = 11
CHUNK = ROWS + 1
HEAD_ROWS = PIECES * CHUNK
PACKED = PAIRS * CHUNK

surge_log_factor = math.log(0.6)
F32 = jnp.float32
BF16 = jnp.bfloat16
VMEM_LIMIT = 24 * 1024 * 1024
TERMS_LIMIT = 60_000_000
STAGE_LIMIT = 46 * 1024 * 1024

SIDE_GROUPS = [[2 * pair + side for pair in range(PAIRS)] for side in range(2)]
SIDE_SWAP = [(i, i ^ 1) for i in range(2 * PAIRS)]
CORE_SWAP = [(i, i ^ 1) for i in range(8)]
ONWARD = [(i, (i + (2 if i % 2 == 0 else 6)) % 8) for i in range(8)]
BACK = [(i, (i + (6 if i % 2 == 0 else 2)) % 8) for i in range(8)]


def piece_rows(piece):
    return min(ROWS, HEAD_DIM - ROWS * piece)


def call(kernel, outs, args, scalars=0, scratch=(), flops=0, moved=0, space=pltpu.VMEM, limit=VMEM_LIMIT):
    specs = [pl.BlockSpec(memory_space=pltpu.SMEM)] * scalars
    specs += [pl.BlockSpec(memory_space=space)] * (len(args) - scalars)
    return pl.pallas_call(
        kernel,
        out_shape=[jax.ShapeDtypeStruct(shape, dtype) for shape, dtype in outs],
        in_specs=specs,
        out_specs=[pl.BlockSpec(memory_space=pltpu.VMEM)] * len(outs),
        scratch_shapes=list(scratch),
        compiler_params=pltpu.CompilerParams(vmem_limit_bytes=limit),
        cost_estimate=pl.CostEstimate(flops=flops, bytes_accessed=moved, transcendentals=0),
    )(*args)


def event_sums(log_ref, boundary_ref):
    rate = log_ref[...] + surge_log_factor * boundary_ref[...].astype(F32)
    row = lax.broadcasted_iota(jnp.int32, (EVENTS, EVENTS), 0)
    column = lax.broadcasted_iota(jnp.int32, (EVENTS, EVENTS), 1)
    lower = (column <= row).astype(F32)
    upper = (row <= column).astype(F32)
    columns = lax.dot_general(
        lower, rate, (((1,), (1,)), ((), ())), precision=lax.Precision.HIGHEST, preferred_element_type=F32
    )
    return rate, columns, upper


def factors(side, columns):
    ends = columns[EVENTS - 1 : EVENTS, :]
    toward_end = jnp.exp(ends - columns)
    from_start = jnp.exp(columns)
    sent = jnp.where(side == 0, toward_end, from_start)
    kept = jnp.where(side == 0, from_start, toward_end)
    return ends, sent, kept


def halves(wide):
    high = wide.astype(BF16)
    low = (wide - high.astype(F32)).astype(BF16)
    return high, low


def terms_kernel(
    side_ref,
    key_hbm,
    value_hbm,
    log_hbm,
    boundary_hbm,
    sent_ref,
    kept_ref,
    decay_ref,
    key_ref,
    value_ref,
    log_ref,
    boundary_ref,
    sems,
):
    copies = [
        pltpu.make_async_copy(log_hbm, log_ref, sems.at[0]),
        pltpu.make_async_copy(boundary_hbm, boundary_ref, sems.at[1]),
        pltpu.make_async_copy(key_hbm, key_ref, sems.at[2]),
        pltpu.make_async_copy(value_hbm, value_ref, sems.at[3]),
    ]
    for copy in copies:
        copy.start()
    for copy in copies:
        copy.wait()
    _, columns, _ = event_sums(log_ref, boundary_ref)
    ends, sent, kept = factors(side_ref[0], columns)
    decay = jnp.exp(ends)
    sent_ref[...] = jnp.zeros_like(sent_ref)
    kept_ref[...] = jnp.zeros_like(kept_ref)
    for head in range(HEADS_DEV):
        lanes = slice(head * HEAD_DIM, (head + 1) * HEAD_DIM)
        value = value_ref[:, lanes].astype(F32)
        sides = halves(value * sent[:, head : head + 1]) + halves(value * kept[:, head : head + 1])
        product = lax.dot_general(
            key_ref[:, lanes],
            jnp.concatenate(sides, axis=1),
            (((0,), (0,)), ((), ())),
            preferred_element_type=F32,
        )
        sent_term = product[:, :128] + product[:, 128:256]
        kept_term = product[:, 256:384] + product[:, 384:]
        whole_row = jnp.broadcast_to(decay[:, head : head + 1], (1, HEAD_DIM))
        decay_ref[head : head + 1, :] = whole_row
        for piece in range(PIECES):
            count, first = piece_rows(piece), head * HEAD_ROWS + piece * CHUNK
            rows = slice(ROWS * piece, ROWS * piece + count)
            sent_ref[first : first + count, :] = sent_term[rows]
            kept_ref[first : first + count, :] = kept_term[rows]
            sent_ref[first + ROWS : first + CHUNK, :] = whole_row


def combine_kernel(kept_ref, got_ref, decay_ref, out_ref):
    for head in range(HEADS_DEV):
        rows = slice(head * HEAD_ROWS, (head + 1) * HEAD_ROWS)
        out_ref[rows, :] = kept_ref[rows, :] + decay_ref[head : head + 1, :] * got_ref[rows, :]


def scan_kernel(side_ref, term_ref, out_ref):
    def run(pairs):
        state = jnp.zeros((CHUNK, HEAD_DIM), F32)
        for pair in pairs:
            rows = slice(pair * CHUNK, (pair + 1) * CHUNK)
            out_ref[rows, :] = state
            term = term_ref[rows, :]
            state = term[ROWS:, :] * state + term

    @pl.when(side_ref[0] == 1)
    def _():
        run(range(PAIRS))

    @pl.when(side_ref[0] == 0)
    def _():
        run(range(PAIRS - 1, -1, -1))


def unpack(packed_ref, head):
    parts = []
    for piece in range(PIECES):
        first = head * HEAD_ROWS + piece * CHUNK
        parts.append(packed_ref[first : first + piece_rows(piece), :])
    return jnp.concatenate(parts, axis=0)


def times_state(query, state):
    product = jnp.dot(query, jnp.concatenate(halves(state), axis=1), preferred_element_type=F32)
    return product[:, :128] + product[:, 128:]


def inner_kernel(
    side_ref, query_ref, key_ref, value_ref, log_ref, boundary_ref, got_ref, own_ref, total_ref, factor_ref
):
    rate, columns, upper = event_sums(log_ref, boundary_ref)
    rows_cum = lax.dot_general(
        rate, upper, (((1,), (0,)), ((), ())), precision=lax.Precision.HIGHEST, preferred_element_type=F32
    )
    _, own, other = factors(side_ref[0], columns)
    for head in range(HEADS_DEV):
        lanes = slice(head * HEAD_DIM, (head + 1) * HEAD_DIM)
        query = query_ref[:, lanes]
        logits = lax.dot_general(
            query, key_ref[:, lanes], (((1,), (1,)), ((), ())), preferred_element_type=F32
        )
        weight = jnp.exp(-jnp.abs(columns[:, head : head + 1] - rows_cum[head : head + 1, :]))
        probs = (logits * weight).astype(BF16)
        intra = jnp.dot(probs, value_ref[:, lanes], preferred_element_type=F32)
        last = head * HEAD_ROWS + ROWS
        state = unpack(got_ref, head) + got_ref[last : last + 1, :] * unpack(own_ref, head)
        total_ref[:, lanes] = intra + own[:, head : head + 1] * times_state(query, state)
        factor_ref[:, lanes] = jnp.broadcast_to(other[:, head : head + 1], (EVENTS, HEAD_DIM))


def stage_kernel(w_hbm, staged_ref, sems):
    copies = [
        pltpu.make_async_copy(w_hbm.at[:, pl.ds(block * COLS, COLS)], staged_ref.at[block], sems.at[block])
        for block in range(D // COLS)
    ]
    for copy in copies:
        copy.start()
    for copy in copies:
        copy.wait()


def block_of(place, far, core):
    return 2 * (((place >> 1) + far) & 3) + core


def first_kernel(
    place_ref, query_ref, total_ref, factor_ref, other_ref, gain_ref, w_ref, normed_ref, send_ref, mine_ref
):
    for head in range(HEADS_DEV):
        lanes = slice(head * HEAD_DIM, (head + 1) * HEAD_DIM)
        total = total_ref[:, lanes] + factor_ref[:, lanes] * times_state(
            query_ref[:, lanes], unpack(other_ref, head)
        )
        average = jnp.mean(total * total, axis=1, keepdims=True)
        scaled = total * lax.rsqrt(average + 1e-06) * gain_ref[:, lanes]
        normed_ref[:, lanes] = scaled.astype(BF16)
    place = place_ref[0]
    core = place & 1
    normed = normed_ref[...]
    send_ref[...] = jnp.dot(normed, w_ref[block_of(place, 2, 1 - core)], preferred_element_type=F32)
    mine_ref[...] = jnp.dot(normed, w_ref[block_of(place, 2, core)], preferred_element_type=F32)


def rest_kernel(place_ref, normed_ref, w_ref, send_ref, mine_ref):
    place = place_ref[0]
    core = place & 1
    normed = normed_ref[...]
    for target_ref, whose in ((send_ref, 1 - core), (mine_ref, core)):
        for slot, far in enumerate((3 - 2 * whose, 1 + 2 * whose, 0)):
            target_ref[slot] = jnp.dot(
                normed, w_ref[block_of(place, far, whose)], preferred_element_type=F32
            )


def far_kernel(mine_ref, got_ref, out_ref):
    out_ref[...] = mine_ref[...] + got_ref[...]


def near_kernel(mine_ref, got_ref, behind_ref, ahead_ref, own_ref):
    behind_ref[...] = mine_ref[0] + got_ref[0]
    ahead_ref[...] = mine_ref[1] + got_ref[1]
    own_ref[...] = mine_ref[2] + got_ref[2]


def final_kernel(one_ref, two_ref, out_ref):
    out_ref[...] = (one_ref[...] + two_ref[...]).astype(BF16)


def exchange_pieces(packed):
    pieces = packed.reshape(PAIRS, 3, 4, HEAD_DIM)
    pieces = lax.all_to_all(pieces, "ctx", 0, 0, axis_index_groups=SIDE_GROUPS)
    return pieces.reshape(PACKED, HEAD_DIM)


def body(queries, keys, values, state_retention_log, boundary, gain, w_out):
    side = (lax.axis_index("ctx") & 1).reshape(1)
    place = lax.axis_index("tp").reshape(1)
    boundary = boundary.reshape(1, EVENTS)
    gain = gain.reshape(1, 512)
    packed = ((PACKED, HEAD_DIM), F32)

    sent, kept, decay = call(
        terms_kernel,
        [packed, packed, ((HEADS_DEV, HEAD_DIM), F32)],
        (side, keys, values, state_retention_log, boundary),
        scalars=1,
        scratch=[
            pltpu.VMEM((EVENTS, 512), BF16),
            pltpu.VMEM((EVENTS, 512), BF16),
            pltpu.VMEM((HEADS_DEV, EVENTS), F32),
            pltpu.VMEM((1, EVENTS), jnp.int32),
            pltpu.SemaphoreType.DMA((4,)),
        ],
        flops=70_000_000,
        moved=900_000,
        space=pltpu.HBM,
        limit=TERMS_LIMIT,
    )
    sent, w_out = lax.optimization_barrier((sent, w_out))
    got = lax.ppermute(sent, "ctx", SIDE_SWAP)
    (staged,) = call(
        stage_kernel,
        [((D // COLS, 512, COLS), BF16)],
        (w_out,),
        scratch=[pltpu.SemaphoreType.DMA((D // COLS,))],
        moved=12_600_000,
        space=pltpu.HBM,
        limit=STAGE_LIMIT,
    )
    got, staged = lax.optimization_barrier((got, staged))
    (pair_terms,) = call(combine_kernel, [packed], (kept, got, decay), flops=200_000, moved=900_000)
    slices = exchange_pieces(pair_terms)
    (states,) = call(scan_kernel, [packed], (side, slices), scalars=1, flops=200_000, moved=600_000)
    own = exchange_pieces(states)
    other = lax.ppermute(own, "ctx", SIDE_SWAP)
    inner = ((EVENTS, 512), F32)
    total, factor = call(
        inner_kernel,
        [inner, inner],
        (side, queries, keys, values, state_retention_log, boundary, got, own),
        scalars=1,
        flops=100_000_000,
        moved=1_500_000,
    )
    block = ((EVENTS, COLS), F32)
    three = ((3, EVENTS, COLS), F32)
    normed, send, mine = call(
        first_kernel,
        [((EVENTS, 512), BF16), block, block],
        (place, queries, total, factor, other, gain, staged),
        scalars=1,
        flops=230_000_000,
        moved=3_500_000,
    )
    far_got = lax.ppermute(send, "tp", CORE_SWAP)
    (far,) = call(far_kernel, [block], (mine, far_got), moved=1_200_000)
    near_send, near_mine = call(
        rest_kernel, [three, three], (place, normed, staged), scalars=1, flops=604_000_000, moved=7_500_000
    )
    far, near_send = lax.optimization_barrier((far, near_send))
    ahead_got = lax.ppermute(far, "tp", ONWARD)
    near_got = lax.ppermute(near_send, "tp", CORE_SWAP)
    behind, ahead, own_sum = call(near_kernel, [block] * 3, (near_mine, near_got), moved=3_600_000)
    one = lax.ppermute(behind, "tp", BACK)
    (passed,) = call(far_kernel, [block], (ahead, ahead_got), moved=1_200_000)
    two = lax.ppermute(passed, "tp", ONWARD)
    (own_and_one,) = call(far_kernel, [block], (own_sum, one), moved=1_200_000)
    (out,) = call(final_kernel, [((EVENTS, COLS), BF16)], (own_and_one, two), moved=1_000_000)
    return out


def solution(mesh):
    in_specs = (
        P("ctx", "tp"),
        P("ctx", "tp"),
        P("ctx", "tp"),
        P("tp", "ctx"),
        P("ctx"),
        P("tp"),
        P("tp", None),
    )
    out_specs = P("ctx", "tp")
    return jax.shard_map(body, mesh=mesh, in_specs=in_specs, out_specs=out_specs, check_vma=False)
```

```python
import math

import jax
import jax.numpy as jnp
from jax import lax
from jax.experimental import pallas as pl
from jax.experimental.pallas import tpu as pltpu
from jax.sharding import PartitionSpec as P

HEAD_DIM = 128
EVENTS = 128
HEADS_DEV = 4
D = 6144
COLS = 768
PAIRS = 48
PIECES = PAIRS // HEADS_DEV
ROWS = 11
CHUNK = ROWS + 1
HEAD_ROWS = PIECES * CHUNK
PACKED = PAIRS * CHUNK
RING = 4

surge_log_factor = math.log(0.6)
F32 = jnp.float32
BF16 = jnp.bfloat16
VMEM_LIMIT = 24 * 1024 * 1024

SIDE_GROUPS = [[2 * pair + side for pair in range(PAIRS)] for side in range(2)]
SIDE_SWAP = [(i, i ^ 1) for i in range(2 * PAIRS)]
CORE_SWAP = [(i, i ^ 1) for i in range(8)]
CORE_PAIRS = [[i, i + 1] for i in range(0, 8, 2)]
ONWARD = [(i, (i + (2 if i % 2 == 0 else 6)) % 8) for i in range(8)]
BACK = [(i, (i + (6 if i % 2 == 0 else 2)) % 8) for i in range(8)]


def piece_rows(piece):
    return min(ROWS, HEAD_DIM - ROWS * piece)


def call(kernel, outs, args, scalars=0, scratch=(), flops=0, moved=0, space=pltpu.VMEM, out_space=None):
    specs = [pl.BlockSpec(memory_space=pltpu.SMEM)] * scalars
    specs += [pl.BlockSpec(memory_space=space)] * (len(args) - scalars)
    if space is pltpu.HBM:
        args = args[:scalars] + tuple(pltpu.with_memory_space_constraint(x, space) for x in args[scalars:])
    shapes = [jax.ShapeDtypeStruct(shape, dtype) if out_space is None else out_space(shape, dtype) for shape, dtype in outs]
    return pl.pallas_call(
        kernel,
        out_shape=shapes,
        in_specs=specs,
        out_specs=[pl.BlockSpec(memory_space=out_space or pltpu.VMEM)] * len(outs),
        scratch_shapes=list(scratch),
        compiler_params=pltpu.CompilerParams(vmem_limit_bytes=VMEM_LIMIT),
        cost_estimate=pl.CostEstimate(flops=flops, bytes_accessed=moved, transcendentals=0),
    )(*args)


def event_sums(log_ref, boundary_ref):
    rate = log_ref[...] + surge_log_factor * boundary_ref[...].astype(F32)
    row = lax.broadcasted_iota(jnp.int32, (EVENTS, EVENTS), 0)
    column = lax.broadcasted_iota(jnp.int32, (EVENTS, EVENTS), 1)
    lower = (column <= row).astype(F32)
    upper = (row <= column).astype(F32)
    columns = lax.dot_general(
        lower, rate, (((1,), (1,)), ((), ())), precision=lax.Precision.HIGHEST, preferred_element_type=F32
    )
    return rate, columns, upper


def factors(side, columns):
    ends = columns[EVENTS - 1 : EVENTS, :]
    toward_end = jnp.exp(ends - columns)
    from_start = jnp.exp(columns)
    sent = jnp.where(side == 0, toward_end, from_start)
    kept = jnp.where(side == 0, from_start, toward_end)
    return ends, sent, kept


def halves(wide):
    high = wide.astype(BF16)
    low = (wide - high.astype(F32)).astype(BF16)
    return high, low


def terms_kernel(
    side_ref,
    key_hbm,
    value_hbm,
    log_hbm,
    boundary_hbm,
    sent_ref,
    kept_ref,
    decay_ref,
    key_ref,
    value_ref,
    log_ref,
    boundary_ref,
    sems,
):
    copies = [
        pltpu.make_async_copy(log_hbm, log_ref, sems.at[0]),
        pltpu.make_async_copy(boundary_hbm, boundary_ref, sems.at[1]),
        pltpu.make_async_copy(key_hbm, key_ref, sems.at[2]),
        pltpu.make_async_copy(value_hbm, value_ref, sems.at[3]),
    ]
    for copy in copies:
        copy.start()
    for copy in copies:
        copy.wait()
    _, columns, _ = event_sums(log_ref, boundary_ref)
    ends, sent, kept = factors(side_ref[0], columns)
    decay = jnp.exp(ends)
    sent_ref[...] = jnp.zeros_like(sent_ref)
    kept_ref[...] = jnp.zeros_like(kept_ref)
    for head in range(HEADS_DEV):
        lanes = slice(head * HEAD_DIM, (head + 1) * HEAD_DIM)
        value = value_ref[:, lanes].astype(F32)
        sides = halves(value * sent[:, head : head + 1]) + halves(value * kept[:, head : head + 1])
        product = lax.dot_general(
            key_ref[:, lanes],
            jnp.concatenate(sides, axis=1),
            (((0,), (0,)), ((), ())),
            preferred_element_type=F32,
        )
        sent_term = product[:, :128] + product[:, 128:256]
        kept_term = product[:, 256:384] + product[:, 384:]
        whole_row = jnp.broadcast_to(decay[:, head : head + 1], (1, HEAD_DIM))
        decay_ref[head : head + 1, :] = whole_row
        for piece in range(PIECES):
            count, first = piece_rows(piece), head * HEAD_ROWS + piece * CHUNK
            rows = slice(ROWS * piece, ROWS * piece + count)
            sent_ref[first : first + count, :] = sent_term[rows]
            kept_ref[first : first + count, :] = kept_term[rows]
            sent_ref[first + ROWS : first + CHUNK, :] = whole_row


def combine_kernel(kept_ref, got_ref, decay_ref, out_ref):
    for head in range(HEADS_DEV):
        rows = slice(head * HEAD_ROWS, (head + 1) * HEAD_ROWS)
        out_ref[rows, :] = kept_ref[rows, :] + decay_ref[head : head + 1, :] * got_ref[rows, :]


def scan_kernel(side_ref, term_ref, out_ref):
    def run(pairs):
        state = jnp.zeros((CHUNK, HEAD_DIM), F32)
        for pair in pairs:
            rows = slice(pair * CHUNK, (pair + 1) * CHUNK)
            out_ref[rows, :] = state
            term = term_ref[rows, :]
            state = term[ROWS:, :] * state + term

    @pl.when(side_ref[0] == 1)
    def _():
        run(range(PAIRS))

    @pl.when(side_ref[0] == 0)
    def _():
        run(range(PAIRS - 1, -1, -1))


def unpack(packed_ref, head):
    parts = []
    for piece in range(PIECES):
        first = head * HEAD_ROWS + piece * CHUNK
        parts.append(packed_ref[first : first + piece_rows(piece), :])
    return jnp.concatenate(parts, axis=0)


def times_state(query, state):
    product = jnp.dot(query, jnp.concatenate(halves(state), axis=1), preferred_element_type=F32)
    return product[:, :128] + product[:, 128:]


def inner_kernel(
    side_ref, query_ref, key_ref, value_ref, log_ref, boundary_ref, got_ref, own_ref, total_ref, factor_ref
):
    rate, columns, upper = event_sums(log_ref, boundary_ref)
    rows_cum = lax.dot_general(
        rate, upper, (((1,), (0,)), ((), ())), precision=lax.Precision.HIGHEST, preferred_element_type=F32
    )
    _, own, other = factors(side_ref[0], columns)
    for head in range(HEADS_DEV):
        lanes = slice(head * HEAD_DIM, (head + 1) * HEAD_DIM)
        query = query_ref[:, lanes]
        logits = lax.dot_general(
            query, key_ref[:, lanes], (((1,), (1,)), ((), ())), preferred_element_type=F32
        )
        weight = jnp.exp(-jnp.abs(columns[:, head : head + 1] - rows_cum[head : head + 1, :]))
        probs = (logits * weight).astype(BF16)
        intra = jnp.dot(probs, value_ref[:, lanes], preferred_element_type=F32)
        last = head * HEAD_ROWS + ROWS
        state = unpack(got_ref, head) + got_ref[last : last + 1, :] * unpack(own_ref, head)
        total_ref[:, lanes] = intra + own[:, head : head + 1] * times_state(query, state)
        factor_ref[:, lanes] = jnp.broadcast_to(other[:, head : head + 1], (EVENTS, HEAD_DIM))


def widen_kernel(place_ref, w_ref, wide_ref):
    wide_ref[0] = w_ref[...].astype(F32)


def widen_partner_columns(place, w_out):
    rows = w_out.shape[0] // 2
    spec = pltpu.PrefetchScalarGridSpec(
        num_scalar_prefetch=1,
        grid=(RING, 2),
        in_specs=[pl.BlockSpec((rows, COLS), lambda t, r, place: (r, 2 * t + 1 - (place[0] & 1)))],
        out_specs=pl.BlockSpec((1, rows, COLS), lambda t, r, place: (t, r, 0)),
    )
    return pl.pallas_call(
        widen_kernel,
        grid_spec=spec,
        out_shape=pltpu.HBM((RING, w_out.shape[0], COLS), F32),
        compiler_params=pltpu.CompilerParams(vmem_limit_bytes=VMEM_LIMIT),
        cost_estimate=pl.CostEstimate(flops=0, bytes_accessed=9_500_000, transcendentals=0),
    )(place, pltpu.with_memory_space_constraint(w_out, pltpu.HBM))


def stage_kernel(place_ref, w_hbm, wide_hbm, staged_ref, wide_ref, sems):
    rows = w_hbm.shape[0]
    core = place_ref[0] & 1
    arriving, owned = [], []
    for t in range(RING):
        arriving.append(pltpu.make_async_copy(wide_hbm.at[1 - core, t], wide_ref.at[t], sems.at[t]))
        columns = pl.ds(pl.multiple_of((2 * t + core) * COLS, COLS), COLS)
        owned.append(
            pltpu.make_async_copy(
                w_hbm.at[:, columns], staged_ref.at[t, pl.ds(0, rows)], sems.at[RING + t]
            )
        )
    for copy in arriving + owned:
        copy.start()
    for t in range(RING):
        arriving[t].wait()
        staged_ref[t, rows:, :] = wide_ref[t].astype(BF16)
    for copy in owned:
        copy.wait()


def normed_kernel(query_ref, total_ref, factor_ref, other_ref, gain_ref, normed_ref):
    for head in range(HEADS_DEV):
        lanes = slice(head * HEAD_DIM, (head + 1) * HEAD_DIM)
        total = total_ref[:, lanes] + factor_ref[:, lanes] * times_state(
            query_ref[:, lanes], unpack(other_ref, head)
        )
        average = jnp.mean(total * total, axis=1, keepdims=True)
        scaled = total * lax.rsqrt(average + 1e-06) * gain_ref[:, lanes]
        normed_ref[:, lanes] = scaled.astype(BF16).astype(F32)


def project(place_ref, own_ref, got_ref, w_ref, out_refs, fars):
    place = place_ref[0]
    normed = jnp.concatenate([own_ref[...].astype(BF16), got_ref[...].astype(BF16)], axis=1)
    for out_ref, far in zip(out_refs, fars):
        block = ((place >> 1) + far) & 3
        out_ref[...] = jnp.dot(normed, w_ref[block], preferred_element_type=F32)


def opposite_kernel(place_ref, own_ref, got_ref, w_ref, out_ref):
    project(place_ref, own_ref, got_ref, w_ref, [out_ref], [2])


def rest_kernel(place_ref, own_ref, got_ref, w_ref, behind_ref, ahead_ref, mine_ref):
    core = place_ref[0] & 1
    project(
        place_ref, own_ref, got_ref, w_ref, [behind_ref, ahead_ref, mine_ref], [3 - 2 * core, 1 + 2 * core, 0]
    )


def far_kernel(mine_ref, got_ref, out_ref):
    out_ref[...] = mine_ref[...] + got_ref[...]


def final_kernel(one_ref, two_ref, out_ref):
    out_ref[...] = (one_ref[...] + two_ref[...]).astype(BF16)


def exchange_pieces(packed):
    pieces = packed.reshape(PAIRS, 3, 4, HEAD_DIM)
    pieces = lax.all_to_all(pieces, "ctx", 0, 0, axis_index_groups=SIDE_GROUPS)
    return pieces.reshape(PACKED, HEAD_DIM)


def body(queries, keys, values, state_retention_log, boundary, gain, w_out):
    side = (lax.axis_index("ctx") & 1).reshape(1)
    place = lax.axis_index("tp").reshape(1)
    boundary = boundary.reshape(1, EVENTS)
    gain = gain.reshape(1, 512)
    packed = ((PACKED, HEAD_DIM), F32)

    sent, kept, decay = call(
        terms_kernel,
        [packed, packed, ((HEADS_DEV, HEAD_DIM), F32)],
        (side, keys, values, state_retention_log, boundary),
        scalars=1,
        scratch=[
            pltpu.VMEM((EVENTS, 512), BF16),
            pltpu.VMEM((EVENTS, 512), BF16),
            pltpu.VMEM((HEADS_DEV, EVENTS), F32),
            pltpu.VMEM((1, EVENTS), jnp.int32),
            pltpu.SemaphoreType.DMA((4,)),
        ],
        flops=70_000_000,
        moved=900_000,
        space=pltpu.HBM,
        out_space=pltpu.VMEM,
    )
    sent, w_late = lax.optimization_barrier((sent, w_out))
    got = lax.ppermute(sent, "ctx", SIDE_SWAP)
    wide = widen_partner_columns(place, w_late)
    got, wide = lax.optimization_barrier((got, wide))
    wide_both = lax.all_gather(wide, "tp", axis_index_groups=CORE_PAIRS)
    (pair_terms,) = call(combine_kernel, [packed], (kept, got, decay), flops=200_000, moved=900_000)
    slices = exchange_pieces(pair_terms)
    (states,) = call(scan_kernel, [packed], (side, slices), scalars=1, flops=200_000, moved=600_000)
    own = exchange_pieces(states)
    own, w_late = lax.optimization_barrier((own, w_late))
    other = lax.ppermute(own, "ctx", SIDE_SWAP)
    (staged,) = call(
        stage_kernel,
        [((RING, 1024, COLS), BF16)],
        (place, w_late, wide_both),
        scalars=1,
        scratch=[
            pltpu.VMEM((RING, 512, COLS), F32),
            pltpu.SemaphoreType.DMA((2 * RING,)),
        ],
        moved=16_000_000,
        space=pltpu.HBM,
        out_space=pltpu.VMEM,
    )
    other, staged = lax.optimization_barrier((other, staged))
    inner = ((EVENTS, 512), F32)
    total, factor = call(
        inner_kernel,
        [inner, inner],
        (side, queries, keys, values, state_retention_log, boundary, got, own),
        scalars=1,
        flops=100_000_000,
        moved=1_500_000,
    )
    block = ((EVENTS, COLS), F32)
    (normed,) = call(
        normed_kernel,
        [inner],
        (queries, total, factor, other, gain),
        flops=70_000_000,
        moved=1_300_000,
    )
    normed_got = lax.ppermute(normed, "tp", CORE_SWAP)
    (opposite,) = call(
        opposite_kernel,
        [block],
        (place, normed, normed_got, staged),
        scalars=1,
        flops=200_000_000,
        moved=2_500_000,
    )
    ahead_got = lax.ppermute(opposite, "tp", ONWARD)
    behind, ahead, own_sum = call(
        rest_kernel,
        [block] * 3,
        (place, normed, normed_got, staged),
        scalars=1,
        flops=600_000_000,
        moved=6_000_000,
    )
    one = lax.ppermute(behind, "tp", BACK)
    (passed,) = call(far_kernel, [block], (ahead, ahead_got), moved=1_200_000)
    two = lax.ppermute(passed, "tp", ONWARD)
    (own_and_one,) = call(far_kernel, [block], (own_sum, one), moved=1_200_000)
    (out,) = call(final_kernel, [((EVENTS, COLS), BF16)], (own_and_one, two), moved=1_000_000)
    return out


def solution(mesh):
    in_specs = (
        P("ctx", "tp"),
        P("ctx", "tp"),
        P("ctx", "tp"),
        P("tp", "ctx"),
        P("ctx"),
        P("tp"),
        P("tp", None),
    )
    out_specs = P("ctx", "tp")
    return jax.shard_map(body, mesh=mesh, in_specs=in_specs, out_specs=out_specs, check_vma=False)
```

```python
import math

import jax
import jax.numpy as jnp
from jax import lax
from jax.experimental import pallas as pl
from jax.experimental.pallas import tpu as pltpu
from jax.sharding import PartitionSpec as P

HEAD_DIM = 128
EVENTS = 128
HEADS_DEV = 4
D = 6144
COLS = 768
PAIRS = 48
PIECES = PAIRS // HEADS_DEV
ROWS = 11
CHUNK = ROWS + 1
HEAD_ROWS = PIECES * CHUNK
PACKED = PAIRS * CHUNK

surge_log_factor = math.log(0.6)
F32 = jnp.float32
BF16 = jnp.bfloat16
VMEM_LIMIT = 24 * 1024 * 1024

SIDE_GROUPS = [[2 * pair + side for pair in range(PAIRS)] for side in range(2)]
SIDE_SWAP = [(i, i ^ 1) for i in range(2 * PAIRS)]
SIDE_PAIRS = [[i, i + 1] for i in range(0, 2 * PAIRS, 2)]
CORE_SWAP = [(i, i ^ 1) for i in range(8)]
CORE_PAIRS = [[i, i + 1] for i in range(0, 8, 2)]
ONWARD = [(i, (i + (2 if i % 2 == 0 else 6)) % 8) for i in range(8)]
BACK = [(i, (i + (6 if i % 2 == 0 else 2)) % 8) for i in range(8)]


def piece_rows(piece):
    return min(ROWS, HEAD_DIM - ROWS * piece)


def call(kernel, outs, args, scalars=0, scratch=(), flops=0, moved=0, space=pltpu.VMEM, out_space=None):
    specs = [pl.BlockSpec(memory_space=pltpu.SMEM)] * scalars
    specs += [pl.BlockSpec(memory_space=space)] * (len(args) - scalars)
    if space is pltpu.HBM:
        args = args[:scalars] + tuple(pltpu.with_memory_space_constraint(x, space) for x in args[scalars:])
    shapes = [(out_space or jax.ShapeDtypeStruct)(shape, dtype) for shape, dtype in outs]
    return pl.pallas_call(
        kernel,
        out_shape=shapes,
        in_specs=specs,
        out_specs=[pl.BlockSpec(memory_space=out_space or pltpu.VMEM)] * len(outs),
        scratch_shapes=list(scratch),
        compiler_params=pltpu.CompilerParams(vmem_limit_bytes=VMEM_LIMIT),
        cost_estimate=pl.CostEstimate(flops=flops, bytes_accessed=moved, transcendentals=0),
    )(*args)


def event_sums(log_ref, boundary_ref):
    rate = log_ref[...] + surge_log_factor * boundary_ref[...].astype(F32)
    row = lax.broadcasted_iota(jnp.int32, (EVENTS, EVENTS), 0)
    column = lax.broadcasted_iota(jnp.int32, (EVENTS, EVENTS), 1)
    lower = (column <= row).astype(F32)
    upper = (row <= column).astype(F32)
    columns = lax.dot_general(
        lower, rate, (((1,), (1,)), ((), ())), precision=lax.Precision.HIGHEST, preferred_element_type=F32
    )
    return rate, columns, upper


def factors(side, columns):
    ends = columns[EVENTS - 1 : EVENTS, :]
    toward_end = jnp.exp(ends - columns)
    from_start = jnp.exp(columns)
    sent = jnp.where(side == 0, toward_end, from_start)
    kept = jnp.where(side == 0, from_start, toward_end)
    return ends, sent, kept


def halves(wide):
    high = wide.astype(BF16)
    low = (wide - high.astype(F32)).astype(BF16)
    return high, low


def terms_kernel(
    side_ref,
    key_hbm,
    value_hbm,
    log_hbm,
    boundary_hbm,
    sent_ref,
    kept_ref,
    decay_ref,
    key_ref,
    value_ref,
    log_ref,
    boundary_ref,
    sems,
):
    copies = [
        pltpu.make_async_copy(log_hbm, log_ref, sems.at[0]),
        pltpu.make_async_copy(boundary_hbm, boundary_ref, sems.at[1]),
        pltpu.make_async_copy(key_hbm, key_ref, sems.at[2]),
        pltpu.make_async_copy(value_hbm, value_ref, sems.at[3]),
    ]
    for copy in copies:
        copy.start()
    for copy in copies:
        copy.wait()
    _, columns, _ = event_sums(log_ref, boundary_ref)
    ends, sent, kept = factors(side_ref[0], columns)
    decay = jnp.exp(ends)
    sent_ref[...] = jnp.zeros_like(sent_ref)
    kept_ref[...] = jnp.zeros_like(kept_ref)
    for head in range(HEADS_DEV):
        lanes = slice(head * HEAD_DIM, (head + 1) * HEAD_DIM)
        value = value_ref[:, lanes].astype(F32)
        sides = halves(value * sent[:, head : head + 1]) + halves(value * kept[:, head : head + 1])
        product = lax.dot_general(
            key_ref[:, lanes],
            jnp.concatenate(sides, axis=1),
            (((0,), (0,)), ((), ())),
            preferred_element_type=F32,
        )
        sent_term = product[:, :128] + product[:, 128:256]
        kept_term = product[:, 256:384] + product[:, 384:]
        whole_row = jnp.broadcast_to(decay[:, head : head + 1], (1, HEAD_DIM))
        decay_ref[head : head + 1, :] = whole_row
        for piece in range(PIECES):
            count, first = piece_rows(piece), head * HEAD_ROWS + piece * CHUNK
            rows = slice(ROWS * piece, ROWS * piece + count)
            sent_ref[first : first + count, :] = sent_term[rows]
            kept_ref[first : first + count, :] = kept_term[rows]
            sent_ref[first + ROWS : first + CHUNK, :] = whole_row


def combine_kernel(side_ref, kept_ref, both_ref, decay_ref, out_ref, got_ref):
    got_ref[...] = both_ref[1 - side_ref[0]]
    for head in range(HEADS_DEV):
        rows = slice(head * HEAD_ROWS, (head + 1) * HEAD_ROWS)
        out_ref[rows, :] = kept_ref[rows, :] + decay_ref[head : head + 1, :] * got_ref[rows, :]


def scan_kernel(side_ref, term_ref, out_ref):
    def run(pairs):
        state = jnp.zeros((CHUNK, HEAD_DIM), F32)
        for pair in pairs:
            rows = slice(pair * CHUNK, (pair + 1) * CHUNK)
            out_ref[rows, :] = state
            term = term_ref[rows, :]
            state = term[ROWS:, :] * state + term

    @pl.when(side_ref[0] == 1)
    def _():
        run(range(PAIRS))

    @pl.when(side_ref[0] == 0)
    def _():
        run(range(PAIRS - 1, -1, -1))


def unpack(packed_ref, head):
    parts = []
    for piece in range(PIECES):
        first = head * HEAD_ROWS + piece * CHUNK
        parts.append(packed_ref[first : first + piece_rows(piece), :])
    return jnp.concatenate(parts, axis=0)


def times_state(query, state):
    product = jnp.dot(query, jnp.concatenate(halves(state), axis=1), preferred_element_type=F32)
    return product[:, :128] + product[:, 128:]


def inner_kernel(
    side_ref, query_ref, key_ref, value_ref, log_ref, boundary_ref, got_ref, own_ref, total_ref, factor_ref
):
    rate, columns, upper = event_sums(log_ref, boundary_ref)
    rows_cum = lax.dot_general(
        rate, upper, (((1,), (0,)), ((), ())), precision=lax.Precision.HIGHEST, preferred_element_type=F32
    )
    _, own, other = factors(side_ref[0], columns)
    for head in range(HEADS_DEV):
        lanes = slice(head * HEAD_DIM, (head + 1) * HEAD_DIM)
        query = query_ref[:, lanes]
        logits = lax.dot_general(
            query, key_ref[:, lanes], (((1,), (1,)), ((), ())), preferred_element_type=F32
        )
        weight = jnp.exp(-jnp.abs(columns[:, head : head + 1] - rows_cum[head : head + 1, :]))
        probs = (logits * weight).astype(BF16)
        intra = jnp.dot(probs, value_ref[:, lanes], preferred_element_type=F32)
        last = head * HEAD_ROWS + ROWS
        state = unpack(got_ref, head) + got_ref[last : last + 1, :] * unpack(own_ref, head)
        total_ref[:, lanes] = intra + own[:, head : head + 1] * times_state(query, state)
        factor_ref[:, lanes] = jnp.broadcast_to(other[:, head : head + 1], (EVENTS, HEAD_DIM))


def stage_kernel(w_hbm, staged_ref, sems):
    copies = [
        pltpu.make_async_copy(w_hbm.at[:, pl.ds(block * COLS, COLS)], staged_ref.at[block], sems.at[block])
        for block in range(D // COLS)
    ]
    for copy in copies:
        copy.start()
    for copy in copies:
        copy.wait()


def block_of(place, far, core):
    return 2 * (((place >> 1) + far) & 3) + core


def first_kernel(
    place_ref,
    query_ref,
    total_ref,
    factor_ref,
    other_ref,
    gain_ref,
    w_ref,
    normed_ref,
    opposite_send_ref,
    opposite_ref,
    behind_send_ref,
    behind_ref,
):
    for head in range(HEADS_DEV):
        lanes = slice(head * HEAD_DIM, (head + 1) * HEAD_DIM)
        total = total_ref[:, lanes] + factor_ref[:, lanes] * times_state(
            query_ref[:, lanes], unpack(other_ref, head)
        )
        average = jnp.mean(total * total, axis=1, keepdims=True)
        scaled = total * lax.rsqrt(average + 1e-06) * gain_ref[:, lanes]
        normed_ref[:, lanes] = scaled.astype(BF16)
    place = place_ref[0]
    core = place & 1
    normed = normed_ref[...]
    for out_ref, far, whose in (
        (opposite_send_ref, 2, 1 - core),
        (opposite_ref, 2, core),
        (behind_send_ref, 1 + 2 * core, 1 - core),
        (behind_ref, 3 - 2 * core, core),
    ):
        out_ref[...] = jnp.dot(normed, w_ref[block_of(place, far, whose)], preferred_element_type=F32)


def rest_kernel(place_ref, normed_ref, w_ref, ahead_send_ref, ahead_ref, own_send_ref, own_ref):
    place = place_ref[0]
    core = place & 1
    normed = normed_ref[...]
    for out_ref, far, whose in (
        (ahead_send_ref, 3 - 2 * core, 1 - core),
        (ahead_ref, 1 + 2 * core, core),
        (own_send_ref, 0, 1 - core),
        (own_ref, 0, core),
    ):
        out_ref[...] = jnp.dot(normed, w_ref[block_of(place, far, whose)], preferred_element_type=F32)


def core_sum_kernel(place_ref, mine_ref, both_ref, out_ref):
    out_ref[...] = mine_ref[...] + both_ref[1 - (place_ref[0] & 1)]


def three_kernel(place_ref, mine_ref, both_ref, more_ref, out_ref):
    out_ref[...] = mine_ref[...] + both_ref[1 - (place_ref[0] & 1)] + more_ref[...]


def final_kernel(one_ref, two_ref, out_ref):
    out_ref[...] = (one_ref[...] + two_ref[...]).astype(BF16)


def exchange_pieces(packed):
    pieces = packed.reshape(PAIRS, 3, 4, HEAD_DIM)
    pieces = lax.all_to_all(pieces, "ctx", 0, 0, axis_index_groups=SIDE_GROUPS)
    return pieces.reshape(PACKED, HEAD_DIM)


def body(queries, keys, values, state_retention_log, boundary, gain, w_out):
    side = (lax.axis_index("ctx") & 1).reshape(1)
    place = lax.axis_index("tp").reshape(1)
    boundary = boundary.reshape(1, EVENTS)
    gain = gain.reshape(1, 512)
    packed = ((PACKED, HEAD_DIM), F32)

    sent, kept, decay = call(
        terms_kernel,
        [packed, packed, ((HEADS_DEV, HEAD_DIM), F32)],
        (side, keys, values, state_retention_log, boundary),
        scalars=1,
        scratch=[
            pltpu.VMEM((EVENTS, 512), BF16),
            pltpu.VMEM((EVENTS, 512), BF16),
            pltpu.VMEM((HEADS_DEV, EVENTS), F32),
            pltpu.VMEM((1, EVENTS), jnp.int32),
            pltpu.SemaphoreType.DMA((4,)),
        ],
        flops=70_000_000,
        moved=900_000,
        space=pltpu.HBM,
        out_space=pltpu.VMEM,
    )
    both = lax.all_gather(sent, "ctx", axis_index_groups=SIDE_PAIRS)
    pair_terms, got = call(
        combine_kernel, [packed, packed], (side, kept, both, decay), scalars=1, flops=200_000, moved=1_500_000
    )
    slices = exchange_pieces(pair_terms)
    (states,) = call(scan_kernel, [packed], (side, slices), scalars=1, flops=200_000, moved=600_000)
    own = exchange_pieces(states)
    own, w_late = lax.optimization_barrier((own, w_out))
    other = lax.ppermute(own, "ctx", SIDE_SWAP)
    (staged,) = call(
        stage_kernel,
        [((D // COLS, 512, COLS), BF16)],
        (w_late,),
        scratch=[pltpu.SemaphoreType.DMA((D // COLS,))],
        moved=12_600_000,
        space=pltpu.HBM,
        out_space=pltpu.VMEM,
    )
    other, staged = lax.optimization_barrier((other, staged))
    inner = ((EVENTS, 512), F32)
    total, factor = call(
        inner_kernel,
        [inner, inner],
        (side, queries, keys, values, state_retention_log, boundary, got, own),
        scalars=1,
        flops=100_000_000,
        moved=1_500_000,
    )
    block = ((EVENTS, COLS), F32)
    two_blocks = ((2, EVENTS, COLS), F32)
    normed, opposite_send, opposite_mine, behind_send, behind_mine = call(
        first_kernel,
        [((EVENTS, 512), BF16)] + [block] * 4,
        (place, queries, total, factor, other, gain, staged),
        scalars=1,
        flops=430_000_000,
        moved=6_000_000,
    )

    def core_sum(mine, both):
        return call(core_sum_kernel, [block], (place, mine, both), scalars=1)[0]

    opposite_both = lax.all_gather(opposite_send, "tp", axis_index_groups=CORE_PAIRS)
    opposite = core_sum(opposite_mine, opposite_both)
    opposite, behind_send = lax.optimization_barrier((opposite, behind_send))
    ahead_got = lax.ppermute(opposite, "tp", ONWARD)
    behind_both = lax.all_gather(behind_send, "tp", axis_index_groups=CORE_PAIRS)
    behind_both, normed = lax.optimization_barrier((behind_both, normed))
    behind = core_sum(behind_mine, behind_both)
    one = lax.ppermute(behind, "tp", BACK)
    ahead_send, ahead_mine, own_send, own_mine = call(
        rest_kernel, [block] * 4, (place, normed, staged), scalars=1, flops=400_000_000, moved=5_000_000
    )
    ahead_both = lax.all_gather(ahead_send, "tp", axis_index_groups=CORE_PAIRS)
    own_both = lax.all_gather(own_send, "tp", axis_index_groups=CORE_PAIRS)
    (passed,) = call(three_kernel, [block], (place, ahead_mine, ahead_both, ahead_got), scalars=1)
    two = lax.ppermute(passed, "tp", ONWARD)
    (own_and_one,) = call(three_kernel, [block], (place, own_mine, own_both, one), scalars=1, moved=1_600_000)
    (out,) = call(final_kernel, [((EVENTS, COLS), BF16)], (own_and_one, two), moved=1_000_000)
    return out


def solution(mesh):
    in_specs = (
        P("ctx", "tp"),
        P("ctx", "tp"),
        P("ctx", "tp"),
        P("tp", "ctx"),
        P("ctx"),
        P("tp"),
        P("tp", None),
    )
    out_specs = P("ctx", "tp")
    return jax.shard_map(body, mesh=mesh, in_specs=in_specs, out_specs=out_specs, check_vma=False)
```

```python
import math

import jax
import jax.numpy as jnp
from jax import lax
from jax.experimental import pallas as pl
from jax.experimental.pallas import tpu as pltpu
from jax.sharding import PartitionSpec as P

HEAD_DIM = 128
EVENTS = 128
HEADS_DEV = 4
D = 6144
COLS = 768
PAIRS = 48
PIECES = PAIRS // HEADS_DEV
ROWS = 11
CHUNK = ROWS + 1
HEAD_ROWS = PIECES * CHUNK
PACKED = PAIRS * CHUNK
RING = 4

surge_log_factor = math.log(0.6)
F32 = jnp.float32
BF16 = jnp.bfloat16
VMEM_LIMIT = 24 * 1024 * 1024

SIDE_GROUPS = [[2 * pair + side for pair in range(PAIRS)] for side in range(2)]
SIDE_SWAP = [(i, i ^ 1) for i in range(2 * PAIRS)]
SIDE_PAIRS = [[i, i + 1] for i in range(0, 2 * PAIRS, 2)]
CORE_SWAP = [(i, i ^ 1) for i in range(8)]
CORE_PAIRS = [[i, i + 1] for i in range(0, 8, 2)]
ONWARD = [(i, (i + (2 if i % 2 == 0 else 6)) % 8) for i in range(8)]
BACK = [(i, (i + (6 if i % 2 == 0 else 2)) % 8) for i in range(8)]


def piece_rows(piece):
    return min(ROWS, HEAD_DIM - ROWS * piece)


def call(kernel, outs, args, scalars=0, scratch=(), flops=0, moved=0, space=pltpu.VMEM, out_space=None):
    specs = [pl.BlockSpec(memory_space=pltpu.SMEM)] * scalars
    specs += [pl.BlockSpec(memory_space=space)] * (len(args) - scalars)
    if space is pltpu.HBM:
        args = args[:scalars] + tuple(pltpu.with_memory_space_constraint(x, space) for x in args[scalars:])
    shapes = [(out_space or jax.ShapeDtypeStruct)(shape, dtype) for shape, dtype in outs]
    return pl.pallas_call(
        kernel,
        out_shape=shapes,
        in_specs=specs,
        out_specs=[pl.BlockSpec(memory_space=out_space or pltpu.VMEM)] * len(outs),
        scratch_shapes=list(scratch),
        compiler_params=pltpu.CompilerParams(vmem_limit_bytes=VMEM_LIMIT),
        cost_estimate=pl.CostEstimate(flops=flops, bytes_accessed=moved, transcendentals=0),
    )(*args)


def event_sums(log_ref, boundary_ref):
    rate = log_ref[...] + surge_log_factor * boundary_ref[...].astype(F32)
    row = lax.broadcasted_iota(jnp.int32, (EVENTS, EVENTS), 0)
    column = lax.broadcasted_iota(jnp.int32, (EVENTS, EVENTS), 1)
    lower = (column <= row).astype(F32)
    upper = (row <= column).astype(F32)
    columns = lax.dot_general(
        lower, rate, (((1,), (1,)), ((), ())), precision=lax.Precision.HIGHEST, preferred_element_type=F32
    )
    return rate, columns, upper


def factors(side, columns):
    ends = columns[EVENTS - 1 : EVENTS, :]
    toward_end = jnp.exp(ends - columns)
    from_start = jnp.exp(columns)
    sent = jnp.where(side == 0, toward_end, from_start)
    kept = jnp.where(side == 0, from_start, toward_end)
    return ends, sent, kept


def halves(wide):
    high = wide.astype(BF16)
    low = (wide - high.astype(F32)).astype(BF16)
    return high, low


def terms_kernel(
    side_ref,
    key_hbm,
    value_hbm,
    log_hbm,
    boundary_hbm,
    sent_ref,
    kept_ref,
    decay_ref,
    key_ref,
    value_ref,
    log_ref,
    boundary_ref,
    sems,
):
    copies = [
        pltpu.make_async_copy(log_hbm, log_ref, sems.at[0]),
        pltpu.make_async_copy(boundary_hbm, boundary_ref, sems.at[1]),
        pltpu.make_async_copy(key_hbm, key_ref, sems.at[2]),
        pltpu.make_async_copy(value_hbm, value_ref, sems.at[3]),
    ]
    for copy in copies:
        copy.start()
    for copy in copies:
        copy.wait()
    _, columns, _ = event_sums(log_ref, boundary_ref)
    ends, sent, kept = factors(side_ref[0], columns)
    decay = jnp.exp(ends)
    sent_ref[...] = jnp.zeros_like(sent_ref)
    kept_ref[...] = jnp.zeros_like(kept_ref)
    for head in range(HEADS_DEV):
        lanes = slice(head * HEAD_DIM, (head + 1) * HEAD_DIM)
        value = value_ref[:, lanes].astype(F32)
        sides = halves(value * sent[:, head : head + 1]) + halves(value * kept[:, head : head + 1])
        product = lax.dot_general(
            key_ref[:, lanes],
            jnp.concatenate(sides, axis=1),
            (((0,), (0,)), ((), ())),
            preferred_element_type=F32,
        )
        sent_term = product[:, :128] + product[:, 128:256]
        kept_term = product[:, 256:384] + product[:, 384:]
        whole_row = jnp.broadcast_to(decay[:, head : head + 1], (1, HEAD_DIM))
        decay_ref[head : head + 1, :] = whole_row
        for piece in range(PIECES):
            count, first = piece_rows(piece), head * HEAD_ROWS + piece * CHUNK
            rows = slice(ROWS * piece, ROWS * piece + count)
            sent_ref[first : first + count, :] = sent_term[rows]
            kept_ref[first : first + count, :] = kept_term[rows]
            sent_ref[first + ROWS : first + CHUNK, :] = whole_row


def combine_kernel(side_ref, kept_ref, both_ref, decay_ref, out_ref, got_ref):
    got_ref[...] = both_ref[1 - side_ref[0]]
    for head in range(HEADS_DEV):
        rows = slice(head * HEAD_ROWS, (head + 1) * HEAD_ROWS)
        out_ref[rows, :] = kept_ref[rows, :] + decay_ref[head : head + 1, :] * got_ref[rows, :]


def scan_kernel(side_ref, term_ref, out_ref):
    def run(pairs):
        state = jnp.zeros((CHUNK, HEAD_DIM), F32)
        for pair in pairs:
            rows = slice(pair * CHUNK, (pair + 1) * CHUNK)
            out_ref[rows, :] = state
            term = term_ref[rows, :]
            state = term[ROWS:, :] * state + term

    @pl.when(side_ref[0] == 1)
    def _():
        run(range(PAIRS))

    @pl.when(side_ref[0] == 0)
    def _():
        run(range(PAIRS - 1, -1, -1))


def unpack(packed_ref, head):
    parts = []
    for piece in range(PIECES):
        first = head * HEAD_ROWS + piece * CHUNK
        parts.append(packed_ref[first : first + piece_rows(piece), :])
    return jnp.concatenate(parts, axis=0)


def times_state(query, state):
    product = jnp.dot(query, jnp.concatenate(halves(state), axis=1), preferred_element_type=F32)
    return product[:, :128] + product[:, 128:]


def inner_kernel(
    side_ref, query_ref, key_ref, value_ref, log_ref, boundary_ref, got_ref, own_ref, total_ref, factor_ref
):
    rate, columns, upper = event_sums(log_ref, boundary_ref)
    rows_cum = lax.dot_general(
        rate, upper, (((1,), (0,)), ((), ())), precision=lax.Precision.HIGHEST, preferred_element_type=F32
    )
    _, own, other = factors(side_ref[0], columns)
    for head in range(HEADS_DEV):
        lanes = slice(head * HEAD_DIM, (head + 1) * HEAD_DIM)
        query = query_ref[:, lanes]
        logits = lax.dot_general(
            query, key_ref[:, lanes], (((1,), (1,)), ((), ())), preferred_element_type=F32
        )
        weight = jnp.exp(-jnp.abs(columns[:, head : head + 1] - rows_cum[head : head + 1, :]))
        probs = (logits * weight).astype(BF16)
        intra = jnp.dot(probs, value_ref[:, lanes], preferred_element_type=F32)
        last = head * HEAD_ROWS + ROWS
        state = unpack(got_ref, head) + got_ref[last : last + 1, :] * unpack(own_ref, head)
        total_ref[:, lanes] = intra + own[:, head : head + 1] * times_state(query, state)
        factor_ref[:, lanes] = jnp.broadcast_to(other[:, head : head + 1], (EVENTS, HEAD_DIM))


def widen_kernel(place_ref, w_hbm, wide_hbm, narrow_ref, wide_ref, sems):
    core = place_ref[0] & 1
    incoming, outgoing = [], []
    for t in range(RING):
        columns = pl.ds(pl.multiple_of((2 * t + 1 - core) * COLS, COLS), COLS)
        incoming.append(pltpu.make_async_copy(w_hbm.at[:, columns], narrow_ref.at[t], sems.at[t]))
        outgoing.append(pltpu.make_async_copy(wide_ref.at[t], wide_hbm.at[t], sems.at[RING + t]))
    for copy in incoming:
        copy.start()
    for t in range(RING):
        incoming[t].wait()
        wide_ref[t] = narrow_ref[t].astype(F32)
        outgoing[t].start()
    for copy in outgoing:
        copy.wait()


def stage_kernel(place_ref, w_hbm, wide_ref, staged_ref, sems):
    rows = w_hbm.shape[0]
    core = place_ref[0] & 1
    copies = []
    for t in range(RING):
        columns = pl.ds(pl.multiple_of((2 * t + core) * COLS, COLS), COLS)
        copies.append(
            pltpu.make_async_copy(w_hbm.at[:, columns], staged_ref.at[t, pl.ds(0, rows)], sems.at[t])
        )
    for copy in copies:
        copy.start()
    for t in range(RING):
        staged_ref[t, rows:, :] = wide_ref[t].astype(BF16)
    for copy in copies:
        copy.wait()


def stage(place, w_out, wide):
    return pl.pallas_call(
        stage_kernel,
        in_specs=[
            pl.BlockSpec(memory_space=pltpu.SMEM),
            pl.BlockSpec(memory_space=pltpu.HBM),
            pl.BlockSpec(memory_space=pltpu.VMEM),
        ],
        out_specs=pl.BlockSpec(memory_space=pltpu.VMEM),
        out_shape=pltpu.VMEM((RING, 2 * w_out.shape[0], COLS), BF16),
        scratch_shapes=[pltpu.SemaphoreType.DMA((RING,))],
        compiler_params=pltpu.CompilerParams(vmem_limit_bytes=VMEM_LIMIT),
        cost_estimate=pl.CostEstimate(flops=0, bytes_accessed=16_000_000, transcendentals=0),
    )(place, pltpu.with_memory_space_constraint(w_out, pltpu.HBM), wide)


def normed_kernel(query_ref, total_ref, factor_ref, other_ref, gain_ref, normed_ref):
    for head in range(HEADS_DEV):
        lanes = slice(head * HEAD_DIM, (head + 1) * HEAD_DIM)
        total = total_ref[:, lanes] + factor_ref[:, lanes] * times_state(
            query_ref[:, lanes], unpack(other_ref, head)
        )
        average = jnp.mean(total * total, axis=1, keepdims=True)
        scaled = total * lax.rsqrt(average + 1e-06) * gain_ref[:, lanes]
        normed_ref[:, lanes] = scaled.astype(BF16).astype(F32)


def project(place, both_ref, w_ref, far):
    core = place & 1
    normed = jnp.concatenate([both_ref[core].astype(BF16), both_ref[1 - core].astype(BF16)], axis=1)
    return jnp.dot(normed, w_ref[((place >> 1) + far) & 3], preferred_element_type=F32)


def opposite_kernel(place_ref, both_ref, w_ref, out_ref):
    out_ref[...] = project(place_ref[0], both_ref, w_ref, 2)


def behind_kernel(place_ref, both_ref, w_ref, out_ref):
    place = place_ref[0]
    out_ref[...] = project(place, both_ref, w_ref, 3 - 2 * (place & 1))


def ahead_kernel(place_ref, both_ref, w_ref, got_ref, out_ref):
    place = place_ref[0]
    out_ref[...] = project(place, both_ref, w_ref, 1 + 2 * (place & 1)) + got_ref[...]


def own_kernel(place_ref, both_ref, w_ref, got_ref, out_ref):
    out_ref[...] = project(place_ref[0], both_ref, w_ref, 0) + got_ref[...]


def final_kernel(one_ref, two_ref, out_ref):
    out_ref[...] = (one_ref[...] + two_ref[...]).astype(BF16)


def exchange_pieces(packed):
    pieces = packed.reshape(PAIRS, 3, 4, HEAD_DIM)
    pieces = lax.all_to_all(pieces, "ctx", 0, 0, axis_index_groups=SIDE_GROUPS)
    return pieces.reshape(PACKED, HEAD_DIM)


def body(queries, keys, values, state_retention_log, boundary, gain, w_out):
    side = (lax.axis_index("ctx") & 1).reshape(1)
    place = lax.axis_index("tp").reshape(1)
    boundary = boundary.reshape(1, EVENTS)
    gain = gain.reshape(1, 512)
    packed = ((PACKED, HEAD_DIM), F32)

    sent, kept, decay = call(
        terms_kernel,
        [packed, packed, ((HEADS_DEV, HEAD_DIM), F32)],
        (side, keys, values, state_retention_log, boundary),
        scalars=1,
        scratch=[
            pltpu.VMEM((EVENTS, 512), BF16),
            pltpu.VMEM((EVENTS, 512), BF16),
            pltpu.VMEM((HEADS_DEV, EVENTS), F32),
            pltpu.VMEM((1, EVENTS), jnp.int32),
            pltpu.SemaphoreType.DMA((4,)),
        ],
        flops=70_000_000,
        moved=900_000,
        space=pltpu.HBM,
        out_space=pltpu.VMEM,
    )
    both = lax.all_gather(sent, "ctx", axis_index_groups=SIDE_PAIRS)
    pair_terms, got = call(
        combine_kernel, [packed, packed], (side, kept, both, decay), scalars=1, flops=200_000, moved=1_500_000
    )
    pair_terms, w_late = lax.optimization_barrier((pair_terms, w_out))
    (wide,) = call(
        widen_kernel,
        [((RING, 512, COLS), F32)],
        (place, w_late),
        scalars=1,
        scratch=[
            pltpu.VMEM((RING, 512, COLS), BF16),
            pltpu.VMEM((RING, 512, COLS), F32),
            pltpu.SemaphoreType.DMA((2 * RING,)),
        ],
        moved=9_500_000,
        space=pltpu.HBM,
        out_space=pltpu.HBM,
    )
    wide_got = lax.ppermute(wide, "tp", CORE_SWAP)
    slices = exchange_pieces(pair_terms)
    (states,) = call(scan_kernel, [packed], (side, slices), scalars=1, flops=50_000_000_000, moved=600_000)
    own = exchange_pieces(states)
    own, w_late = lax.optimization_barrier((own, w_late))
    other = lax.ppermute(own, "ctx", SIDE_SWAP)
    staged = stage(place, w_late, wide_got)
    other, staged = lax.optimization_barrier((other, staged))
    inner = ((EVENTS, 512), F32)
    total, factor = call(
        inner_kernel,
        [inner, inner],
        (side, queries, keys, values, state_retention_log, boundary, got, own),
        scalars=1,
        flops=100_000_000,
        moved=1_500_000,
    )
    block = ((EVENTS, COLS), F32)
    (normed,) = call(
        normed_kernel, [inner], (queries, total, factor, other, gain), flops=70_000_000, moved=1_300_000
    )
    both = lax.all_gather(normed, "tp", axis_index_groups=CORE_PAIRS)

    def step(kernel, *args):
        args = (place, both, staged) + args
        return call(kernel, [block], args, scalars=1, flops=200_000_000, moved=2_500_000)[0]

    ahead_got = lax.ppermute(step(opposite_kernel), "tp", ONWARD)
    one = lax.ppermute(step(behind_kernel), "tp", BACK)
    two = lax.ppermute(step(ahead_kernel, ahead_got), "tp", ONWARD)
    own_and_one = step(own_kernel, one)
    (out,) = call(final_kernel, [((EVENTS, COLS), BF16)], (own_and_one, two), moved=1_000_000)
    return out


def solution(mesh):
    in_specs = (
        P("ctx", "tp"),
        P("ctx", "tp"),
        P("ctx", "tp"),
        P("tp", "ctx"),
        P("ctx"),
        P("tp"),
        P("tp", None),
    )
    out_specs = P("ctx", "tp")
    return jax.shard_map(body, mesh=mesh, in_specs=in_specs, out_specs=out_specs, check_vma=False)
```

```python
import math

import jax
import jax.numpy as jnp
from jax import lax
from jax.experimental import pallas as pl
from jax.experimental.pallas import tpu as pltpu
from jax.sharding import PartitionSpec as P

HEAD_DIM = 128
EVENTS = 128
HEADS_DEV = 4
D = 6144
COLS = 768
PAIRS = 48
PIECES = PAIRS // HEADS_DEV
ROWS = 11
CHUNK = ROWS + 1
HEAD_ROWS = PIECES * CHUNK
PACKED = PAIRS * CHUNK

surge_log_factor = math.log(0.6)
F32 = jnp.float32
BF16 = jnp.bfloat16
VMEM_LIMIT = 24 * 1024 * 1024

SIDE_GROUPS = [[2 * pair + side for pair in range(PAIRS)] for side in range(2)]
SIDE_SWAP = [(i, i ^ 1) for i in range(2 * PAIRS)]
SIDE_PAIRS = [[i, i + 1] for i in range(0, 2 * PAIRS, 2)]
CORE_SWAP = [(i, i ^ 1) for i in range(8)]
CORE_PAIRS = [[i, i + 1] for i in range(0, 8, 2)]
ONWARD = [(i, (i + (2 if i % 2 == 0 else 6)) % 8) for i in range(8)]
BACK = [(i, (i + (6 if i % 2 == 0 else 2)) % 8) for i in range(8)]


def piece_rows(piece):
    return min(ROWS, HEAD_DIM - ROWS * piece)


def call(kernel, outs, args, scalars=0, scratch=(), flops=0, moved=0, space=pltpu.VMEM, out_space=None):
    specs = [pl.BlockSpec(memory_space=pltpu.SMEM)] * scalars
    specs += [pl.BlockSpec(memory_space=space)] * (len(args) - scalars)
    if space is pltpu.HBM:
        args = args[:scalars] + tuple(pltpu.with_memory_space_constraint(x, space) for x in args[scalars:])
    shapes = [(out_space or jax.ShapeDtypeStruct)(shape, dtype) for shape, dtype in outs]
    return pl.pallas_call(
        kernel,
        out_shape=shapes,
        in_specs=specs,
        out_specs=[pl.BlockSpec(memory_space=out_space or pltpu.VMEM)] * len(outs),
        scratch_shapes=list(scratch),
        compiler_params=pltpu.CompilerParams(vmem_limit_bytes=VMEM_LIMIT),
        cost_estimate=pl.CostEstimate(flops=flops, bytes_accessed=moved, transcendentals=0),
    )(*args)


def event_sums(log_ref, boundary_ref):
    rate = log_ref[...] + surge_log_factor * boundary_ref[...].astype(F32)
    row = lax.broadcasted_iota(jnp.int32, (EVENTS, EVENTS), 0)
    column = lax.broadcasted_iota(jnp.int32, (EVENTS, EVENTS), 1)
    lower = (column <= row).astype(F32)
    upper = (row <= column).astype(F32)
    columns = lax.dot_general(
        lower, rate, (((1,), (1,)), ((), ())), precision=lax.Precision.HIGHEST, preferred_element_type=F32
    )
    return rate, columns, upper


def factors(side, columns):
    ends = columns[EVENTS - 1 : EVENTS, :]
    toward_end = jnp.exp(ends - columns)
    from_start = jnp.exp(columns)
    sent = jnp.where(side == 0, toward_end, from_start)
    kept = jnp.where(side == 0, from_start, toward_end)
    return ends, sent, kept


def halves(wide):
    high = wide.astype(BF16)
    low = (wide - high.astype(F32)).astype(BF16)
    return high, low


def terms_kernel(
    side_ref,
    key_hbm,
    value_hbm,
    log_hbm,
    boundary_hbm,
    sent_ref,
    kept_ref,
    decay_ref,
    key_ref,
    value_ref,
    log_ref,
    boundary_ref,
    sems,
):
    copies = [
        pltpu.make_async_copy(log_hbm, log_ref, sems.at[0]),
        pltpu.make_async_copy(boundary_hbm, boundary_ref, sems.at[1]),
        pltpu.make_async_copy(key_hbm, key_ref, sems.at[2]),
        pltpu.make_async_copy(value_hbm, value_ref, sems.at[3]),
    ]
    for copy in copies:
        copy.start()
    for copy in copies:
        copy.wait()
    _, columns, _ = event_sums(log_ref, boundary_ref)
    ends, sent, kept = factors(side_ref[0], columns)
    decay = jnp.exp(ends)
    sent_ref[...] = jnp.zeros_like(sent_ref)
    kept_ref[...] = jnp.zeros_like(kept_ref)
    for head in range(HEADS_DEV):
        lanes = slice(head * HEAD_DIM, (head + 1) * HEAD_DIM)
        value = value_ref[:, lanes].astype(F32)
        sides = halves(value * sent[:, head : head + 1]) + halves(value * kept[:, head : head + 1])
        product = lax.dot_general(
            key_ref[:, lanes],
            jnp.concatenate(sides, axis=1),
            (((0,), (0,)), ((), ())),
            preferred_element_type=F32,
        )
        sent_term = product[:, :128] + product[:, 128:256]
        kept_term = product[:, 256:384] + product[:, 384:]
        whole_row = jnp.broadcast_to(decay[:, head : head + 1], (1, HEAD_DIM))
        decay_ref[head : head + 1, :] = whole_row
        for piece in range(PIECES):
            count, first = piece_rows(piece), head * HEAD_ROWS + piece * CHUNK
            rows = slice(ROWS * piece, ROWS * piece + count)
            sent_ref[first : first + count, :] = sent_term[rows]
            kept_ref[first : first + count, :] = kept_term[rows]
            sent_ref[first + ROWS : first + CHUNK, :] = whole_row


def combine_kernel(side_ref, kept_ref, both_ref, decay_ref, out_ref, got_ref):
    got_ref[...] = both_ref[1 - side_ref[0]]
    for head in range(HEADS_DEV):
        rows = slice(head * HEAD_ROWS, (head + 1) * HEAD_ROWS)
        out_ref[rows, :] = kept_ref[rows, :] + decay_ref[head : head + 1, :] * got_ref[rows, :]


def scan_kernel(side_ref, term_ref, out_ref):
    def run(pairs):
        state = jnp.zeros((CHUNK, HEAD_DIM), F32)
        for pair in pairs:
            rows = slice(pair * CHUNK, (pair + 1) * CHUNK)
            out_ref[rows, :] = state
            term = term_ref[rows, :]
            state = term[ROWS:, :] * state + term

    @pl.when(side_ref[0] == 1)
    def _():
        run(range(PAIRS))

    @pl.when(side_ref[0] == 0)
    def _():
        run(range(PAIRS - 1, -1, -1))


def unpack(packed_ref, head):
    parts = []
    for piece in range(PIECES):
        first = head * HEAD_ROWS + piece * CHUNK
        parts.append(packed_ref[first : first + piece_rows(piece), :])
    return jnp.concatenate(parts, axis=0)


def times_state(query, state):
    product = jnp.dot(query, jnp.concatenate(halves(state), axis=1), preferred_element_type=F32)
    return product[:, :128] + product[:, 128:]


def inner_kernel(
    side_ref, query_ref, key_ref, value_ref, log_ref, boundary_ref, got_ref, own_ref, total_ref, factor_ref
):
    rate, columns, upper = event_sums(log_ref, boundary_ref)
    rows_cum = lax.dot_general(
        rate, upper, (((1,), (0,)), ((), ())), precision=lax.Precision.HIGHEST, preferred_element_type=F32
    )
    _, own, other = factors(side_ref[0], columns)
    for head in range(HEADS_DEV):
        lanes = slice(head * HEAD_DIM, (head + 1) * HEAD_DIM)
        query = query_ref[:, lanes]
        logits = lax.dot_general(
            query, key_ref[:, lanes], (((1,), (1,)), ((), ())), preferred_element_type=F32
        )
        weight = jnp.exp(-jnp.abs(columns[:, head : head + 1] - rows_cum[head : head + 1, :]))
        probs = (logits * weight).astype(BF16)
        intra = jnp.dot(probs, value_ref[:, lanes], preferred_element_type=F32)
        last = head * HEAD_ROWS + ROWS
        state = unpack(got_ref, head) + got_ref[last : last + 1, :] * unpack(own_ref, head)
        total_ref[:, lanes] = intra + own[:, head : head + 1] * times_state(query, state)
        factor_ref[:, lanes] = jnp.broadcast_to(other[:, head : head + 1], (EVENTS, HEAD_DIM))


def stage_kernel(w_hbm, staged_ref, sems):
    copies = [
        pltpu.make_async_copy(w_hbm.at[:, pl.ds(block * COLS, COLS)], staged_ref.at[block], sems.at[block])
        for block in range(D // COLS)
    ]
    for copy in copies:
        copy.start()
    for copy in copies:
        copy.wait()


def block_of(place, far, core):
    return 2 * (((place >> 1) + far) & 3) + core


def first_kernel(
    place_ref,
    query_ref,
    total_ref,
    factor_ref,
    other_ref,
    gain_ref,
    w_ref,
    normed_ref,
    opposite_send_ref,
    opposite_ref,
    behind_send_ref,
    behind_ref,
):
    for head in range(HEADS_DEV):
        lanes = slice(head * HEAD_DIM, (head + 1) * HEAD_DIM)
        total = total_ref[:, lanes] + factor_ref[:, lanes] * times_state(
            query_ref[:, lanes], unpack(other_ref, head)
        )
        average = jnp.mean(total * total, axis=1, keepdims=True)
        scaled = total * lax.rsqrt(average + 1e-06) * gain_ref[:, lanes]
        normed_ref[:, lanes] = scaled.astype(BF16)
    place = place_ref[0]
    core = place & 1
    normed = normed_ref[...]
    for out_ref, far, whose in (
        (opposite_send_ref, 2, 1 - core),
        (opposite_ref, 2, core),
        (behind_send_ref, 1 + 2 * core, 1 - core),
        (behind_ref, 3 - 2 * core, core),
    ):
        out_ref[...] = jnp.dot(normed, w_ref[block_of(place, far, whose)], preferred_element_type=F32)


def rest_kernel(place_ref, normed_ref, w_ref, ahead_send_ref, ahead_ref, own_send_ref, own_ref):
    place = place_ref[0]
    core = place & 1
    normed = normed_ref[...]
    for out_ref, far, whose in (
        (ahead_send_ref, 3 - 2 * core, 1 - core),
        (ahead_ref, 1 + 2 * core, core),
        (own_send_ref, 0, 1 - core),
        (own_ref, 0, core),
    ):
        out_ref[...] = jnp.dot(normed, w_ref[block_of(place, far, whose)], preferred_element_type=F32)


def core_sum_kernel(place_ref, mine_ref, both_ref, out_ref):
    out_ref[...] = mine_ref[...] + both_ref[1 - (place_ref[0] & 1)]


def three_kernel(place_ref, mine_ref, both_ref, more_ref, out_ref):
    out_ref[...] = mine_ref[...] + both_ref[1 - (place_ref[0] & 1)] + more_ref[...]


def final_kernel(place_ref, mine_ref, both_ref, one_ref, two_ref, out_ref):
    own = mine_ref[...] + both_ref[1 - (place_ref[0] & 1)]
    out_ref[...] = (own + (one_ref[...] + two_ref[...])).astype(BF16)


def exchange_pieces(packed):
    pieces = packed.reshape(PAIRS, 3, 4, HEAD_DIM)
    pieces = lax.all_to_all(pieces, "ctx", 0, 0, axis_index_groups=SIDE_GROUPS)
    return pieces.reshape(PACKED, HEAD_DIM)


def body(queries, keys, values, state_retention_log, boundary, gain, w_out):
    side = (lax.axis_index("ctx") & 1).reshape(1)
    place = lax.axis_index("tp").reshape(1)
    boundary = boundary.reshape(1, EVENTS)
    gain = gain.reshape(1, 512)
    packed = ((PACKED, HEAD_DIM), F32)

    sent, kept, decay = call(
        terms_kernel,
        [packed, packed, ((HEADS_DEV, HEAD_DIM), F32)],
        (side, keys, values, state_retention_log, boundary),
        scalars=1,
        scratch=[
            pltpu.VMEM((EVENTS, 512), BF16),
            pltpu.VMEM((EVENTS, 512), BF16),
            pltpu.VMEM((HEADS_DEV, EVENTS), F32),
            pltpu.VMEM((1, EVENTS), jnp.int32),
            pltpu.SemaphoreType.DMA((4,)),
        ],
        flops=70_000_000,
        moved=900_000,
        space=pltpu.HBM,
        out_space=pltpu.VMEM,
    )
    both = lax.all_gather(sent, "ctx", axis_index_groups=SIDE_PAIRS)
    pair_terms, got = call(
        combine_kernel, [packed, packed], (side, kept, both, decay), scalars=1, flops=200_000, moved=1_500_000
    )
    slices = exchange_pieces(pair_terms)
    (states,) = call(scan_kernel, [packed], (side, slices), scalars=1, flops=200_000, moved=600_000)
    own = exchange_pieces(states)
    own, w_late = lax.optimization_barrier((own, w_out))
    other = lax.ppermute(own, "ctx", SIDE_SWAP)
    (staged,) = call(
        stage_kernel,
        [((D // COLS, 512, COLS), BF16)],
        (w_late,),
        scratch=[pltpu.SemaphoreType.DMA((D // COLS,))],
        moved=12_600_000,
        space=pltpu.HBM,
        out_space=pltpu.VMEM,
    )
    other, staged = lax.optimization_barrier((other, staged))
    inner = ((EVENTS, 512), F32)
    total, factor = call(
        inner_kernel,
        [inner, inner],
        (side, queries, keys, values, state_retention_log, boundary, got, own),
        scalars=1,
        flops=100_000_000,
        moved=1_500_000,
    )
    block = ((EVENTS, COLS), F32)
    two_blocks = ((2, EVENTS, COLS), F32)
    normed, opposite_send, opposite_mine, behind_send, behind_mine = call(
        first_kernel,
        [((EVENTS, 512), BF16)] + [block] * 4,
        (place, queries, total, factor, other, gain, staged),
        scalars=1,
        flops=430_000_000,
        moved=6_000_000,
    )

    def core_sum(mine, both):
        return call(core_sum_kernel, [block], (place, mine, both), scalars=1)[0]

    opposite_both = lax.all_gather(opposite_send, "tp", axis_index_groups=CORE_PAIRS)
    opposite = core_sum(opposite_mine, opposite_both)
    opposite, behind_send = lax.optimization_barrier((opposite, behind_send))
    ahead_got = lax.ppermute(opposite, "tp", ONWARD)
    behind_both = lax.all_gather(behind_send, "tp", axis_index_groups=CORE_PAIRS)
    behind_both, normed = lax.optimization_barrier((behind_both, normed))
    behind = core_sum(behind_mine, behind_both)
    ahead_send, ahead_mine, own_send, own_mine = call(
        rest_kernel, [block] * 4, (place, normed, staged), scalars=1, flops=400_000_000, moved=5_000_000
    )
    ahead_both = lax.all_gather(ahead_send, "tp", axis_index_groups=CORE_PAIRS)
    own_both = lax.all_gather(own_send, "tp", axis_index_groups=CORE_PAIRS)
    ahead_got, behind = lax.optimization_barrier((ahead_got, behind))
    one = lax.ppermute(behind, "tp", BACK)
    (passed,) = call(three_kernel, [block], (place, ahead_mine, ahead_both, ahead_got), scalars=1)
    two = lax.ppermute(passed, "tp", ONWARD)
    (out,) = call(
        final_kernel,
        [((EVENTS, COLS), BF16)],
        (place, own_mine, own_both, one, two),
        scalars=1,
        moved=2_000_000,
    )
    return out


def solution(mesh):
    in_specs = (
        P("ctx", "tp"),
        P("ctx", "tp"),
        P("ctx", "tp"),
        P("tp", "ctx"),
        P("ctx"),
        P("tp"),
        P("tp", None),
    )
    out_specs = P("ctx", "tp")
    return jax.shard_map(body, mesh=mesh, in_specs=in_specs, out_specs=out_specs, check_vma=False)
```

```python
import math

import jax
import jax.numpy as jnp
from jax import lax
from jax.experimental import pallas as pl
from jax.experimental.pallas import tpu as pltpu
from jax.sharding import PartitionSpec as P

HEAD_DIM = 128
EVENTS = 128
HEADS_DEV = 4
D = 6144
COLS = 768
PAIRS = 48
PIECES = PAIRS // HEADS_DEV
ROWS = 11
CHUNK = ROWS + 1
HEAD_ROWS = PIECES * CHUNK
PACKED = PAIRS * CHUNK

surge_log_factor = math.log(0.6)
F32 = jnp.float32
BF16 = jnp.bfloat16
VMEM_LIMIT = 24 * 1024 * 1024

SIDE_GROUPS = [[2 * pair + side for pair in range(PAIRS)] for side in range(2)]
SIDE_SWAP = [(i, i ^ 1) for i in range(2 * PAIRS)]
SIDE_PAIRS = [[i, i + 1] for i in range(0, 2 * PAIRS, 2)]
CORE_SWAP = [(i, i ^ 1) for i in range(8)]
CORE_PAIRS = [[i, i + 1] for i in range(0, 8, 2)]
ONWARD = [(i, (i + (2 if i % 2 == 0 else 6)) % 8) for i in range(8)]
BACK = [(i, (i + (6 if i % 2 == 0 else 2)) % 8) for i in range(8)]


def piece_rows(piece):
    return min(ROWS, HEAD_DIM - ROWS * piece)


def call(kernel, outs, args, scalars=0, scratch=(), flops=0, moved=0, space=pltpu.VMEM, out_space=None):
    specs = [pl.BlockSpec(memory_space=pltpu.SMEM)] * scalars
    specs += [pl.BlockSpec(memory_space=space)] * (len(args) - scalars)
    if space is pltpu.HBM:
        args = args[:scalars] + tuple(pltpu.with_memory_space_constraint(x, space) for x in args[scalars:])
    shapes = [(out_space or jax.ShapeDtypeStruct)(shape, dtype) for shape, dtype in outs]
    return pl.pallas_call(
        kernel,
        out_shape=shapes,
        in_specs=specs,
        out_specs=[pl.BlockSpec(memory_space=out_space or pltpu.VMEM)] * len(outs),
        scratch_shapes=list(scratch),
        compiler_params=pltpu.CompilerParams(vmem_limit_bytes=VMEM_LIMIT),
        cost_estimate=pl.CostEstimate(flops=flops, bytes_accessed=moved, transcendentals=0),
    )(*args)


def event_sums(log_ref, boundary_ref):
    rate = log_ref[...] + surge_log_factor * boundary_ref[...].astype(F32)
    row = lax.broadcasted_iota(jnp.int32, (EVENTS, EVENTS), 0)
    column = lax.broadcasted_iota(jnp.int32, (EVENTS, EVENTS), 1)
    lower = (column <= row).astype(F32)
    upper = (row <= column).astype(F32)
    columns = lax.dot_general(
        lower, rate, (((1,), (1,)), ((), ())), precision=lax.Precision.HIGHEST, preferred_element_type=F32
    )
    return rate, columns, upper


def factors(side, columns):
    ends = columns[EVENTS - 1 : EVENTS, :]
    toward_end = jnp.exp(ends - columns)
    from_start = jnp.exp(columns)
    sent = jnp.where(side == 0, toward_end, from_start)
    kept = jnp.where(side == 0, from_start, toward_end)
    return ends, sent, kept


def halves(wide):
    high = wide.astype(BF16)
    low = (wide - high.astype(F32)).astype(BF16)
    return high, low


def terms_kernel(
    side_ref,
    key_hbm,
    value_hbm,
    log_hbm,
    boundary_hbm,
    sent_ref,
    kept_ref,
    decay_ref,
    key_ref,
    value_ref,
    log_ref,
    boundary_ref,
    sems,
):
    copies = [
        pltpu.make_async_copy(log_hbm, log_ref, sems.at[0]),
        pltpu.make_async_copy(boundary_hbm, boundary_ref, sems.at[1]),
        pltpu.make_async_copy(key_hbm, key_ref, sems.at[2]),
        pltpu.make_async_copy(value_hbm, value_ref, sems.at[3]),
    ]
    for copy in copies:
        copy.start()
    for copy in copies:
        copy.wait()
    _, columns, _ = event_sums(log_ref, boundary_ref)
    ends, sent, kept = factors(side_ref[0], columns)
    decay = jnp.exp(ends)
    sent_ref[...] = jnp.zeros_like(sent_ref)
    kept_ref[...] = jnp.zeros_like(kept_ref)
    for head in range(HEADS_DEV):
        lanes = slice(head * HEAD_DIM, (head + 1) * HEAD_DIM)
        value = value_ref[:, lanes].astype(F32)
        sides = halves(value * sent[:, head : head + 1]) + halves(value * kept[:, head : head + 1])
        product = lax.dot_general(
            key_ref[:, lanes],
            jnp.concatenate(sides, axis=1),
            (((0,), (0,)), ((), ())),
            preferred_element_type=F32,
        )
        sent_term = product[:, :128] + product[:, 128:256]
        kept_term = product[:, 256:384] + product[:, 384:]
        whole_row = jnp.broadcast_to(decay[:, head : head + 1], (1, HEAD_DIM))
        decay_ref[head : head + 1, :] = whole_row
        for piece in range(PIECES):
            count, first = piece_rows(piece), head * HEAD_ROWS + piece * CHUNK
            rows = slice(ROWS * piece, ROWS * piece + count)
            sent_ref[first : first + count, :] = sent_term[rows]
            kept_ref[first : first + count, :] = kept_term[rows]
            sent_ref[first + ROWS : first + CHUNK, :] = whole_row


def combine_kernel(side_ref, kept_ref, both_ref, decay_ref, out_ref, got_ref):
    got_ref[...] = both_ref[1 - side_ref[0]]
    for head in range(HEADS_DEV):
        rows = slice(head * HEAD_ROWS, (head + 1) * HEAD_ROWS)
        out_ref[rows, :] = kept_ref[rows, :] + decay_ref[head : head + 1, :] * got_ref[rows, :]


def scan_kernel(side_ref, term_ref, out_ref):
    def run(pairs):
        state = jnp.zeros((CHUNK, HEAD_DIM), F32)
        for pair in pairs:
            rows = slice(pair * CHUNK, (pair + 1) * CHUNK)
            out_ref[rows, :] = state
            term = term_ref[rows, :]
            state = term[ROWS:, :] * state + term

    @pl.when(side_ref[0] == 1)
    def _():
        run(range(PAIRS))

    @pl.when(side_ref[0] == 0)
    def _():
        run(range(PAIRS - 1, -1, -1))


def unpack(packed_ref, head):
    parts = []
    for piece in range(PIECES):
        first = head * HEAD_ROWS + piece * CHUNK
        parts.append(packed_ref[first : first + piece_rows(piece), :])
    return jnp.concatenate(parts, axis=0)


def times_state(query, state):
    product = jnp.dot(query, jnp.concatenate(halves(state), axis=1), preferred_element_type=F32)
    return product[:, :128] + product[:, 128:]


def inner_kernel(
    side_ref, query_ref, key_ref, value_ref, log_ref, boundary_ref, got_ref, own_ref, total_ref, factor_ref
):
    rate, columns, upper = event_sums(log_ref, boundary_ref)
    rows_cum = lax.dot_general(
        rate, upper, (((1,), (0,)), ((), ())), precision=lax.Precision.HIGHEST, preferred_element_type=F32
    )
    _, own, other = factors(side_ref[0], columns)
    for head in range(HEADS_DEV):
        lanes = slice(head * HEAD_DIM, (head + 1) * HEAD_DIM)
        query = query_ref[:, lanes]
        logits = lax.dot_general(
            query, key_ref[:, lanes], (((1,), (1,)), ((), ())), preferred_element_type=F32
        )
        weight = jnp.exp(-jnp.abs(columns[:, head : head + 1] - rows_cum[head : head + 1, :]))
        probs = (logits * weight).astype(BF16)
        intra = jnp.dot(probs, value_ref[:, lanes], preferred_element_type=F32)
        last = head * HEAD_ROWS + ROWS
        state = unpack(got_ref, head) + got_ref[last : last + 1, :] * unpack(own_ref, head)
        total_ref[:, lanes] = intra + own[:, head : head + 1] * times_state(query, state)
        factor_ref[:, lanes] = jnp.broadcast_to(other[:, head : head + 1], (EVENTS, HEAD_DIM))


def stage_kernel(w_hbm, staged_ref, sems):
    copies = [
        pltpu.make_async_copy(w_hbm.at[:, pl.ds(block * COLS, COLS)], staged_ref.at[block], sems.at[block])
        for block in range(D // COLS)
    ]
    for copy in copies:
        copy.start()
    for copy in copies:
        copy.wait()


def block_of(place, far, core):
    return 2 * (((place >> 1) + far) & 3) + core


def first_kernel(
    place_ref,
    query_ref,
    total_ref,
    factor_ref,
    other_ref,
    gain_ref,
    w_ref,
    normed_ref,
    opposite_send_ref,
    opposite_ref,
    behind_send_ref,
    behind_ref,
):
    for head in range(HEADS_DEV):
        lanes = slice(head * HEAD_DIM, (head + 1) * HEAD_DIM)
        total = total_ref[:, lanes] + factor_ref[:, lanes] * times_state(
            query_ref[:, lanes], unpack(other_ref, head)
        )
        average = jnp.mean(total * total, axis=1, keepdims=True)
        scaled = total * lax.rsqrt(average + 1e-06) * gain_ref[:, lanes]
        normed_ref[:, lanes] = scaled.astype(BF16)
    place = place_ref[0]
    core = place & 1
    normed = normed_ref[...]
    for out_ref, far, whose in (
        (opposite_send_ref, 2, 1 - core),
        (opposite_ref, 2, core),
        (behind_send_ref, 1 + 2 * core, 1 - core),
        (behind_ref, 3 - 2 * core, core),
    ):
        out_ref[...] = jnp.dot(normed, w_ref[block_of(place, far, whose)], preferred_element_type=F32)


def rest_kernel(place_ref, normed_ref, w_ref, ahead_send_ref, ahead_ref, own_send_ref, own_ref):
    place = place_ref[0]
    core = place & 1
    normed = normed_ref[...]
    for out_ref, far, whose in (
        (ahead_send_ref, 3 - 2 * core, 1 - core),
        (ahead_ref, 1 + 2 * core, core),
        (own_send_ref, 0, 1 - core),
        (own_ref, 0, core),
    ):
        out_ref[...] = jnp.dot(normed, w_ref[block_of(place, far, whose)], preferred_element_type=F32)


def core_sum_kernel(place_ref, mine_ref, both_ref, out_ref):
    out_ref[...] = mine_ref[...] + both_ref[1 - (place_ref[0] & 1)]


def three_kernel(place_ref, mine_ref, both_ref, more_ref, out_ref):
    out_ref[...] = mine_ref[...] + both_ref[1 - (place_ref[0] & 1)] + more_ref[...]


def final_kernel(one_ref, two_ref, out_ref):
    out_ref[...] = (one_ref[...] + two_ref[...]).astype(BF16)


def exchange_pieces(packed):
    pieces = packed.reshape(PAIRS, 3, 4, HEAD_DIM)
    pieces = lax.all_to_all(pieces, "ctx", 0, 0, axis_index_groups=SIDE_GROUPS)
    return pieces.reshape(PACKED, HEAD_DIM)


def body(queries, keys, values, state_retention_log, boundary, gain, w_out):
    side = (lax.axis_index("ctx") & 1).reshape(1)
    place = lax.axis_index("tp").reshape(1)
    boundary = boundary.reshape(1, EVENTS)
    gain = gain.reshape(1, 512)
    packed = ((PACKED, HEAD_DIM), F32)

    sent, kept, decay = call(
        terms_kernel,
        [packed, packed, ((HEADS_DEV, HEAD_DIM), F32)],
        (side, keys, values, state_retention_log, boundary),
        scalars=1,
        scratch=[
            pltpu.VMEM((EVENTS, 512), BF16),
            pltpu.VMEM((EVENTS, 512), BF16),
            pltpu.VMEM((HEADS_DEV, EVENTS), F32),
            pltpu.VMEM((1, EVENTS), jnp.int32),
            pltpu.SemaphoreType.DMA((4,)),
        ],
        flops=70_000_000,
        moved=900_000,
        space=pltpu.HBM,
        out_space=pltpu.VMEM,
    )
    both = lax.all_gather(sent, "ctx", axis_index_groups=SIDE_PAIRS)
    pair_terms, got = call(
        combine_kernel, [packed, packed], (side, kept, both, decay), scalars=1, flops=200_000, moved=1_500_000
    )
    slices = exchange_pieces(pair_terms)
    (states,) = call(scan_kernel, [packed], (side, slices), scalars=1, flops=200_000, moved=600_000)
    own = exchange_pieces(states)
    own, w_late = lax.optimization_barrier((own, w_out))
    other = lax.ppermute(own, "ctx", SIDE_SWAP)
    (staged,) = call(
        stage_kernel,
        [((D // COLS, 512, COLS), BF16)],
        (w_late,),
        scratch=[pltpu.SemaphoreType.DMA((D // COLS,))],
        moved=12_600_000,
        space=pltpu.HBM,
        out_space=pltpu.VMEM,
    )
    other, staged = lax.optimization_barrier((other, staged))
    inner = ((EVENTS, 512), F32)
    total, factor = call(
        inner_kernel,
        [inner, inner],
        (side, queries, keys, values, state_retention_log, boundary, got, own),
        scalars=1,
        flops=100_000_000,
        moved=1_500_000,
    )
    block = ((EVENTS, COLS), F32)
    two_blocks = ((2, EVENTS, COLS), F32)
    normed, opposite_send, opposite_mine, behind_send, behind_mine = call(
        first_kernel,
        [((EVENTS, 512), BF16)] + [block] * 4,
        (place, queries, total, factor, other, gain, staged),
        scalars=1,
        flops=430_000_000,
        moved=6_000_000,
    )

    def core_sum(mine, both):
        return call(core_sum_kernel, [block], (place, mine, both), scalars=1)[0]

    opposite_both = lax.all_gather(opposite_send, "tp", axis_index_groups=CORE_PAIRS)
    opposite = core_sum(opposite_mine, opposite_both)
    opposite, behind_send = lax.optimization_barrier((opposite, behind_send))
    ahead_got = lax.ppermute(opposite, "tp", ONWARD)
    behind_both = lax.all_gather(behind_send, "tp", axis_index_groups=CORE_PAIRS)
    behind_both, normed = lax.optimization_barrier((behind_both, normed))
    behind = core_sum(behind_mine, behind_both)
    ahead_send, ahead_mine, own_send, own_mine = call(
        rest_kernel, [block] * 4, (place, normed, staged), scalars=1, flops=400_000_000, moved=5_000_000
    )
    ahead_both = lax.all_gather(ahead_send, "tp", axis_index_groups=CORE_PAIRS)
    own_both = lax.all_gather(own_send, "tp", axis_index_groups=CORE_PAIRS)
    behind, ahead_both = lax.optimization_barrier((behind, ahead_both))
    one = lax.ppermute(behind, "tp", BACK)
    (passed,) = call(three_kernel, [block], (place, ahead_mine, ahead_both, ahead_got), scalars=1)
    two = lax.ppermute(passed, "tp", ONWARD)
    (own_and_one,) = call(three_kernel, [block], (place, own_mine, own_both, one), scalars=1, moved=1_600_000)
    (out,) = call(final_kernel, [((EVENTS, COLS), BF16)], (own_and_one, two), moved=1_000_000)
    return out


def solution(mesh):
    in_specs = (
        P("ctx", "tp"),
        P("ctx", "tp"),
        P("ctx", "tp"),
        P("tp", "ctx"),
        P("ctx"),
        P("tp"),
        P("tp", None),
    )
    out_specs = P("ctx", "tp")
    return jax.shard_map(body, mesh=mesh, in_specs=in_specs, out_specs=out_specs, check_vma=False)
```

```python
import math

import jax
import jax.numpy as jnp
from jax import lax
from jax.experimental import pallas as pl
from jax.experimental.pallas import tpu as pltpu
from jax.sharding import PartitionSpec as P

HEAD_DIM = 128
EVENTS = 128
HEADS_DEV = 4
D = 6144
COLS = 768
PAIRS = 48
PIECES = PAIRS // HEADS_DEV
ROWS = 11
CHUNK = ROWS + 1
HEAD_ROWS = PIECES * CHUNK
PACKED = PAIRS * CHUNK
STATE_ROWS = HEADS_DEV * HEAD_DIM
SENT_ROWS = STATE_ROWS + 8

surge_log_factor = math.log(0.6)
F32 = jnp.float32
BF16 = jnp.bfloat16
VMEM_LIMIT = 24 * 1024 * 1024

SIDE_GROUPS = [[2 * pair + side for pair in range(PAIRS)] for side in range(2)]
SIDE_SWAP = [(i, i ^ 1) for i in range(2 * PAIRS)]
SIDE_PAIRS = [[i, i + 1] for i in range(0, 2 * PAIRS, 2)]
CORE_SWAP = [(i, i ^ 1) for i in range(8)]
CORE_PAIRS = [[i, i + 1] for i in range(0, 8, 2)]
ONWARD = [(i, (i + (2 if i % 2 == 0 else 6)) % 8) for i in range(8)]
BACK = [(i, (i + (6 if i % 2 == 0 else 2)) % 8) for i in range(8)]


def piece_rows(piece):
    return min(ROWS, HEAD_DIM - ROWS * piece)


def call(kernel, outs, args, scalars=0, scratch=(), flops=0, moved=0, space=pltpu.VMEM, out_space=None):
    specs = [pl.BlockSpec(memory_space=pltpu.SMEM)] * scalars
    specs += [pl.BlockSpec(memory_space=space)] * (len(args) - scalars)
    if space is pltpu.HBM:
        args = args[:scalars] + tuple(pltpu.with_memory_space_constraint(x, space) for x in args[scalars:])
    shapes = [(out_space or jax.ShapeDtypeStruct)(shape, dtype) for shape, dtype in outs]
    return pl.pallas_call(
        kernel,
        out_shape=shapes,
        in_specs=specs,
        out_specs=[pl.BlockSpec(memory_space=out_space or pltpu.VMEM)] * len(outs),
        scratch_shapes=list(scratch),
        compiler_params=pltpu.CompilerParams(vmem_limit_bytes=VMEM_LIMIT),
        cost_estimate=pl.CostEstimate(flops=flops, bytes_accessed=moved, transcendentals=0),
    )(*args)


def event_sums(log_ref, boundary_ref):
    rate = log_ref[...] + surge_log_factor * boundary_ref[...].astype(F32)
    row = lax.broadcasted_iota(jnp.int32, (EVENTS, EVENTS), 0)
    column = lax.broadcasted_iota(jnp.int32, (EVENTS, EVENTS), 1)
    lower = (column <= row).astype(F32)
    upper = (row <= column).astype(F32)
    columns = lax.dot_general(
        lower, rate, (((1,), (1,)), ((), ())), precision=lax.Precision.HIGHEST, preferred_element_type=F32
    )
    return rate, columns, upper


def factors(side, columns):
    ends = columns[EVENTS - 1 : EVENTS, :]
    toward_end = jnp.exp(ends - columns)
    from_start = jnp.exp(columns)
    sent = jnp.where(side == 0, toward_end, from_start)
    kept = jnp.where(side == 0, from_start, toward_end)
    return ends, sent, kept


def halves(wide):
    high = wide.astype(BF16)
    low = (wide - high.astype(F32)).astype(BF16)
    return high, low


def terms_kernel(
    side_ref,
    key_hbm,
    value_hbm,
    log_hbm,
    boundary_hbm,
    sent_ref,
    kept_ref,
    decay_ref,
    key_ref,
    value_ref,
    log_ref,
    boundary_ref,
    sems,
):
    copies = [
        pltpu.make_async_copy(log_hbm, log_ref, sems.at[0]),
        pltpu.make_async_copy(boundary_hbm, boundary_ref, sems.at[1]),
        pltpu.make_async_copy(key_hbm, key_ref, sems.at[2]),
        pltpu.make_async_copy(value_hbm, value_ref, sems.at[3]),
    ]
    for copy in copies:
        copy.start()
    for copy in copies[:2]:
        copy.wait()
    _, columns, _ = event_sums(log_ref, boundary_ref)
    ends, sent, kept = factors(side_ref[0], columns)
    decay = jnp.exp(ends)
    for copy in copies[2:]:
        copy.wait()
    sent_ref[STATE_ROWS:, :] = jnp.zeros((SENT_ROWS - STATE_ROWS, HEAD_DIM), F32)
    for head in range(HEADS_DEV):
        lanes = slice(head * HEAD_DIM, (head + 1) * HEAD_DIM)
        value = value_ref[:, lanes].astype(F32)
        sides = halves(value * sent[:, head : head + 1]) + halves(value * kept[:, head : head + 1])
        product = lax.dot_general(
            key_ref[:, lanes],
            jnp.concatenate(sides, axis=1),
            (((0,), (0,)), ((), ())),
            preferred_element_type=F32,
        )
        sent_ref[lanes, :] = product[:, :128] + product[:, 128:256]
        kept_ref[lanes, :] = product[:, 256:384] + product[:, 384:]
        whole_row = jnp.broadcast_to(decay[:, head : head + 1], (1, HEAD_DIM))
        decay_ref[head : head + 1, :] = whole_row
        sent_ref[STATE_ROWS + head : STATE_ROWS + head + 1, :] = whole_row


def combine_kernel(side_ref, kept_ref, both_ref, decay_ref, out_ref):
    other = 1 - side_ref[0]
    for head in range(HEADS_DEV):
        decay = decay_ref[head : head + 1, :]
        rows = slice(head * HEAD_DIM, (head + 1) * HEAD_DIM)
        state = kept_ref[rows, :] + decay * both_ref[other, rows, :]
        last = STATE_ROWS + head
        decay = decay * both_ref[other, last : last + 1, :]
        for piece in range(PIECES):
            count, first = piece_rows(piece), head * HEAD_ROWS + piece * CHUNK
            part = [state[ROWS * piece : ROWS * piece + count]]
            if count < ROWS:
                part.append(jnp.zeros((ROWS - count, HEAD_DIM), F32))
            out_ref[first : first + CHUNK, :] = jnp.concatenate(part + [decay], axis=0)


def scan_kernel(side_ref, term_ref, out_ref):
    def run(pairs):
        state = jnp.zeros((CHUNK, HEAD_DIM), F32)
        for pair in pairs:
            rows = slice(pair * CHUNK, (pair + 1) * CHUNK)
            out_ref[rows, :] = state
            term = term_ref[rows, :]
            state = term[ROWS:, :] * state + term

    @pl.when(side_ref[0] == 1)
    def _():
        run(range(PAIRS))

    @pl.when(side_ref[0] == 0)
    def _():
        run(range(PAIRS - 1, -1, -1))


def unpack_kernel(packed_ref, state_ref):
    for piece in range(PAIRS):
        head, place = divmod(piece, PIECES)
        first = head * HEAD_DIM + ROWS * place
        count = piece_rows(place)
        state_ref[first : first + count, :] = packed_ref[piece * CHUNK : piece * CHUNK + count, :]


def times_state(query, state):
    product = jnp.dot(query, jnp.concatenate(halves(state), axis=1), preferred_element_type=F32)
    return product[:, :128] + product[:, 128:]


def inner_kernel(
    side_ref, query_ref, key_ref, value_ref, log_ref, boundary_ref, both_ref, own_ref, total_ref, factor_ref
):
    rate, columns, upper = event_sums(log_ref, boundary_ref)
    rows_cum = lax.dot_general(
        rate, upper, (((1,), (0,)), ((), ())), precision=lax.Precision.HIGHEST, preferred_element_type=F32
    )
    side = side_ref[0]
    _, own, other = factors(side, columns)
    for head in range(HEADS_DEV):
        lanes = slice(head * HEAD_DIM, (head + 1) * HEAD_DIM)
        query = query_ref[:, lanes]
        logits = lax.dot_general(
            query, key_ref[:, lanes], (((1,), (1,)), ((), ())), preferred_element_type=F32
        )
        weight = jnp.exp(-jnp.abs(columns[:, head : head + 1] - rows_cum[head : head + 1, :]))
        probs = (logits * weight).astype(BF16)
        intra = jnp.dot(probs, value_ref[:, lanes], preferred_element_type=F32)
        last = STATE_ROWS + head
        got_decay = both_ref[1 - side, last : last + 1, :]
        state = both_ref[1 - side, lanes, :] + got_decay * own_ref[lanes, :]
        total_ref[:, lanes] = intra + own[:, head : head + 1] * times_state(query, state)
        factor_ref[:, lanes] = jnp.broadcast_to(other[:, head : head + 1], (EVENTS, HEAD_DIM))


def stage_kernel(w_hbm, staged_ref, sems):
    copies = [
        pltpu.make_async_copy(w_hbm.at[:, pl.ds(block * COLS, COLS)], staged_ref.at[block], sems.at[block])
        for block in range(D // COLS)
    ]
    for copy in copies:
        copy.start()
    for copy in copies:
        copy.wait()


def block_of(place, far, core):
    return 2 * (((place >> 1) + far) & 3) + core


def first_kernel(
    place_ref,
    query_ref,
    total_ref,
    factor_ref,
    other_ref,
    gain_ref,
    w_ref,
    normed_ref,
    opposite_send_ref,
    opposite_ref,
):
    for head in range(HEADS_DEV):
        lanes = slice(head * HEAD_DIM, (head + 1) * HEAD_DIM)
        total = total_ref[:, lanes] + factor_ref[:, lanes] * times_state(
            query_ref[:, lanes], other_ref[lanes, :]
        )
        average = jnp.mean(total * total, axis=1, keepdims=True)
        scaled = total * lax.rsqrt(average + 1e-06) * gain_ref[:, lanes]
        normed_ref[:, lanes] = scaled.astype(BF16)
    place = place_ref[0]
    core = place & 1
    normed = normed_ref[...]
    for out_ref, whose in ((opposite_send_ref, 1 - core), (opposite_ref, core)):
        out_ref[...] = jnp.dot(normed, w_ref[block_of(place, 2, whose)], preferred_element_type=F32)


def behind_kernel(place_ref, normed_ref, w_ref, send_ref, mine_ref):
    place = place_ref[0]
    core = place & 1
    normed = normed_ref[...]
    for out_ref, whose in ((send_ref, 1 - core), (mine_ref, core)):
        out_ref[...] = jnp.dot(normed, w_ref[block_of(place, 3 - 2 * whose, whose)], preferred_element_type=F32)


def rest_kernel(place_ref, normed_ref, w_ref, ahead_send_ref, ahead_ref, own_send_ref, own_ref):
    place = place_ref[0]
    core = place & 1
    normed = normed_ref[...]
    for out_ref, far, whose in (
        (ahead_send_ref, 3 - 2 * core, 1 - core),
        (ahead_ref, 1 + 2 * core, core),
        (own_send_ref, 0, 1 - core),
        (own_ref, 0, core),
    ):
        out_ref[...] = jnp.dot(normed, w_ref[block_of(place, far, whose)], preferred_element_type=F32)


def core_sum_kernel(place_ref, mine_ref, both_ref, out_ref):
    out_ref[...] = mine_ref[...] + both_ref[1 - (place_ref[0] & 1)]


def three_kernel(place_ref, mine_ref, both_ref, more_ref, out_ref):
    out_ref[...] = mine_ref[...] + both_ref[1 - (place_ref[0] & 1)] + more_ref[...]


def final_kernel(one_ref, two_ref, out_ref):
    out_ref[...] = (one_ref[...] + two_ref[...]).astype(BF16)


def exchange_pieces(packed):
    pieces = packed.reshape(PAIRS, 3, 4, HEAD_DIM)
    pieces = lax.all_to_all(pieces, "ctx", 0, 0, axis_index_groups=SIDE_GROUPS)
    return pieces.reshape(PACKED, HEAD_DIM)


def body(queries, keys, values, state_retention_log, boundary, gain, w_out):
    side = (lax.axis_index("ctx") & 1).reshape(1)
    place = lax.axis_index("tp").reshape(1)
    boundary = boundary.reshape(1, EVENTS)
    gain = gain.reshape(1, 512)
    packed = ((PACKED, HEAD_DIM), F32)
    state = ((STATE_ROWS, HEAD_DIM), F32)

    sent, kept, decay = call(
        terms_kernel,
        [((SENT_ROWS, HEAD_DIM), F32), state, ((HEADS_DEV, HEAD_DIM), F32)],
        (side, keys, values, state_retention_log, boundary),
        scalars=1,
        scratch=[
            pltpu.VMEM((EVENTS, 512), BF16),
            pltpu.VMEM((EVENTS, 512), BF16),
            pltpu.VMEM((HEADS_DEV, EVENTS), F32),
            pltpu.VMEM((1, EVENTS), jnp.int32),
            pltpu.SemaphoreType.DMA((4,)),
        ],
        flops=70_000_000,
        moved=900_000,
        space=pltpu.HBM,
        out_space=pltpu.VMEM,
    )
    both = lax.all_gather(sent, "ctx", axis_index_groups=SIDE_PAIRS)
    (pair_terms,) = call(
        combine_kernel, [packed], (side, kept, both, decay), scalars=1, flops=200_000, moved=1_100_000
    )
    slices = exchange_pieces(pair_terms)
    (states,) = call(scan_kernel, [packed], (side, slices), scalars=1, flops=200_000, moved=600_000)
    (own,) = call(unpack_kernel, [state], (exchange_pieces(states),), moved=600_000)
    own, w_late = lax.optimization_barrier((own, w_out))
    other = lax.ppermute(own, "ctx", SIDE_SWAP)
    (staged,) = call(
        stage_kernel,
        [((D // COLS, 512, COLS), BF16)],
        (w_late,),
        scratch=[pltpu.SemaphoreType.DMA((D // COLS,))],
        moved=12_600_000,
        space=pltpu.HBM,
        out_space=pltpu.VMEM,
    )
    other, staged = lax.optimization_barrier((other, staged))
    inner = ((EVENTS, 512), F32)
    total, factor = call(
        inner_kernel,
        [inner, inner],
        (side, queries, keys, values, state_retention_log, boundary, both, own),
        scalars=1,
        flops=100_000_000,
        moved=1_500_000,
    )
    block = ((EVENTS, COLS), F32)
    two_blocks = ((2, EVENTS, COLS), F32)
    normed, opposite_send, opposite_mine = call(
        first_kernel,
        [((EVENTS, 512), BF16), block, block],
        (place, queries, total, factor, other, gain, staged),
        scalars=1,
        flops=230_000_000,
        moved=4_000_000,
    )

    def core_sum(mine, both):
        return call(core_sum_kernel, [block], (place, mine, both), scalars=1)[0]

    opposite_both = lax.all_gather(opposite_send, "tp", axis_index_groups=CORE_PAIRS)
    opposite = core_sum(opposite_mine, opposite_both)
    opposite, normed = lax.optimization_barrier((opposite, normed))
    ahead_got = lax.ppermute(opposite, "tp", ONWARD)
    behind_send, behind_mine = call(
        behind_kernel, [block, block], (place, normed, staged), scalars=1, flops=200_000_000, moved=2_500_000
    )
    behind_both = lax.all_gather(behind_send, "tp", axis_index_groups=CORE_PAIRS)
    behind_both, normed = lax.optimization_barrier((behind_both, normed))
    behind = core_sum(behind_mine, behind_both)
    one = lax.ppermute(behind, "tp", BACK)
    ahead_send, ahead_mine, own_send, own_mine = call(
        rest_kernel, [block] * 4, (place, normed, staged), scalars=1, flops=400_000_000, moved=5_000_000
    )
    ahead_both = lax.all_gather(ahead_send, "tp", axis_index_groups=CORE_PAIRS)
    own_both = lax.all_gather(own_send, "tp", axis_index_groups=CORE_PAIRS)
    (passed,) = call(three_kernel, [block], (place, ahead_mine, ahead_both, ahead_got), scalars=1)
    two = lax.ppermute(passed, "tp", ONWARD)
    (own_and_one,) = call(three_kernel, [block], (place, own_mine, own_both, one), scalars=1, moved=1_600_000)
    (out,) = call(final_kernel, [((EVENTS, COLS), BF16)], (own_and_one, two), moved=1_000_000)
    return out


def solution(mesh):
    in_specs = (
        P("ctx", "tp"),
        P("ctx", "tp"),
        P("ctx", "tp"),
        P("tp", "ctx"),
        P("ctx"),
        P("tp"),
        P("tp", None),
    )
    out_specs = P("ctx", "tp")
    return jax.shard_map(body, mesh=mesh, in_specs=in_specs, out_specs=out_specs, check_vma=False)
```

```python
import math

import jax
import jax.numpy as jnp
from jax import lax
from jax.experimental import pallas as pl
from jax.experimental.pallas import tpu as pltpu
from jax.sharding import PartitionSpec as P

HEAD_DIM = 128
EVENTS = 128
HEADS_DEV = 4
D = 6144
COLS = 768
PAIRS = 48
PIECES = PAIRS // HEADS_DEV
ROWS = 11
CHUNK = ROWS + 1
HEAD_ROWS = PIECES * CHUNK
PACKED = PAIRS * CHUNK
STATE_ROWS = HEADS_DEV * HEAD_DIM
SENT_ROWS = STATE_ROWS + 8
HALF = EVENTS // 2

surge_log_factor = math.log(0.6)
F32 = jnp.float32
BF16 = jnp.bfloat16
VMEM_LIMIT = 24 * 1024 * 1024

SIDE_GROUPS = [[2 * pair + side for pair in range(PAIRS)] for side in range(2)]
SIDE_SWAP = [(i, i ^ 1) for i in range(2 * PAIRS)]
SIDE_PAIRS = [[i, i + 1] for i in range(0, 2 * PAIRS, 2)]
CORE_SWAP = [(i, i ^ 1) for i in range(8)]
CORE_PAIRS = [[i, i + 1] for i in range(0, 8, 2)]
ONWARD = [(i, (i + (2 if i % 2 == 0 else 6)) % 8) for i in range(8)]
BACK = [(i, (i + (6 if i % 2 == 0 else 2)) % 8) for i in range(8)]


def piece_rows(piece):
    return min(ROWS, HEAD_DIM - ROWS * piece)


def call(kernel, outs, args, scalars=0, scratch=(), flops=0, moved=0, space=pltpu.VMEM, out_space=None):
    specs = [pl.BlockSpec(memory_space=pltpu.SMEM)] * scalars
    specs += [pl.BlockSpec(memory_space=space)] * (len(args) - scalars)
    if space is pltpu.HBM:
        args = args[:scalars] + tuple(pltpu.with_memory_space_constraint(x, space) for x in args[scalars:])
    shapes = [(out_space or jax.ShapeDtypeStruct)(shape, dtype) for shape, dtype in outs]
    return pl.pallas_call(
        kernel,
        out_shape=shapes,
        in_specs=specs,
        out_specs=[pl.BlockSpec(memory_space=out_space or pltpu.VMEM)] * len(outs),
        scratch_shapes=list(scratch),
        compiler_params=pltpu.CompilerParams(vmem_limit_bytes=VMEM_LIMIT),
        cost_estimate=pl.CostEstimate(flops=flops, bytes_accessed=moved, transcendentals=0),
    )(*args)


def event_sums(log_ref, boundary_ref):
    rate = log_ref[...] + surge_log_factor * boundary_ref[...].astype(F32)
    row = lax.broadcasted_iota(jnp.int32, (EVENTS, EVENTS), 0)
    column = lax.broadcasted_iota(jnp.int32, (EVENTS, EVENTS), 1)
    lower = (column <= row).astype(F32)
    upper = (row <= column).astype(F32)
    columns = lax.dot_general(
        lower, rate, (((1,), (1,)), ((), ())), precision=lax.Precision.HIGHEST, preferred_element_type=F32
    )
    return rate, columns, upper


def factors(side, columns):
    ends = columns[EVENTS - 1 : EVENTS, :]
    toward_end = jnp.exp(ends - columns)
    from_start = jnp.exp(columns)
    sent = jnp.where(side == 0, toward_end, from_start)
    kept = jnp.where(side == 0, from_start, toward_end)
    return ends, sent, kept


def halves(wide):
    high = wide.astype(BF16)
    low = (wide - high.astype(F32)).astype(BF16)
    return high, low


def terms_kernel(
    side_ref,
    key_hbm,
    value_hbm,
    log_hbm,
    boundary_hbm,
    sent_ref,
    kept_ref,
    decay_ref,
    key_ref,
    value_ref,
    log_ref,
    boundary_ref,
    sems,
):
    copies = [
        pltpu.make_async_copy(log_hbm, log_ref, sems.at[0]),
        pltpu.make_async_copy(boundary_hbm, boundary_ref, sems.at[1]),
        pltpu.make_async_copy(key_hbm, key_ref, sems.at[2]),
        pltpu.make_async_copy(value_hbm, value_ref, sems.at[3]),
    ]
    for copy in copies:
        copy.start()
    for copy in copies[:2]:
        copy.wait()
    _, columns, _ = event_sums(log_ref, boundary_ref)
    ends, sent, kept = factors(side_ref[0], columns)
    decay = jnp.exp(ends)
    for copy in copies[2:]:
        copy.wait()
    sent_ref[STATE_ROWS:, :] = jnp.zeros((SENT_ROWS - STATE_ROWS, HEAD_DIM), F32)
    for head in range(HEADS_DEV):
        lanes = slice(head * HEAD_DIM, (head + 1) * HEAD_DIM)
        value = value_ref[:, lanes].astype(F32)
        sides = halves(value * sent[:, head : head + 1]) + halves(value * kept[:, head : head + 1])
        product = lax.dot_general(
            key_ref[:, lanes],
            jnp.concatenate(sides, axis=1),
            (((0,), (0,)), ((), ())),
            preferred_element_type=F32,
        )
        sent_ref[lanes, :] = product[:, :128] + product[:, 128:256]
        kept_ref[lanes, :] = product[:, 256:384] + product[:, 384:]
        whole_row = jnp.broadcast_to(decay[:, head : head + 1], (1, HEAD_DIM))
        decay_ref[head : head + 1, :] = whole_row
        sent_ref[STATE_ROWS + head : STATE_ROWS + head + 1, :] = whole_row


def combine_kernel(side_ref, kept_ref, both_ref, decay_ref, out_ref):
    other = 1 - side_ref[0]
    for head in range(HEADS_DEV):
        decay = decay_ref[head : head + 1, :]
        rows = slice(head * HEAD_DIM, (head + 1) * HEAD_DIM)
        state = kept_ref[rows, :] + decay * both_ref[other, rows, :]
        last = STATE_ROWS + head
        decay = decay * both_ref[other, last : last + 1, :]
        for piece in range(PIECES):
            count, first = piece_rows(piece), head * HEAD_ROWS + piece * CHUNK
            part = [state[ROWS * piece : ROWS * piece + count]]
            if count < ROWS:
                part.append(jnp.zeros((ROWS - count, HEAD_DIM), F32))
            out_ref[first : first + CHUNK, :] = jnp.concatenate(part + [decay], axis=0)


def scan_kernel(side_ref, term_ref, out_ref):
    def run(pairs):
        state = jnp.zeros((CHUNK, HEAD_DIM), F32)
        for pair in pairs:
            rows = slice(pair * CHUNK, (pair + 1) * CHUNK)
            out_ref[rows, :] = state
            term = term_ref[rows, :]
            state = term[ROWS:, :] * state + term

    @pl.when(side_ref[0] == 1)
    def _():
        run(range(PAIRS))

    @pl.when(side_ref[0] == 0)
    def _():
        run(range(PAIRS - 1, -1, -1))


def unpack_kernel(packed_ref, state_ref):
    for piece in range(PAIRS):
        head, place = divmod(piece, PIECES)
        first = head * HEAD_DIM + ROWS * place
        count = piece_rows(place)
        state_ref[first : first + count, :] = packed_ref[piece * CHUNK : piece * CHUNK + count, :]


def times_state(query, state):
    product = jnp.dot(query, jnp.concatenate(halves(state), axis=1), preferred_element_type=F32)
    return product[:, :128] + product[:, 128:]


def inner_kernel(
    side_ref, query_ref, key_ref, value_ref, log_ref, boundary_ref, both_ref, own_ref, total_ref, factor_ref
):
    rate, columns, upper = event_sums(log_ref, boundary_ref)
    rows_cum = lax.dot_general(
        rate, upper, (((1,), (0,)), ((), ())), precision=lax.Precision.HIGHEST, preferred_element_type=F32
    )
    side = side_ref[0]
    _, own, other = factors(side, columns)
    for head in range(HEADS_DEV):
        lanes = slice(head * HEAD_DIM, (head + 1) * HEAD_DIM)
        query = query_ref[:, lanes]
        logits = lax.dot_general(
            query, key_ref[:, lanes], (((1,), (1,)), ((), ())), preferred_element_type=F32
        )
        weight = jnp.exp(-jnp.abs(columns[:, head : head + 1] - rows_cum[head : head + 1, :]))
        probs = (logits * weight).astype(BF16)
        intra = jnp.dot(probs, value_ref[:, lanes], preferred_element_type=F32)
        last = STATE_ROWS + head
        got_decay = both_ref[1 - side, last : last + 1, :]
        state = both_ref[1 - side, lanes, :] + got_decay * own_ref[lanes, :]
        total_ref[:, lanes] = intra + own[:, head : head + 1] * times_state(query, state)
        factor_ref[:, lanes] = jnp.broadcast_to(other[:, head : head + 1], (EVENTS, HEAD_DIM))


def stage_kernel(w_hbm, staged_ref, sems):
    copies = [
        pltpu.make_async_copy(w_hbm.at[:, pl.ds(block * COLS, COLS)], staged_ref.at[block], sems.at[block])
        for block in range(D // COLS)
    ]
    for copy in copies:
        copy.start()
    for copy in copies:
        copy.wait()


def block_of(place, far, core):
    return 2 * (((place >> 1) + far) & 3) + core


def first_kernel(
    place_ref,
    query_ref,
    total_ref,
    factor_ref,
    other_ref,
    gain_ref,
    w_ref,
    normed_ref,
    opposite_send_ref,
    opposite_ref,
):
    for head in range(HEADS_DEV):
        lanes = slice(head * HEAD_DIM, (head + 1) * HEAD_DIM)
        total = total_ref[:, lanes] + factor_ref[:, lanes] * times_state(
            query_ref[:, lanes], other_ref[lanes, :]
        )
        average = jnp.mean(total * total, axis=1, keepdims=True)
        scaled = total * lax.rsqrt(average + 1e-06) * gain_ref[:, lanes]
        normed_ref[:, lanes] = scaled.astype(BF16)
    place = place_ref[0]
    core = place & 1
    normed = normed_ref[...]
    for out_ref, whose in ((opposite_send_ref, 1 - core), (opposite_ref, core)):
        out_ref[...] = jnp.dot(normed, w_ref[block_of(place, 2, whose)], preferred_element_type=F32)


def behind_kernel(place_ref, normed_ref, w_ref, send_ref, mine_ref):
    place = place_ref[0]
    core = place & 1
    normed = normed_ref[...]
    for out_ref, whose in ((send_ref, 1 - core), (mine_ref, core)):
        out_ref[...] = jnp.dot(normed, w_ref[block_of(place, 3 - 2 * whose, whose)], preferred_element_type=F32)


def rest_kernel(place_ref, normed_ref, w_ref, ahead_send_ref, ahead_ref, own_send_ref, own_ref):
    place = place_ref[0]
    core = place & 1
    normed = normed_ref[...]
    for out_ref, far, whose in (
        (ahead_send_ref, 3 - 2 * core, 1 - core),
        (ahead_ref, 1 + 2 * core, core),
        (own_send_ref, 0, 1 - core),
        (own_ref, 0, core),
    ):
        out_ref[...] = jnp.dot(normed, w_ref[block_of(place, far, whose)], preferred_element_type=F32)


def core_sum_kernel(place_ref, mine_ref, both_ref, out_ref):
    out_ref[...] = mine_ref[...] + both_ref[1 - (place_ref[0] & 1)]


def core_sum_halves_kernel(place_ref, mine_ref, both_ref, top_ref, bottom_ref):
    total = mine_ref[...] + both_ref[1 - (place_ref[0] & 1)]
    top_ref[...] = total[:HALF]
    bottom_ref[...] = total[HALF:]


def top_kernel(ahead_ref, got_ref, out_ref):
    out_ref[...] = ahead_ref[:HALF] + got_ref[...]


def bottom_kernel(ahead_ref, got_ref, out_ref):
    out_ref[...] = ahead_ref[HALF:] + got_ref[...]


def three_kernel(place_ref, mine_ref, both_ref, more_ref, out_ref):
    out_ref[...] = mine_ref[...] + both_ref[1 - (place_ref[0] & 1)] + more_ref[...]


def final_kernel(one_ref, top_ref, bottom_ref, out_ref):
    out_ref[:HALF] = (one_ref[:HALF] + top_ref[...]).astype(BF16)
    out_ref[HALF:] = (one_ref[HALF:] + bottom_ref[...]).astype(BF16)


def exchange_pieces(packed):
    pieces = packed.reshape(PAIRS, 3, 4, HEAD_DIM)
    pieces = lax.all_to_all(pieces, "ctx", 0, 0, axis_index_groups=SIDE_GROUPS)
    return pieces.reshape(PACKED, HEAD_DIM)


def body(queries, keys, values, state_retention_log, boundary, gain, w_out):
    side = (lax.axis_index("ctx") & 1).reshape(1)
    place = lax.axis_index("tp").reshape(1)
    boundary = boundary.reshape(1, EVENTS)
    gain = gain.reshape(1, 512)
    packed = ((PACKED, HEAD_DIM), F32)
    state = ((STATE_ROWS, HEAD_DIM), F32)

    sent, kept, decay = call(
        terms_kernel,
        [((SENT_ROWS, HEAD_DIM), F32), state, ((HEADS_DEV, HEAD_DIM), F32)],
        (side, keys, values, state_retention_log, boundary),
        scalars=1,
        scratch=[
            pltpu.VMEM((EVENTS, 512), BF16),
            pltpu.VMEM((EVENTS, 512), BF16),
            pltpu.VMEM((HEADS_DEV, EVENTS), F32),
            pltpu.VMEM((1, EVENTS), jnp.int32),
            pltpu.SemaphoreType.DMA((4,)),
        ],
        flops=70_000_000,
        moved=900_000,
        space=pltpu.HBM,
        out_space=pltpu.VMEM,
    )
    both = lax.all_gather(sent, "ctx", axis_index_groups=SIDE_PAIRS)
    (pair_terms,) = call(
        combine_kernel, [packed], (side, kept, both, decay), scalars=1, flops=200_000, moved=1_100_000
    )
    slices = exchange_pieces(pair_terms)
    (states,) = call(scan_kernel, [packed], (side, slices), scalars=1, flops=200_000, moved=600_000)
    (own,) = call(unpack_kernel, [state], (exchange_pieces(states),), moved=600_000)
    own, w_late = lax.optimization_barrier((own, w_out))
    other = lax.ppermute(own, "ctx", SIDE_SWAP)
    (staged,) = call(
        stage_kernel,
        [((D // COLS, 512, COLS), BF16)],
        (w_late,),
        scratch=[pltpu.SemaphoreType.DMA((D // COLS,))],
        moved=12_600_000,
        space=pltpu.HBM,
        out_space=pltpu.VMEM,
    )
    other, staged = lax.optimization_barrier((other, staged))
    inner = ((EVENTS, 512), F32)
    total, factor = call(
        inner_kernel,
        [inner, inner],
        (side, queries, keys, values, state_retention_log, boundary, both, own),
        scalars=1,
        flops=100_000_000,
        moved=1_500_000,
    )
    block = ((EVENTS, COLS), F32)
    two_blocks = ((2, EVENTS, COLS), F32)
    normed, opposite_send, opposite_mine = call(
        first_kernel,
        [((EVENTS, 512), BF16), block, block],
        (place, queries, total, factor, other, gain, staged),
        scalars=1,
        flops=230_000_000,
        moved=4_000_000,
    )

    def core_sum(mine, both):
        return call(core_sum_kernel, [block], (place, mine, both), scalars=1)[0]

    opposite_both = lax.all_gather(opposite_send, "tp", axis_index_groups=CORE_PAIRS)
    half = ((HALF, COLS), F32)
    top, bottom = call(
        core_sum_halves_kernel, [half, half], (place, opposite_mine, opposite_both), scalars=1
    )
    top, bottom, normed = lax.optimization_barrier((top, bottom, normed))
    top_got = lax.ppermute(top, "tp", ONWARD)
    bottom_got = lax.ppermute(bottom, "tp", ONWARD)
    behind_send, behind_mine = call(
        behind_kernel, [block, block], (place, normed, staged), scalars=1, flops=200_000_000, moved=2_500_000
    )
    behind_both = lax.all_gather(behind_send, "tp", axis_index_groups=CORE_PAIRS)
    behind_both, normed = lax.optimization_barrier((behind_both, normed))
    behind = core_sum(behind_mine, behind_both)
    one = lax.ppermute(behind, "tp", BACK)
    ahead_send, ahead_mine, own_send, own_mine = call(
        rest_kernel, [block] * 4, (place, normed, staged), scalars=1, flops=400_000_000, moved=5_000_000
    )
    ahead_both = lax.all_gather(ahead_send, "tp", axis_index_groups=CORE_PAIRS)
    own_both = lax.all_gather(own_send, "tp", axis_index_groups=CORE_PAIRS)
    ahead = core_sum(ahead_mine, ahead_both)
    (top,) = call(top_kernel, [half], (ahead, top_got))
    top_two = lax.ppermute(top, "tp", ONWARD)
    (bottom,) = call(bottom_kernel, [half], (ahead, bottom_got))
    bottom_two = lax.ppermute(bottom, "tp", ONWARD)
    (own_and_one,) = call(three_kernel, [block], (place, own_mine, own_both, one), scalars=1, moved=1_600_000)
    (out,) = call(
        final_kernel, [((EVENTS, COLS), BF16)], (own_and_one, top_two, bottom_two), moved=1_000_000
    )
    return out


def solution(mesh):
    in_specs = (
        P("ctx", "tp"),
        P("ctx", "tp"),
        P("ctx", "tp"),
        P("tp", "ctx"),
        P("ctx"),
        P("tp"),
        P("tp", None),
    )
    out_specs = P("ctx", "tp")
    return jax.shard_map(body, mesh=mesh, in_specs=in_specs, out_specs=out_specs, check_vma=False)
```

```python
import math

import jax
import jax.numpy as jnp
from jax import lax
from jax.experimental import pallas as pl
from jax.experimental.pallas import tpu as pltpu
from jax.sharding import PartitionSpec as P

HEAD_DIM = 128
EVENTS = 128
HEADS_DEV = 4
D = 6144
COLS = 768
PAIRS = 48
PIECES = PAIRS // HEADS_DEV
ROWS = 11
CHUNK = ROWS + 1
HEAD_ROWS = PIECES * CHUNK
PACKED = PAIRS * CHUNK
STATE_ROWS = HEADS_DEV * HEAD_DIM
SENT_ROWS = STATE_ROWS + 8
HALF = EVENTS // 2
RING = 4

surge_log_factor = math.log(0.6)
F32 = jnp.float32
BF16 = jnp.bfloat16
VMEM_LIMIT = 24 * 1024 * 1024

SIDE_GROUPS = [[2 * pair + side for pair in range(PAIRS)] for side in range(2)]
SIDE_SWAP = [(i, i ^ 1) for i in range(2 * PAIRS)]
SIDE_PAIRS = [[i, i + 1] for i in range(0, 2 * PAIRS, 2)]
CORE_SWAP = [(i, i ^ 1) for i in range(8)]
CORE_PAIRS = [[i, i + 1] for i in range(0, 8, 2)]
ONWARD = [(i, (i + (2 if i % 2 == 0 else 6)) % 8) for i in range(8)]
BACK = [(i, (i + (6 if i % 2 == 0 else 2)) % 8) for i in range(8)]


def piece_rows(piece):
    return min(ROWS, HEAD_DIM - ROWS * piece)


def call(kernel, outs, args, scalars=0, scratch=(), flops=0, moved=0, space=pltpu.VMEM, out_space=None):
    specs = [pl.BlockSpec(memory_space=pltpu.SMEM)] * scalars
    specs += [pl.BlockSpec(memory_space=space)] * (len(args) - scalars)
    if space is pltpu.HBM:
        args = args[:scalars] + tuple(pltpu.with_memory_space_constraint(x, space) for x in args[scalars:])
    shapes = [(out_space or jax.ShapeDtypeStruct)(shape, dtype) for shape, dtype in outs]
    return pl.pallas_call(
        kernel,
        out_shape=shapes,
        in_specs=specs,
        out_specs=[pl.BlockSpec(memory_space=out_space or pltpu.VMEM)] * len(outs),
        scratch_shapes=list(scratch),
        compiler_params=pltpu.CompilerParams(vmem_limit_bytes=VMEM_LIMIT),
        cost_estimate=pl.CostEstimate(flops=flops, bytes_accessed=moved, transcendentals=0),
    )(*args)


def event_sums(log_ref, boundary_ref):
    rate = log_ref[...] + surge_log_factor * boundary_ref[...].astype(F32)
    row = lax.broadcasted_iota(jnp.int32, (EVENTS, EVENTS), 0)
    column = lax.broadcasted_iota(jnp.int32, (EVENTS, EVENTS), 1)
    lower = (column <= row).astype(F32)
    upper = (row <= column).astype(F32)
    columns = lax.dot_general(
        lower, rate, (((1,), (1,)), ((), ())), precision=lax.Precision.HIGHEST, preferred_element_type=F32
    )
    return rate, columns, upper


def factors(side, columns):
    ends = columns[EVENTS - 1 : EVENTS, :]
    toward_end = jnp.exp(ends - columns)
    from_start = jnp.exp(columns)
    sent = jnp.where(side == 0, toward_end, from_start)
    kept = jnp.where(side == 0, from_start, toward_end)
    return ends, sent, kept


def halves(wide):
    high = wide.astype(BF16)
    low = (wide - high.astype(F32)).astype(BF16)
    return high, low


def terms_kernel(
    side_ref,
    key_hbm,
    value_hbm,
    log_hbm,
    boundary_hbm,
    sent_ref,
    kept_ref,
    decay_ref,
    key_ref,
    value_ref,
    log_ref,
    boundary_ref,
    sems,
):
    copies = [
        pltpu.make_async_copy(log_hbm, log_ref, sems.at[0]),
        pltpu.make_async_copy(boundary_hbm, boundary_ref, sems.at[1]),
        pltpu.make_async_copy(key_hbm, key_ref, sems.at[2]),
        pltpu.make_async_copy(value_hbm, value_ref, sems.at[3]),
    ]
    for copy in copies:
        copy.start()
    for copy in copies[:2]:
        copy.wait()
    _, columns, _ = event_sums(log_ref, boundary_ref)
    ends, sent, kept = factors(side_ref[0], columns)
    decay = jnp.exp(ends)
    for copy in copies[2:]:
        copy.wait()
    sent_ref[STATE_ROWS:, :] = jnp.zeros((SENT_ROWS - STATE_ROWS, HEAD_DIM), F32)
    for head in range(HEADS_DEV):
        lanes = slice(head * HEAD_DIM, (head + 1) * HEAD_DIM)
        value = value_ref[:, lanes].astype(F32)
        sides = halves(value * sent[:, head : head + 1]) + halves(value * kept[:, head : head + 1])
        product = lax.dot_general(
            key_ref[:, lanes],
            jnp.concatenate(sides, axis=1),
            (((0,), (0,)), ((), ())),
            preferred_element_type=F32,
        )
        sent_ref[lanes, :] = product[:, :128] + product[:, 128:256]
        kept_ref[lanes, :] = product[:, 256:384] + product[:, 384:]
        whole_row = jnp.broadcast_to(decay[:, head : head + 1], (1, HEAD_DIM))
        decay_ref[head : head + 1, :] = whole_row
        sent_ref[STATE_ROWS + head : STATE_ROWS + head + 1, :] = whole_row


def combine_kernel(side_ref, kept_ref, both_ref, decay_ref, out_ref):
    other = 1 - side_ref[0]
    for head in range(HEADS_DEV):
        decay = decay_ref[head : head + 1, :]
        rows = slice(head * HEAD_DIM, (head + 1) * HEAD_DIM)
        state = kept_ref[rows, :] + decay * both_ref[other, rows, :]
        last = STATE_ROWS + head
        decay = decay * both_ref[other, last : last + 1, :]
        for piece in range(PIECES):
            count, first = piece_rows(piece), head * HEAD_ROWS + piece * CHUNK
            part = [state[ROWS * piece : ROWS * piece + count]]
            if count < ROWS:
                part.append(jnp.zeros((ROWS - count, HEAD_DIM), F32))
            out_ref[first : first + CHUNK, :] = jnp.concatenate(part + [decay], axis=0)


def scan_kernel(side_ref, term_ref, out_ref):
    def run(pairs):
        state = jnp.zeros((CHUNK, HEAD_DIM), F32)
        for pair in pairs:
            rows = slice(pair * CHUNK, (pair + 1) * CHUNK)
            out_ref[rows, :] = state
            term = term_ref[rows, :]
            state = term[ROWS:, :] * state + term

    @pl.when(side_ref[0] == 1)
    def _():
        run(range(PAIRS))

    @pl.when(side_ref[0] == 0)
    def _():
        run(range(PAIRS - 1, -1, -1))


def unpack_kernel(packed_ref, state_ref):
    for piece in range(PAIRS):
        head, place = divmod(piece, PIECES)
        first = head * HEAD_DIM + ROWS * place
        count = piece_rows(place)
        state_ref[first : first + count, :] = packed_ref[piece * CHUNK : piece * CHUNK + count, :]


def times_state(query, state):
    product = jnp.dot(query, jnp.concatenate(halves(state), axis=1), preferred_element_type=F32)
    return product[:, :128] + product[:, 128:]


def inner_kernel(
    side_ref, query_ref, key_ref, value_ref, log_ref, boundary_ref, both_ref, own_ref, total_ref, factor_ref
):
    rate, columns, upper = event_sums(log_ref, boundary_ref)
    rows_cum = lax.dot_general(
        rate, upper, (((1,), (0,)), ((), ())), precision=lax.Precision.HIGHEST, preferred_element_type=F32
    )
    side = side_ref[0]
    _, own, other = factors(side, columns)
    for head in range(HEADS_DEV):
        lanes = slice(head * HEAD_DIM, (head + 1) * HEAD_DIM)
        query = query_ref[:, lanes]
        logits = lax.dot_general(
            query, key_ref[:, lanes], (((1,), (1,)), ((), ())), preferred_element_type=F32
        )
        weight = jnp.exp(-jnp.abs(columns[:, head : head + 1] - rows_cum[head : head + 1, :]))
        probs = (logits * weight).astype(BF16)
        intra = jnp.dot(probs, value_ref[:, lanes], preferred_element_type=F32)
        last = STATE_ROWS + head
        got_decay = both_ref[1 - side, last : last + 1, :]
        state = both_ref[1 - side, lanes, :] + got_decay * own_ref[lanes, :]
        total_ref[:, lanes] = intra + own[:, head : head + 1] * times_state(query, state)
        factor_ref[:, lanes] = jnp.broadcast_to(other[:, head : head + 1], (EVENTS, HEAD_DIM))


def widen_kernel(place_ref, w_hbm, wide_hbm, narrow_ref, wide_ref, sems):
    core = place_ref[0] & 1
    incoming, outgoing = [], []
    for t in range(RING):
        columns = pl.ds(pl.multiple_of((2 * t + 1 - core) * COLS, COLS), COLS)
        incoming.append(pltpu.make_async_copy(w_hbm.at[:, columns], narrow_ref.at[t], sems.at[t]))
        outgoing.append(pltpu.make_async_copy(wide_ref.at[t], wide_hbm.at[t], sems.at[RING + t]))
    for copy in incoming:
        copy.start()
    for t in range(RING):
        incoming[t].wait()
        wide_ref[t] = narrow_ref[t].astype(F32)
        outgoing[t].start()
    for copy in outgoing:
        copy.wait()


def stage_kernel(place_ref, w_hbm, wide_ref, staged_ref, sems):
    rows = w_hbm.shape[0]
    core = place_ref[0] & 1
    copies = []
    for t in range(RING):
        columns = pl.ds(pl.multiple_of((2 * t + core) * COLS, COLS), COLS)
        copies.append(
            pltpu.make_async_copy(w_hbm.at[:, columns], staged_ref.at[t, pl.ds(0, rows)], sems.at[t])
        )
    for copy in copies:
        copy.start()
    for t in range(RING):
        staged_ref[t, rows:, :] = wide_ref[t].astype(BF16)
    for copy in copies:
        copy.wait()


def stage(place, w_out, wide):
    return pl.pallas_call(
        stage_kernel,
        in_specs=[
            pl.BlockSpec(memory_space=pltpu.SMEM),
            pl.BlockSpec(memory_space=pltpu.HBM),
            pl.BlockSpec(memory_space=pltpu.VMEM),
        ],
        out_specs=pl.BlockSpec(memory_space=pltpu.VMEM),
        out_shape=pltpu.VMEM((RING, 2 * w_out.shape[0], COLS), BF16),
        scratch_shapes=[pltpu.SemaphoreType.DMA((RING,))],
        compiler_params=pltpu.CompilerParams(vmem_limit_bytes=VMEM_LIMIT),
        cost_estimate=pl.CostEstimate(flops=0, bytes_accessed=16_000_000, transcendentals=0),
    )(place, pltpu.with_memory_space_constraint(w_out, pltpu.HBM), wide)


def normed_kernel(query_ref, total_ref, factor_ref, other_ref, gain_ref, normed_ref):
    for head in range(HEADS_DEV):
        lanes = slice(head * HEAD_DIM, (head + 1) * HEAD_DIM)
        total = total_ref[:, lanes] + factor_ref[:, lanes] * times_state(
            query_ref[:, lanes], other_ref[lanes, :]
        )
        average = jnp.mean(total * total, axis=1, keepdims=True)
        scaled = total * lax.rsqrt(average + 1e-06) * gain_ref[:, lanes]
        normed_ref[:, lanes] = scaled.astype(BF16).astype(F32)


def project(place, both_ref, w_ref, far):
    core = place & 1
    normed = jnp.concatenate([both_ref[core].astype(BF16), both_ref[1 - core].astype(BF16)], axis=1)
    return jnp.dot(normed, w_ref[((place >> 1) + far) & 3], preferred_element_type=F32)


def opposite_kernel(place_ref, both_ref, w_ref, top_ref, bottom_ref):
    total = project(place_ref[0], both_ref, w_ref, 2)
    top_ref[...] = total[:HALF]
    bottom_ref[...] = total[HALF:]


def behind_kernel(place_ref, both_ref, w_ref, out_ref):
    place = place_ref[0]
    out_ref[...] = project(place, both_ref, w_ref, 3 - 2 * (place & 1))


def ahead_kernel(place_ref, both_ref, w_ref, out_ref):
    place = place_ref[0]
    out_ref[...] = project(place, both_ref, w_ref, 1 + 2 * (place & 1))


def top_kernel(ahead_ref, got_ref, out_ref):
    out_ref[...] = ahead_ref[:HALF] + got_ref[...]


def bottom_kernel(ahead_ref, got_ref, out_ref):
    out_ref[...] = ahead_ref[HALF:] + got_ref[...]


def own_kernel(place_ref, both_ref, w_ref, got_ref, out_ref):
    out_ref[...] = project(place_ref[0], both_ref, w_ref, 0) + got_ref[...]


def final_kernel(one_ref, top_ref, bottom_ref, out_ref):
    out_ref[:HALF] = (one_ref[:HALF] + top_ref[...]).astype(BF16)
    out_ref[HALF:] = (one_ref[HALF:] + bottom_ref[...]).astype(BF16)


def exchange_pieces(packed):
    pieces = packed.reshape(PAIRS, 3, 4, HEAD_DIM)
    pieces = lax.all_to_all(pieces, "ctx", 0, 0, axis_index_groups=SIDE_GROUPS)
    return pieces.reshape(PACKED, HEAD_DIM)


def body(queries, keys, values, state_retention_log, boundary, gain, w_out):
    side = (lax.axis_index("ctx") & 1).reshape(1)
    place = lax.axis_index("tp").reshape(1)
    boundary = boundary.reshape(1, EVENTS)
    gain = gain.reshape(1, 512)
    packed = ((PACKED, HEAD_DIM), F32)
    state = ((STATE_ROWS, HEAD_DIM), F32)

    sent, kept, decay = call(
        terms_kernel,
        [((SENT_ROWS, HEAD_DIM), F32), state, ((HEADS_DEV, HEAD_DIM), F32)],
        (side, keys, values, state_retention_log, boundary),
        scalars=1,
        scratch=[
            pltpu.VMEM((EVENTS, 512), BF16),
            pltpu.VMEM((EVENTS, 512), BF16),
            pltpu.VMEM((HEADS_DEV, EVENTS), F32),
            pltpu.VMEM((1, EVENTS), jnp.int32),
            pltpu.SemaphoreType.DMA((4,)),
        ],
        flops=70_000_000,
        moved=900_000,
        space=pltpu.HBM,
        out_space=pltpu.VMEM,
    )
    both = lax.all_gather(sent, "ctx", axis_index_groups=SIDE_PAIRS)
    (pair_terms,) = call(
        combine_kernel, [packed], (side, kept, both, decay), scalars=1, flops=200_000, moved=1_100_000
    )
    pair_terms, w_late = lax.optimization_barrier((pair_terms, w_out))
    (wide,) = call(
        widen_kernel,
        [((RING, 512, COLS), F32)],
        (place, w_late),
        scalars=1,
        scratch=[
            pltpu.VMEM((RING, 512, COLS), BF16),
            pltpu.VMEM((RING, 512, COLS), F32),
            pltpu.SemaphoreType.DMA((2 * RING,)),
        ],
        moved=9_500_000,
        space=pltpu.HBM,
        out_space=pltpu.HBM,
    )
    wide_got = lax.ppermute(wide, "tp", CORE_SWAP)
    slices = exchange_pieces(pair_terms)
    (states,) = call(scan_kernel, [packed], (side, slices), scalars=1, flops=50_000_000_000, moved=600_000)
    (own,) = call(unpack_kernel, [state], (exchange_pieces(states),), moved=600_000)
    own, w_late = lax.optimization_barrier((own, w_late))
    other = lax.ppermute(own, "ctx", SIDE_SWAP)
    staged = stage(place, w_late, wide_got)
    other, staged = lax.optimization_barrier((other, staged))
    inner = ((EVENTS, 512), F32)
    total, factor = call(
        inner_kernel,
        [inner, inner],
        (side, queries, keys, values, state_retention_log, boundary, both, own),
        scalars=1,
        flops=100_000_000,
        moved=1_500_000,
    )
    block = ((EVENTS, COLS), F32)
    half = ((HALF, COLS), F32)
    (normed,) = call(
        normed_kernel, [inner], (queries, total, factor, other, gain), flops=70_000_000, moved=1_300_000
    )
    both_normed = lax.all_gather(normed, "tp", axis_index_groups=CORE_PAIRS)

    def step(kernel, outs, *args):
        args = (place, both_normed, staged) + args
        return call(kernel, outs, args, scalars=1)

    top, bottom = step(opposite_kernel, [half, half])
    top, bottom, both_normed = lax.optimization_barrier((top, bottom, both_normed))
    top_got = lax.ppermute(top, "tp", ONWARD)
    bottom_got = lax.ppermute(bottom, "tp", ONWARD)
    (behind,) = step(behind_kernel, [block])
    one = lax.ppermute(behind, "tp", BACK)
    (ahead,) = step(ahead_kernel, [block])
    (top,) = call(top_kernel, [half], (ahead, top_got))
    top_two = lax.ppermute(top, "tp", ONWARD)
    (bottom,) = call(bottom_kernel, [half], (ahead, bottom_got))
    bottom_two = lax.ppermute(bottom, "tp", ONWARD)
    (own_and_one,) = step(own_kernel, [block], one)
    (out,) = call(
        final_kernel, [((EVENTS, COLS), BF16)], (own_and_one, top_two, bottom_two), moved=1_000_000
    )
    return out


def solution(mesh):
    in_specs = (
        P("ctx", "tp"),
        P("ctx", "tp"),
        P("ctx", "tp"),
        P("tp", "ctx"),
        P("ctx"),
        P("tp"),
        P("tp", None),
    )
    out_specs = P("ctx", "tp")
    return jax.shard_map(body, mesh=mesh, in_specs=in_specs, out_specs=out_specs, check_vma=False)
```

```python
import math

import jax
import jax.numpy as jnp
from jax import lax
from jax.experimental import pallas as pl
from jax.experimental.pallas import tpu as pltpu
from jax.sharding import PartitionSpec as P

HEAD_DIM = 128
EVENTS = 128
HEADS_DEV = 4
D = 6144
COLS = 768
PAIRS = 48
PIECES = PAIRS // HEADS_DEV
ROWS = 11
CHUNK = ROWS + 1
HEAD_ROWS = PIECES * CHUNK
PACKED = PAIRS * CHUNK
STATE_ROWS = HEADS_DEV * HEAD_DIM
SENT_ROWS = STATE_ROWS + 8

surge_log_factor = math.log(0.6)
F32 = jnp.float32
BF16 = jnp.bfloat16
VMEM_LIMIT = 24 * 1024 * 1024

SIDE_GROUPS = [[2 * pair + side for pair in range(PAIRS)] for side in range(2)]
SIDE_SWAP = [(i, i ^ 1) for i in range(2 * PAIRS)]
SIDE_PAIRS = [[i, i + 1] for i in range(0, 2 * PAIRS, 2)]
CORE_SWAP = [(i, i ^ 1) for i in range(8)]
CORE_PAIRS = [[i, i + 1] for i in range(0, 8, 2)]
ONWARD = [(i, (i + (2 if i % 2 == 0 else 6)) % 8) for i in range(8)]
BACK = [(i, (i + (6 if i % 2 == 0 else 2)) % 8) for i in range(8)]


def piece_rows(piece):
    return min(ROWS, HEAD_DIM - ROWS * piece)


def call(kernel, outs, args, scalars=0, scratch=(), flops=0, moved=0, space=pltpu.VMEM, out_space=None):
    specs = [pl.BlockSpec(memory_space=pltpu.SMEM)] * scalars
    specs += [pl.BlockSpec(memory_space=space)] * (len(args) - scalars)
    if space is pltpu.HBM:
        args = args[:scalars] + tuple(pltpu.with_memory_space_constraint(x, space) for x in args[scalars:])
    shapes = [(out_space or jax.ShapeDtypeStruct)(shape, dtype) for shape, dtype in outs]
    return pl.pallas_call(
        kernel,
        out_shape=shapes,
        in_specs=specs,
        out_specs=[pl.BlockSpec(memory_space=out_space or pltpu.VMEM)] * len(outs),
        scratch_shapes=list(scratch),
        compiler_params=pltpu.CompilerParams(vmem_limit_bytes=VMEM_LIMIT),
        cost_estimate=pl.CostEstimate(flops=flops, bytes_accessed=moved, transcendentals=0),
    )(*args)


def event_sums(log_ref, boundary_ref):
    rate = log_ref[...] + surge_log_factor * boundary_ref[...].astype(F32)
    row = lax.broadcasted_iota(jnp.int32, (EVENTS, EVENTS), 0)
    column = lax.broadcasted_iota(jnp.int32, (EVENTS, EVENTS), 1)
    lower = (column <= row).astype(F32)
    upper = (row <= column).astype(F32)
    columns = lax.dot_general(
        lower, rate, (((1,), (1,)), ((), ())), precision=lax.Precision.HIGHEST, preferred_element_type=F32
    )
    return rate, columns, upper


def factors(side, columns):
    ends = columns[EVENTS - 1 : EVENTS, :]
    toward_end = jnp.exp(ends - columns)
    from_start = jnp.exp(columns)
    sent = jnp.where(side == 0, toward_end, from_start)
    kept = jnp.where(side == 0, from_start, toward_end)
    return ends, sent, kept


def halves(wide):
    high = wide.astype(BF16)
    low = (wide - high.astype(F32)).astype(BF16)
    return high, low


def terms_kernel(
    side_ref,
    key_hbm,
    value_hbm,
    log_hbm,
    boundary_hbm,
    sent_ref,
    kept_ref,
    decay_ref,
    key_ref,
    value_ref,
    log_ref,
    boundary_ref,
    sems,
):
    copies = [
        pltpu.make_async_copy(log_hbm, log_ref, sems.at[0]),
        pltpu.make_async_copy(boundary_hbm, boundary_ref, sems.at[1]),
        pltpu.make_async_copy(key_hbm, key_ref, sems.at[2]),
        pltpu.make_async_copy(value_hbm, value_ref, sems.at[3]),
    ]
    for copy in copies:
        copy.start()
    for copy in copies[:2]:
        copy.wait()
    _, columns, _ = event_sums(log_ref, boundary_ref)
    ends, sent, kept = factors(side_ref[0], columns)
    decay = jnp.exp(ends)
    for copy in copies[2:]:
        copy.wait()
    sent_ref[STATE_ROWS:, :] = jnp.zeros((SENT_ROWS - STATE_ROWS, HEAD_DIM), F32)
    for head in range(HEADS_DEV):
        lanes = slice(head * HEAD_DIM, (head + 1) * HEAD_DIM)
        value = value_ref[:, lanes].astype(F32)
        sides = halves(value * sent[:, head : head + 1]) + halves(value * kept[:, head : head + 1])
        product = lax.dot_general(
            key_ref[:, lanes],
            jnp.concatenate(sides, axis=1),
            (((0,), (0,)), ((), ())),
            preferred_element_type=F32,
        )
        sent_ref[lanes, :] = product[:, :128] + product[:, 128:256]
        kept_ref[lanes, :] = product[:, 256:384] + product[:, 384:]
        whole_row = jnp.broadcast_to(decay[:, head : head + 1], (1, HEAD_DIM))
        decay_ref[head : head + 1, :] = whole_row
        sent_ref[STATE_ROWS + head : STATE_ROWS + head + 1, :] = whole_row


def combine_kernel(side_ref, kept_ref, both_ref, decay_ref, out_ref):
    other = 1 - side_ref[0]
    for head in range(HEADS_DEV):
        decay = decay_ref[head : head + 1, :]
        rows = slice(head * HEAD_DIM, (head + 1) * HEAD_DIM)
        state = kept_ref[rows, :] + decay * both_ref[other, rows, :]
        last = STATE_ROWS + head
        decay = decay * both_ref[other, last : last + 1, :]
        for piece in range(PIECES):
            count, first = piece_rows(piece), head * HEAD_ROWS + piece * CHUNK
            part = [state[ROWS * piece : ROWS * piece + count]]
            if count < ROWS:
                part.append(jnp.zeros((ROWS - count, HEAD_DIM), F32))
            out_ref[first : first + CHUNK, :] = jnp.concatenate(part + [decay], axis=0)


def scan_kernel(side_ref, term_ref, out_ref):
    def run(pairs):
        state = jnp.zeros((CHUNK, HEAD_DIM), F32)
        for pair in pairs:
            out_ref[pair * ROWS : (pair + 1) * ROWS, :] = state[:ROWS]
            term = term_ref[pair * CHUNK : (pair + 1) * CHUNK, :]
            state = term[ROWS:, :] * state + term

    @pl.when(side_ref[0] == 1)
    def _():
        run(range(PAIRS))

    @pl.when(side_ref[0] == 0)
    def _():
        run(range(PAIRS - 1, -1, -1))


def state_rows(head):
    return slice(head * PIECES * ROWS, head * PIECES * ROWS + HEAD_DIM)


def times_state(query, state):
    product = jnp.dot(query, jnp.concatenate(halves(state), axis=1), preferred_element_type=F32)
    return product[:, :128] + product[:, 128:]


def inner_kernel(
    side_ref, query_ref, key_ref, value_ref, log_ref, boundary_ref, both_ref, own_ref, total_ref, factor_ref
):
    rate, columns, upper = event_sums(log_ref, boundary_ref)
    rows_cum = lax.dot_general(
        rate, upper, (((1,), (0,)), ((), ())), precision=lax.Precision.HIGHEST, preferred_element_type=F32
    )
    side = side_ref[0]
    _, own, other = factors(side, columns)
    for head in range(HEADS_DEV):
        lanes = slice(head * HEAD_DIM, (head + 1) * HEAD_DIM)
        query = query_ref[:, lanes]
        logits = lax.dot_general(
            query, key_ref[:, lanes], (((1,), (1,)), ((), ())), preferred_element_type=F32
        )
        weight = jnp.exp(-jnp.abs(columns[:, head : head + 1] - rows_cum[head : head + 1, :]))
        probs = (logits * weight).astype(BF16)
        intra = jnp.dot(probs, value_ref[:, lanes], preferred_element_type=F32)
        last = STATE_ROWS + head
        got_decay = both_ref[1 - side, last : last + 1, :]
        state = both_ref[1 - side, lanes, :] + got_decay * own_ref[state_rows(head), :]
        total_ref[:, lanes] = intra + own[:, head : head + 1] * times_state(query, state)
        factor_ref[:, lanes] = jnp.broadcast_to(other[:, head : head + 1], (EVENTS, HEAD_DIM))


def stage_kernel(w_hbm, staged_ref, sems):
    copies = [
        pltpu.make_async_copy(w_hbm.at[:, pl.ds(block * COLS, COLS)], staged_ref.at[block], sems.at[block])
        for block in range(D // COLS)
    ]
    for copy in copies:
        copy.start()
    for copy in copies:
        copy.wait()


def block_of(place, far, core):
    return 2 * (((place >> 1) + far) & 3) + core


def first_kernel(
    place_ref,
    query_ref,
    total_ref,
    factor_ref,
    other_ref,
    gain_ref,
    w_ref,
    normed_ref,
    opposite_send_ref,
    opposite_ref,
):
    for head in range(HEADS_DEV):
        lanes = slice(head * HEAD_DIM, (head + 1) * HEAD_DIM)
        total = total_ref[:, lanes] + factor_ref[:, lanes] * times_state(
            query_ref[:, lanes], other_ref[state_rows(head), :]
        )
        average = jnp.mean(total * total, axis=1, keepdims=True)
        scaled = total * lax.rsqrt(average + 1e-06) * gain_ref[:, lanes]
        normed_ref[:, lanes] = scaled.astype(BF16)
    place = place_ref[0]
    core = place & 1
    normed = normed_ref[...]
    for out_ref, whose in ((opposite_send_ref, 1 - core), (opposite_ref, core)):
        out_ref[...] = jnp.dot(normed, w_ref[block_of(place, 2, whose)], preferred_element_type=F32)


def behind_kernel(place_ref, normed_ref, w_ref, send_ref, mine_ref):
    place = place_ref[0]
    core = place & 1
    normed = normed_ref[...]
    for out_ref, whose in ((send_ref, 1 - core), (mine_ref, core)):
        out_ref[...] = jnp.dot(normed, w_ref[block_of(place, 3 - 2 * whose, whose)], preferred_element_type=F32)


def rest_kernel(place_ref, normed_ref, w_ref, ahead_send_ref, ahead_ref, own_send_ref, own_ref):
    place = place_ref[0]
    core = place & 1
    normed = normed_ref[...]
    for out_ref, far, whose in (
        (ahead_send_ref, 3 - 2 * core, 1 - core),
        (ahead_ref, 1 + 2 * core, core),
        (own_send_ref, 0, 1 - core),
        (own_ref, 0, core),
    ):
        out_ref[...] = jnp.dot(normed, w_ref[block_of(place, far, whose)], preferred_element_type=F32)


def core_sum_kernel(place_ref, mine_ref, both_ref, out_ref):
    out_ref[...] = mine_ref[...] + both_ref[1 - (place_ref[0] & 1)]


def three_kernel(place_ref, mine_ref, both_ref, more_ref, out_ref):
    out_ref[...] = mine_ref[...] + both_ref[1 - (place_ref[0] & 1)] + more_ref[...]


def final_kernel(one_ref, two_ref, out_ref):
    out_ref[...] = (one_ref[...] + two_ref[...]).astype(BF16)


def exchange_pieces(packed, shape):
    pieces = packed.reshape((PAIRS,) + shape + (HEAD_DIM,))
    pieces = lax.all_to_all(pieces, "ctx", 0, 0, axis_index_groups=SIDE_GROUPS)
    return pieces.reshape(packed.shape)


def body(queries, keys, values, state_retention_log, boundary, gain, w_out):
    side = (lax.axis_index("ctx") & 1).reshape(1)
    place = lax.axis_index("tp").reshape(1)
    boundary = boundary.reshape(1, EVENTS)
    gain = gain.reshape(1, 512)
    packed = ((PACKED, HEAD_DIM), F32)
    state = ((STATE_ROWS, HEAD_DIM), F32)

    sent, kept, decay = call(
        terms_kernel,
        [((SENT_ROWS, HEAD_DIM), F32), state, ((HEADS_DEV, HEAD_DIM), F32)],
        (side, keys, values, state_retention_log, boundary),
        scalars=1,
        scratch=[
            pltpu.VMEM((EVENTS, 512), BF16),
            pltpu.VMEM((EVENTS, 512), BF16),
            pltpu.VMEM((HEADS_DEV, EVENTS), F32),
            pltpu.VMEM((1, EVENTS), jnp.int32),
            pltpu.SemaphoreType.DMA((4,)),
        ],
        flops=70_000_000,
        moved=900_000,
        space=pltpu.HBM,
        out_space=pltpu.VMEM,
    )
    both = lax.all_gather(sent, "ctx", axis_index_groups=SIDE_PAIRS)
    (pair_terms,) = call(
        combine_kernel, [packed], (side, kept, both, decay), scalars=1, flops=200_000, moved=1_100_000
    )
    slices = exchange_pieces(pair_terms, (3, 4))
    returned = ((PAIRS * ROWS, HEAD_DIM), F32)
    (states,) = call(scan_kernel, [returned], (side, slices), scalars=1, flops=200_000, moved=600_000)
    own = exchange_pieces(states, (ROWS, 1))
    own, w_late = lax.optimization_barrier((own, w_out))
    other = lax.ppermute(own, "ctx", SIDE_SWAP)
    (staged,) = call(
        stage_kernel,
        [((D // COLS, 512, COLS), BF16)],
        (w_late,),
        scratch=[pltpu.SemaphoreType.DMA((D // COLS,))],
        moved=12_600_000,
        space=pltpu.HBM,
        out_space=pltpu.VMEM,
    )
    other, staged = lax.optimization_barrier((other, staged))
    inner = ((EVENTS, 512), F32)
    total, factor = call(
        inner_kernel,
        [inner, inner],
        (side, queries, keys, values, state_retention_log, boundary, both, own),
        scalars=1,
        flops=100_000_000,
        moved=1_500_000,
    )
    block = ((EVENTS, COLS), F32)
    two_blocks = ((2, EVENTS, COLS), F32)
    normed, opposite_send, opposite_mine = call(
        first_kernel,
        [((EVENTS, 512), BF16), block, block],
        (place, queries, total, factor, other, gain, staged),
        scalars=1,
        flops=230_000_000,
        moved=4_000_000,
    )

    def core_sum(mine, both):
        return call(core_sum_kernel, [block], (place, mine, both), scalars=1)[0]

    opposite_both = lax.all_gather(opposite_send, "tp", axis_index_groups=CORE_PAIRS)
    opposite = core_sum(opposite_mine, opposite_both)
    opposite, normed = lax.optimization_barrier((opposite, normed))
    ahead_got = lax.ppermute(opposite, "tp", ONWARD)
    behind_send, behind_mine = call(
        behind_kernel, [block, block], (place, normed, staged), scalars=1, flops=200_000_000, moved=2_500_000
    )
    behind_both = lax.all_gather(behind_send, "tp", axis_index_groups=CORE_PAIRS)
    behind_both, normed = lax.optimization_barrier((behind_both, normed))
    behind = core_sum(behind_mine, behind_both)
    one = lax.ppermute(behind, "tp", BACK)
    ahead_send, ahead_mine, own_send, own_mine = call(
        rest_kernel, [block] * 4, (place, normed, staged), scalars=1, flops=400_000_000, moved=5_000_000
    )
    ahead_both = lax.all_gather(ahead_send, "tp", axis_index_groups=CORE_PAIRS)
    own_both = lax.all_gather(own_send, "tp", axis_index_groups=CORE_PAIRS)
    (passed,) = call(three_kernel, [block], (place, ahead_mine, ahead_both, ahead_got), scalars=1)
    two = lax.ppermute(passed, "tp", ONWARD)
    (own_and_one,) = call(three_kernel, [block], (place, own_mine, own_both, one), scalars=1, moved=1_600_000)
    (out,) = call(final_kernel, [((EVENTS, COLS), BF16)], (own_and_one, two), moved=1_000_000)
    return out


def solution(mesh):
    in_specs = (
        P("ctx", "tp"),
        P("ctx", "tp"),
        P("ctx", "tp"),
        P("tp", "ctx"),
        P("ctx"),
        P("tp"),
        P("tp", None),
    )
    out_specs = P("ctx", "tp")
    return jax.shard_map(body, mesh=mesh, in_specs=in_specs, out_specs=out_specs, check_vma=False)
```

```python
import math

import jax
import jax.numpy as jnp
from jax import lax
from jax.experimental import pallas as pl
from jax.experimental.pallas import tpu as pltpu
from jax.sharding import PartitionSpec as P

HEAD_DIM = 128
EVENTS = 128
HEADS_DEV = 4
D = 6144
COLS = 768
PAIRS = 48
PIECES = PAIRS // HEADS_DEV
ROWS = 11
CHUNK = ROWS + 1
HEAD_ROWS = PIECES * CHUNK
PACKED = PAIRS * CHUNK
STATE_ROWS = HEADS_DEV * HEAD_DIM
SENT_ROWS = STATE_ROWS + 8

surge_log_factor = math.log(0.6)
F32 = jnp.float32
BF16 = jnp.bfloat16
VMEM_LIMIT = 24 * 1024 * 1024

SLOTS = [4 * z + x for x in range(4) for z in range(PAIRS // 4)]
SIDE_GROUPS = [[2 * SLOTS.index(slot) + side for slot in range(PAIRS)] for side in range(2)]
SIDE_SWAP = [(i, i ^ 1) for i in range(2 * PAIRS)]
SIDE_PAIRS = [[i, i + 1] for i in range(0, 2 * PAIRS, 2)]
CORE_SWAP = [(i, i ^ 1) for i in range(8)]
CORE_PAIRS = [[i, i + 1] for i in range(0, 8, 2)]
ONWARD = [(i, (i + (2 if i % 2 == 0 else 6)) % 8) for i in range(8)]
BACK = [(i, (i + (6 if i % 2 == 0 else 2)) % 8) for i in range(8)]


def piece_rows(piece):
    return min(ROWS, HEAD_DIM - ROWS * piece)


def call(kernel, outs, args, scalars=0, scratch=(), flops=0, moved=0, space=pltpu.VMEM, out_space=None):
    specs = [pl.BlockSpec(memory_space=pltpu.SMEM)] * scalars
    specs += [pl.BlockSpec(memory_space=space)] * (len(args) - scalars)
    if space is pltpu.HBM:
        args = args[:scalars] + tuple(pltpu.with_memory_space_constraint(x, space) for x in args[scalars:])
    shapes = [(out_space or jax.ShapeDtypeStruct)(shape, dtype) for shape, dtype in outs]
    return pl.pallas_call(
        kernel,
        out_shape=shapes,
        in_specs=specs,
        out_specs=[pl.BlockSpec(memory_space=out_space or pltpu.VMEM)] * len(outs),
        scratch_shapes=list(scratch),
        compiler_params=pltpu.CompilerParams(vmem_limit_bytes=VMEM_LIMIT),
        cost_estimate=pl.CostEstimate(flops=flops, bytes_accessed=moved, transcendentals=0),
    )(*args)


def event_sums(log_ref, boundary_ref):
    rate = log_ref[...] + surge_log_factor * boundary_ref[...].astype(F32)
    row = lax.broadcasted_iota(jnp.int32, (EVENTS, EVENTS), 0)
    column = lax.broadcasted_iota(jnp.int32, (EVENTS, EVENTS), 1)
    lower = (column <= row).astype(F32)
    upper = (row <= column).astype(F32)
    columns = lax.dot_general(
        lower, rate, (((1,), (1,)), ((), ())), precision=lax.Precision.HIGHEST, preferred_element_type=F32
    )
    return rate, columns, upper


def factors(side, columns):
    ends = columns[EVENTS - 1 : EVENTS, :]
    toward_end = jnp.exp(ends - columns)
    from_start = jnp.exp(columns)
    sent = jnp.where(side == 0, toward_end, from_start)
    kept = jnp.where(side == 0, from_start, toward_end)
    return ends, sent, kept


def halves(wide):
    high = wide.astype(BF16)
    low = (wide - high.astype(F32)).astype(BF16)
    return high, low


def terms_kernel(
    side_ref,
    key_hbm,
    value_hbm,
    log_hbm,
    boundary_hbm,
    sent_ref,
    kept_ref,
    decay_ref,
    key_ref,
    value_ref,
    log_ref,
    boundary_ref,
    sems,
):
    copies = [
        pltpu.make_async_copy(log_hbm, log_ref, sems.at[0]),
        pltpu.make_async_copy(boundary_hbm, boundary_ref, sems.at[1]),
        pltpu.make_async_copy(key_hbm, key_ref, sems.at[2]),
        pltpu.make_async_copy(value_hbm, value_ref, sems.at[3]),
    ]
    for copy in copies:
        copy.start()
    for copy in copies[:2]:
        copy.wait()
    _, columns, _ = event_sums(log_ref, boundary_ref)
    ends, sent, kept = factors(side_ref[0], columns)
    decay = jnp.exp(ends)
    for copy in copies[2:]:
        copy.wait()
    sent_ref[STATE_ROWS:, :] = jnp.zeros((SENT_ROWS - STATE_ROWS, HEAD_DIM), F32)
    for head in range(HEADS_DEV):
        lanes = slice(head * HEAD_DIM, (head + 1) * HEAD_DIM)
        value = value_ref[:, lanes].astype(F32)
        sides = halves(value * sent[:, head : head + 1]) + halves(value * kept[:, head : head + 1])
        product = lax.dot_general(
            key_ref[:, lanes],
            jnp.concatenate(sides, axis=1),
            (((0,), (0,)), ((), ())),
            preferred_element_type=F32,
        )
        sent_ref[lanes, :] = product[:, :128] + product[:, 128:256]
        kept_ref[lanes, :] = product[:, 256:384] + product[:, 384:]
        whole_row = jnp.broadcast_to(decay[:, head : head + 1], (1, HEAD_DIM))
        decay_ref[head : head + 1, :] = whole_row
        sent_ref[STATE_ROWS + head : STATE_ROWS + head + 1, :] = whole_row


def combine_kernel(side_ref, kept_ref, both_ref, decay_ref, out_ref):
    other = 1 - side_ref[0]
    for head in range(HEADS_DEV):
        decay = decay_ref[head : head + 1, :]
        rows = slice(head * HEAD_DIM, (head + 1) * HEAD_DIM)
        state = kept_ref[rows, :] + decay * both_ref[other, rows, :]
        last = STATE_ROWS + head
        decay = decay * both_ref[other, last : last + 1, :]
        for piece in range(PIECES):
            count, first = piece_rows(piece), head * HEAD_ROWS + piece * CHUNK
            part = [state[ROWS * piece : ROWS * piece + count]]
            if count < ROWS:
                part.append(jnp.zeros((ROWS - count, HEAD_DIM), F32))
            out_ref[first : first + CHUNK, :] = jnp.concatenate(part + [decay], axis=0)


def scan_kernel(side_ref, term_ref, out_ref):
    def run(pairs):
        state = jnp.zeros((CHUNK, HEAD_DIM), F32)
        for pair in pairs:
            slot = SLOTS[pair]
            out_ref[slot * ROWS : (slot + 1) * ROWS, :] = state[:ROWS]
            term = term_ref[slot * CHUNK : (slot + 1) * CHUNK, :]
            state = term[ROWS:, :] * state + term

    @pl.when(side_ref[0] == 1)
    def _():
        run(range(PAIRS))

    @pl.when(side_ref[0] == 0)
    def _():
        run(range(PAIRS - 1, -1, -1))


def state_rows(head):
    return slice(head * PIECES * ROWS, head * PIECES * ROWS + HEAD_DIM)


def times_state(query, state):
    product = jnp.dot(query, jnp.concatenate(halves(state), axis=1), preferred_element_type=F32)
    return product[:, :128] + product[:, 128:]


def inner_kernel(
    side_ref, query_ref, key_ref, value_ref, log_ref, boundary_ref, both_ref, own_ref, total_ref, factor_ref
):
    rate, columns, upper = event_sums(log_ref, boundary_ref)
    rows_cum = lax.dot_general(
        rate, upper, (((1,), (0,)), ((), ())), precision=lax.Precision.HIGHEST, preferred_element_type=F32
    )
    side = side_ref[0]
    _, own, other = factors(side, columns)
    for head in range(HEADS_DEV):
        lanes = slice(head * HEAD_DIM, (head + 1) * HEAD_DIM)
        query = query_ref[:, lanes]
        logits = lax.dot_general(
            query, key_ref[:, lanes], (((1,), (1,)), ((), ())), preferred_element_type=F32
        )
        weight = jnp.exp(-jnp.abs(columns[:, head : head + 1] - rows_cum[head : head + 1, :]))
        probs = (logits * weight).astype(BF16)
        intra = jnp.dot(probs, value_ref[:, lanes], preferred_element_type=F32)
        last = STATE_ROWS + head
        got_decay = both_ref[1 - side, last : last + 1, :]
        state = both_ref[1 - side, lanes, :] + got_decay * own_ref[state_rows(head), :]
        total_ref[:, lanes] = intra + own[:, head : head + 1] * times_state(query, state)
        factor_ref[:, lanes] = jnp.broadcast_to(other[:, head : head + 1], (EVENTS, HEAD_DIM))


def stage_kernel(w_hbm, staged_ref, sems):
    copies = [
        pltpu.make_async_copy(w_hbm.at[:, pl.ds(block * COLS, COLS)], staged_ref.at[block], sems.at[block])
        for block in range(D // COLS)
    ]
    for copy in copies:
        copy.start()
    for copy in copies:
        copy.wait()


def block_of(place, far, core):
    return 2 * (((place >> 1) + far) & 3) + core


def first_kernel(
    place_ref,
    query_ref,
    total_ref,
    factor_ref,
    other_ref,
    gain_ref,
    w_ref,
    normed_ref,
    opposite_send_ref,
    opposite_ref,
):
    for head in range(HEADS_DEV):
        lanes = slice(head * HEAD_DIM, (head + 1) * HEAD_DIM)
        total = total_ref[:, lanes] + factor_ref[:, lanes] * times_state(
            query_ref[:, lanes], other_ref[state_rows(head), :]
        )
        average = jnp.mean(total * total, axis=1, keepdims=True)
        scaled = total * lax.rsqrt(average + 1e-06) * gain_ref[:, lanes]
        normed_ref[:, lanes] = scaled.astype(BF16)
    place = place_ref[0]
    core = place & 1
    normed = normed_ref[...]
    for out_ref, whose in ((opposite_send_ref, 1 - core), (opposite_ref, core)):
        out_ref[...] = jnp.dot(normed, w_ref[block_of(place, 2, whose)], preferred_element_type=F32)


def behind_kernel(place_ref, normed_ref, w_ref, send_ref, mine_ref):
    place = place_ref[0]
    core = place & 1
    normed = normed_ref[...]
    for out_ref, whose in ((send_ref, 1 - core), (mine_ref, core)):
        out_ref[...] = jnp.dot(normed, w_ref[block_of(place, 3 - 2 * whose, whose)], preferred_element_type=F32)


def rest_kernel(place_ref, normed_ref, w_ref, ahead_send_ref, ahead_ref, own_send_ref, own_ref):
    place = place_ref[0]
    core = place & 1
    normed = normed_ref[...]
    for out_ref, far, whose in (
        (ahead_send_ref, 3 - 2 * core, 1 - core),
        (ahead_ref, 1 + 2 * core, core),
        (own_send_ref, 0, 1 - core),
        (own_ref, 0, core),
    ):
        out_ref[...] = jnp.dot(normed, w_ref[block_of(place, far, whose)], preferred_element_type=F32)


def core_sum_kernel(place_ref, mine_ref, both_ref, out_ref):
    out_ref[...] = mine_ref[...] + both_ref[1 - (place_ref[0] & 1)]


def three_kernel(place_ref, mine_ref, both_ref, more_ref, out_ref):
    out_ref[...] = mine_ref[...] + both_ref[1 - (place_ref[0] & 1)] + more_ref[...]


def final_kernel(one_ref, two_ref, out_ref):
    out_ref[...] = (one_ref[...] + two_ref[...]).astype(BF16)


def exchange_pieces(packed, shape):
    pieces = packed.reshape((PAIRS,) + shape + (HEAD_DIM,))
    pieces = lax.all_to_all(pieces, "ctx", 0, 0, axis_index_groups=SIDE_GROUPS)
    return pieces.reshape(packed.shape)


def body(queries, keys, values, state_retention_log, boundary, gain, w_out):
    side = (lax.axis_index("ctx") & 1).reshape(1)
    place = lax.axis_index("tp").reshape(1)
    boundary = boundary.reshape(1, EVENTS)
    gain = gain.reshape(1, 512)
    packed = ((PACKED, HEAD_DIM), F32)
    state = ((STATE_ROWS, HEAD_DIM), F32)

    sent, kept, decay = call(
        terms_kernel,
        [((SENT_ROWS, HEAD_DIM), F32), state, ((HEADS_DEV, HEAD_DIM), F32)],
        (side, keys, values, state_retention_log, boundary),
        scalars=1,
        scratch=[
            pltpu.VMEM((EVENTS, 512), BF16),
            pltpu.VMEM((EVENTS, 512), BF16),
            pltpu.VMEM((HEADS_DEV, EVENTS), F32),
            pltpu.VMEM((1, EVENTS), jnp.int32),
            pltpu.SemaphoreType.DMA((4,)),
        ],
        flops=70_000_000,
        moved=900_000,
        space=pltpu.HBM,
        out_space=pltpu.VMEM,
    )
    both = lax.all_gather(sent, "ctx", axis_index_groups=SIDE_PAIRS)
    (pair_terms,) = call(
        combine_kernel, [packed], (side, kept, both, decay), scalars=1, flops=200_000, moved=1_100_000
    )
    slices = exchange_pieces(pair_terms, (3, 4))
    returned = ((PAIRS * ROWS, HEAD_DIM), F32)
    (states,) = call(scan_kernel, [returned], (side, slices), scalars=1, flops=200_000, moved=600_000)
    own = exchange_pieces(states, (ROWS, 1))
    own, w_late = lax.optimization_barrier((own, w_out))
    other = lax.ppermute(own, "ctx", SIDE_SWAP)
    (staged,) = call(
        stage_kernel,
        [((D // COLS, 512, COLS), BF16)],
        (w_late,),
        scratch=[pltpu.SemaphoreType.DMA((D // COLS,))],
        moved=12_600_000,
        space=pltpu.HBM,
        out_space=pltpu.VMEM,
    )
    other, staged = lax.optimization_barrier((other, staged))
    inner = ((EVENTS, 512), F32)
    total, factor = call(
        inner_kernel,
        [inner, inner],
        (side, queries, keys, values, state_retention_log, boundary, both, own),
        scalars=1,
        flops=100_000_000,
        moved=1_500_000,
    )
    block = ((EVENTS, COLS), F32)
    two_blocks = ((2, EVENTS, COLS), F32)
    normed, opposite_send, opposite_mine = call(
        first_kernel,
        [((EVENTS, 512), BF16), block, block],
        (place, queries, total, factor, other, gain, staged),
        scalars=1,
        flops=230_000_000,
        moved=4_000_000,
    )

    def core_sum(mine, both):
        return call(core_sum_kernel, [block], (place, mine, both), scalars=1)[0]

    opposite_both = lax.all_gather(opposite_send, "tp", axis_index_groups=CORE_PAIRS)
    opposite = core_sum(opposite_mine, opposite_both)
    opposite, normed = lax.optimization_barrier((opposite, normed))
    ahead_got = lax.ppermute(opposite, "tp", ONWARD)
    behind_send, behind_mine = call(
        behind_kernel, [block, block], (place, normed, staged), scalars=1, flops=200_000_000, moved=2_500_000
    )
    behind_both = lax.all_gather(behind_send, "tp", axis_index_groups=CORE_PAIRS)
    behind_both, normed = lax.optimization_barrier((behind_both, normed))
    behind = core_sum(behind_mine, behind_both)
    one = lax.ppermute(behind, "tp", BACK)
    ahead_send, ahead_mine, own_send, own_mine = call(
        rest_kernel, [block] * 4, (place, normed, staged), scalars=1, flops=400_000_000, moved=5_000_000
    )
    ahead_both = lax.all_gather(ahead_send, "tp", axis_index_groups=CORE_PAIRS)
    own_both = lax.all_gather(own_send, "tp", axis_index_groups=CORE_PAIRS)
    (passed,) = call(three_kernel, [block], (place, ahead_mine, ahead_both, ahead_got), scalars=1)
    two = lax.ppermute(passed, "tp", ONWARD)
    (own_and_one,) = call(three_kernel, [block], (place, own_mine, own_both, one), scalars=1, moved=1_600_000)
    (out,) = call(final_kernel, [((EVENTS, COLS), BF16)], (own_and_one, two), moved=1_000_000)
    return out


def solution(mesh):
    in_specs = (
        P("ctx", "tp"),
        P("ctx", "tp"),
        P("ctx", "tp"),
        P("tp", "ctx"),
        P("ctx"),
        P("tp"),
        P("tp", None),
    )
    out_specs = P("ctx", "tp")
    return jax.shard_map(body, mesh=mesh, in_specs=in_specs, out_specs=out_specs, check_vma=False)
```

```python
import math

import jax
import jax.numpy as jnp
from jax import lax
from jax.experimental import pallas as pl
from jax.experimental.pallas import tpu as pltpu
from jax.sharding import PartitionSpec as P

HEAD_DIM = 128
EVENTS = 128
HEADS_DEV = 4
D = 6144
COLS = 768
PAIRS = 48
PIECES = PAIRS // HEADS_DEV
ROWS = 11
CHUNK = ROWS + 1
HEAD_ROWS = PIECES * CHUNK
PACKED = PAIRS * CHUNK
STATE_ROWS = HEADS_DEV * HEAD_DIM
SENT_ROWS = STATE_ROWS + 8

surge_log_factor = math.log(0.6)
F32 = jnp.float32
BF16 = jnp.bfloat16
VMEM_LIMIT = 24 * 1024 * 1024

SLOTS = [4 * z + x for x in range(4) for z in range(PAIRS // 4)]
SIDE_GROUPS = [[2 * SLOTS.index(slot) + side for slot in range(PAIRS)] for side in range(2)]
SIDE_SWAP = [(i, i ^ 1) for i in range(2 * PAIRS)]
SIDE_PAIRS = [[i, i + 1] for i in range(0, 2 * PAIRS, 2)]
CORE_SWAP = [(i, i ^ 1) for i in range(8)]
CORE_PAIRS = [[i, i + 1] for i in range(0, 8, 2)]
ONWARD = [(i, (i + (2 if i % 2 == 0 else 6)) % 8) for i in range(8)]
BACK = [(i, (i + (6 if i % 2 == 0 else 2)) % 8) for i in range(8)]


def piece_rows(piece):
    return min(ROWS, HEAD_DIM - ROWS * piece)


def call(kernel, outs, args, scalars=0, scratch=(), flops=0, moved=0, space=pltpu.VMEM, out_space=None):
    specs = [pl.BlockSpec(memory_space=pltpu.SMEM)] * scalars
    specs += [pl.BlockSpec(memory_space=space)] * (len(args) - scalars)
    if space is pltpu.HBM:
        args = args[:scalars] + tuple(pltpu.with_memory_space_constraint(x, space) for x in args[scalars:])
    shapes = [(out_space or jax.ShapeDtypeStruct)(shape, dtype) for shape, dtype in outs]
    return pl.pallas_call(
        kernel,
        out_shape=shapes,
        in_specs=specs,
        out_specs=[pl.BlockSpec(memory_space=out_space or pltpu.VMEM)] * len(outs),
        scratch_shapes=list(scratch),
        compiler_params=pltpu.CompilerParams(vmem_limit_bytes=VMEM_LIMIT),
        cost_estimate=pl.CostEstimate(flops=flops, bytes_accessed=moved, transcendentals=0),
    )(*args)


def event_sums(log_ref, boundary_ref):
    rate = log_ref[...] + surge_log_factor * boundary_ref[...].astype(F32)
    row = lax.broadcasted_iota(jnp.int32, (EVENTS, EVENTS), 0)
    column = lax.broadcasted_iota(jnp.int32, (EVENTS, EVENTS), 1)
    lower = (column <= row).astype(F32)
    upper = (row <= column).astype(F32)
    columns = lax.dot_general(
        lower, rate, (((1,), (1,)), ((), ())), precision=lax.Precision.HIGHEST, preferred_element_type=F32
    )
    return rate, columns, upper


def factors(side, columns):
    ends = columns[EVENTS - 1 : EVENTS, :]
    toward_end = jnp.exp(ends - columns)
    from_start = jnp.exp(columns)
    sent = jnp.where(side == 0, toward_end, from_start)
    kept = jnp.where(side == 0, from_start, toward_end)
    return ends, sent, kept


def halves(wide):
    high = wide.astype(BF16)
    low = (wide - high.astype(F32)).astype(BF16)
    return high, low


def terms_kernel(
    side_ref,
    key_hbm,
    value_hbm,
    log_hbm,
    boundary_hbm,
    sent_ref,
    kept_ref,
    decay_ref,
    key_ref,
    value_ref,
    log_ref,
    boundary_ref,
    sems,
):
    copies = [
        pltpu.make_async_copy(log_hbm, log_ref, sems.at[0]),
        pltpu.make_async_copy(boundary_hbm, boundary_ref, sems.at[1]),
        pltpu.make_async_copy(key_hbm, key_ref, sems.at[2]),
        pltpu.make_async_copy(value_hbm, value_ref, sems.at[3]),
    ]
    for copy in copies:
        copy.start()
    for copy in copies[:2]:
        copy.wait()
    _, columns, _ = event_sums(log_ref, boundary_ref)
    ends, sent, kept = factors(side_ref[0], columns)
    decay = jnp.exp(ends)
    for copy in copies[2:]:
        copy.wait()
    sent_ref[STATE_ROWS:, :] = jnp.zeros((SENT_ROWS - STATE_ROWS, HEAD_DIM), F32)
    for head in range(HEADS_DEV):
        lanes = slice(head * HEAD_DIM, (head + 1) * HEAD_DIM)
        value = value_ref[:, lanes].astype(F32)
        sides = halves(value * sent[:, head : head + 1]) + halves(value * kept[:, head : head + 1])
        product = lax.dot_general(
            key_ref[:, lanes],
            jnp.concatenate(sides, axis=1),
            (((0,), (0,)), ((), ())),
            preferred_element_type=F32,
        )
        sent_ref[lanes, :] = product[:, :128] + product[:, 128:256]
        kept_ref[lanes, :] = product[:, 256:384] + product[:, 384:]
        whole_row = jnp.broadcast_to(decay[:, head : head + 1], (1, HEAD_DIM))
        decay_ref[head : head + 1, :] = whole_row
        sent_ref[STATE_ROWS + head : STATE_ROWS + head + 1, :] = whole_row


def combine_kernel(side_ref, kept_ref, both_ref, decay_ref, out_ref):
    other = 1 - side_ref[0]
    for head in range(HEADS_DEV):
        decay = decay_ref[head : head + 1, :]
        rows = slice(head * HEAD_DIM, (head + 1) * HEAD_DIM)
        state = kept_ref[rows, :] + decay * both_ref[other, rows, :]
        last = STATE_ROWS + head
        decay = decay * both_ref[other, last : last + 1, :]
        for piece in range(PIECES):
            count, first = piece_rows(piece), head * HEAD_ROWS + piece * CHUNK
            part = [state[ROWS * piece : ROWS * piece + count]]
            if count < ROWS:
                part.append(jnp.zeros((ROWS - count, HEAD_DIM), F32))
            out_ref[first : first + CHUNK, :] = jnp.concatenate(part + [decay], axis=0)


def scan_kernel(side_ref, term_ref, out_ref):
    def run(pairs):
        state = jnp.zeros((CHUNK, HEAD_DIM), F32)
        for pair in pairs:
            slot = SLOTS[pair]
            out_ref[slot * ROWS : (slot + 1) * ROWS, :] = state[:ROWS]
            term = term_ref[slot * CHUNK : (slot + 1) * CHUNK, :]
            state = term[ROWS:, :] * state + term

    @pl.when(side_ref[0] == 1)
    def _():
        run(range(PAIRS))

    @pl.when(side_ref[0] == 0)
    def _():
        run(range(PAIRS - 1, -1, -1))


def state_rows(head):
    return slice(head * PIECES * ROWS, head * PIECES * ROWS + HEAD_DIM)


def times_state(query, state):
    product = jnp.dot(query, jnp.concatenate(halves(state), axis=1), preferred_element_type=F32)
    return product[:, :128] + product[:, 128:]


def inner_kernel(
    side_ref, query_ref, key_ref, value_ref, log_ref, boundary_ref, both_ref, own_ref, total_ref, factor_ref
):
    rate, columns, upper = event_sums(log_ref, boundary_ref)
    rows_cum = lax.dot_general(
        rate, upper, (((1,), (0,)), ((), ())), precision=lax.Precision.HIGHEST, preferred_element_type=F32
    )
    side = side_ref[0]
    _, own, other = factors(side, columns)
    for head in range(HEADS_DEV):
        lanes = slice(head * HEAD_DIM, (head + 1) * HEAD_DIM)
        query = query_ref[:, lanes]
        logits = lax.dot_general(
            query, key_ref[:, lanes], (((1,), (1,)), ((), ())), preferred_element_type=F32
        )
        weight = jnp.exp(-jnp.abs(columns[:, head : head + 1] - rows_cum[head : head + 1, :]))
        probs = (logits * weight).astype(BF16)
        intra = jnp.dot(probs, value_ref[:, lanes], preferred_element_type=F32)
        last = STATE_ROWS + head
        got_decay = both_ref[1 - side, last : last + 1, :]
        state = both_ref[1 - side, lanes, :] + got_decay * own_ref[state_rows(head), :]
        total_ref[:, lanes] = intra + own[:, head : head + 1] * times_state(query, state)
        factor_ref[:, lanes] = jnp.broadcast_to(other[:, head : head + 1], (EVENTS, HEAD_DIM))


def stage_kernel(w_hbm, staged_ref, sems):
    copies = [
        pltpu.make_async_copy(w_hbm.at[:, pl.ds(block * COLS, COLS)], staged_ref.at[block], sems.at[block])
        for block in range(D // COLS)
    ]
    for copy in copies:
        copy.start()
    for copy in copies:
        copy.wait()


def block_of(place, far, core):
    return 2 * (((place >> 1) + far) & 3) + core


def first_kernel(
    place_ref,
    query_ref,
    total_ref,
    factor_ref,
    other_ref,
    gain_ref,
    w_ref,
    normed_ref,
    opposite_send_ref,
    opposite_ref,
):
    for head in range(HEADS_DEV):
        lanes = slice(head * HEAD_DIM, (head + 1) * HEAD_DIM)
        total = total_ref[:, lanes] + factor_ref[:, lanes] * times_state(
            query_ref[:, lanes], other_ref[state_rows(head), :]
        )
        average = jnp.mean(total * total, axis=1, keepdims=True)
        scaled = total * lax.rsqrt(average + 1e-06) * gain_ref[:, lanes]
        normed_ref[:, lanes] = scaled.astype(BF16)
    place = place_ref[0]
    core = place & 1
    normed = normed_ref[...]
    for out_ref, whose in ((opposite_send_ref, 1 - core), (opposite_ref, core)):
        out_ref[...] = jnp.dot(normed, w_ref[block_of(place, 2, whose)], preferred_element_type=F32)


def behind_kernel(place_ref, normed_ref, w_ref, send_ref, mine_ref):
    place = place_ref[0]
    core = place & 1
    normed = normed_ref[...]
    for out_ref, whose in ((send_ref, 1 - core), (mine_ref, core)):
        out_ref[...] = jnp.dot(normed, w_ref[block_of(place, 3 - 2 * whose, whose)], preferred_element_type=F32)


def rest_kernel(place_ref, normed_ref, w_ref, ahead_send_ref, ahead_ref, own_send_ref, own_ref):
    place = place_ref[0]
    core = place & 1
    normed = normed_ref[...]
    for out_ref, far, whose in (
        (ahead_send_ref, 3 - 2 * core, 1 - core),
        (ahead_ref, 1 + 2 * core, core),
        (own_send_ref, 0, 1 - core),
        (own_ref, 0, core),
    ):
        out_ref[...] = jnp.dot(normed, w_ref[block_of(place, far, whose)], preferred_element_type=F32)


def core_sum_kernel(place_ref, mine_ref, both_ref, out_ref):
    out_ref[...] = mine_ref[...] + both_ref[1 - (place_ref[0] & 1)]


def three_kernel(place_ref, mine_ref, both_ref, more_ref, out_ref):
    out_ref[...] = mine_ref[...] + both_ref[1 - (place_ref[0] & 1)] + more_ref[...]


def final_kernel(one_ref, two_ref, out_ref):
    out_ref[...] = (one_ref[...] + two_ref[...]).astype(BF16)


def exchange_pieces(packed, shape):
    pieces = packed.reshape((PAIRS,) + shape + (HEAD_DIM,))
    pieces = lax.all_to_all(pieces, "ctx", 0, 0, axis_index_groups=SIDE_GROUPS)
    return pieces.reshape(packed.shape)


def body(queries, keys, values, state_retention_log, boundary, gain, w_out):
    side = (lax.axis_index("ctx") & 1).reshape(1)
    place = lax.axis_index("tp").reshape(1)
    boundary = boundary.reshape(1, EVENTS)
    gain = gain.reshape(1, 512)
    packed = ((PACKED, HEAD_DIM), F32)
    state = ((STATE_ROWS, HEAD_DIM), F32)

    sent, kept, decay = call(
        terms_kernel,
        [((SENT_ROWS, HEAD_DIM), F32), state, ((HEADS_DEV, HEAD_DIM), F32)],
        (side, keys, values, state_retention_log, boundary),
        scalars=1,
        scratch=[
            pltpu.VMEM((EVENTS, 512), BF16),
            pltpu.VMEM((EVENTS, 512), BF16),
            pltpu.VMEM((HEADS_DEV, EVENTS), F32),
            pltpu.VMEM((1, EVENTS), jnp.int32),
            pltpu.SemaphoreType.DMA((4,)),
        ],
        flops=70_000_000,
        moved=900_000,
        space=pltpu.HBM,
        out_space=pltpu.VMEM,
    )
    both = lax.all_gather(sent, "ctx", axis_index_groups=SIDE_PAIRS)
    (pair_terms,) = call(
        combine_kernel, [packed], (side, kept, both, decay), scalars=1, flops=200_000, moved=1_100_000
    )
    slices = exchange_pieces(pair_terms, (CHUNK, 1))
    returned = ((PAIRS * ROWS, HEAD_DIM), F32)
    (states,) = call(scan_kernel, [returned], (side, slices), scalars=1, flops=200_000, moved=600_000)
    own = exchange_pieces(states, (ROWS, 1))
    own, w_late = lax.optimization_barrier((own, w_out))
    other = lax.ppermute(own, "ctx", SIDE_SWAP)
    (staged,) = call(
        stage_kernel,
        [((D // COLS, 512, COLS), BF16)],
        (w_late,),
        scratch=[pltpu.SemaphoreType.DMA((D // COLS,))],
        moved=12_600_000,
        space=pltpu.HBM,
        out_space=pltpu.VMEM,
    )
    other, staged = lax.optimization_barrier((other, staged))
    inner = ((EVENTS, 512), F32)
    total, factor = call(
        inner_kernel,
        [inner, inner],
        (side, queries, keys, values, state_retention_log, boundary, both, own),
        scalars=1,
        flops=100_000_000,
        moved=1_500_000,
    )
    block = ((EVENTS, COLS), F32)
    two_blocks = ((2, EVENTS, COLS), F32)
    normed, opposite_send, opposite_mine = call(
        first_kernel,
        [((EVENTS, 512), BF16), block, block],
        (place, queries, total, factor, other, gain, staged),
        scalars=1,
        flops=230_000_000,
        moved=4_000_000,
    )

    def core_sum(mine, both):
        return call(core_sum_kernel, [block], (place, mine, both), scalars=1)[0]

    opposite_both = lax.all_gather(opposite_send, "tp", axis_index_groups=CORE_PAIRS)
    opposite = core_sum(opposite_mine, opposite_both)
    opposite, normed = lax.optimization_barrier((opposite, normed))
    ahead_got = lax.ppermute(opposite, "tp", ONWARD)
    behind_send, behind_mine = call(
        behind_kernel, [block, block], (place, normed, staged), scalars=1, flops=200_000_000, moved=2_500_000
    )
    behind_both = lax.all_gather(behind_send, "tp", axis_index_groups=CORE_PAIRS)
    behind_both, normed = lax.optimization_barrier((behind_both, normed))
    behind = core_sum(behind_mine, behind_both)
    one = lax.ppermute(behind, "tp", BACK)
    ahead_send, ahead_mine, own_send, own_mine = call(
        rest_kernel, [block] * 4, (place, normed, staged), scalars=1, flops=400_000_000, moved=5_000_000
    )
    ahead_both = lax.all_gather(ahead_send, "tp", axis_index_groups=CORE_PAIRS)
    own_both = lax.all_gather(own_send, "tp", axis_index_groups=CORE_PAIRS)
    (passed,) = call(three_kernel, [block], (place, ahead_mine, ahead_both, ahead_got), scalars=1)
    two = lax.ppermute(passed, "tp", ONWARD)
    (own_and_one,) = call(three_kernel, [block], (place, own_mine, own_both, one), scalars=1, moved=1_600_000)
    (out,) = call(final_kernel, [((EVENTS, COLS), BF16)], (own_and_one, two), moved=1_000_000)
    return out


def solution(mesh):
    in_specs = (
        P("ctx", "tp"),
        P("ctx", "tp"),
        P("ctx", "tp"),
        P("tp", "ctx"),
        P("ctx"),
        P("tp"),
        P("tp", None),
    )
    out_specs = P("ctx", "tp")
    return jax.shard_map(body, mesh=mesh, in_specs=in_specs, out_specs=out_specs, check_vma=False)
```

```python
import math

import jax
import jax.numpy as jnp
from jax import lax
from jax.experimental import pallas as pl
from jax.experimental.pallas import tpu as pltpu
from jax.sharding import PartitionSpec as P

HEAD_DIM = 128
EVENTS = 128
HEADS_DEV = 4
D = 6144
COLS = 768
PAIRS = 48
PIECES = PAIRS // HEADS_DEV
ROWS = 11
CHUNK = ROWS + 1
HEAD_ROWS = PIECES * CHUNK
PACKED = PAIRS * CHUNK
STATE_ROWS = HEADS_DEV * HEAD_DIM
SENT_ROWS = STATE_ROWS + 8

surge_log_factor = math.log(0.6)
F32 = jnp.float32
BF16 = jnp.bfloat16
VMEM_LIMIT = 24 * 1024 * 1024

SLOTS = [4 * z + x for x in range(4) for z in range(PAIRS // 4)]
SIDE_GROUPS = [[2 * SLOTS.index(slot) + side for slot in range(PAIRS)] for side in range(2)]
SIDE_SWAP = [(i, i ^ 1) for i in range(2 * PAIRS)]
SIDE_PAIRS = [[i, i + 1] for i in range(0, 2 * PAIRS, 2)]
CORE_SWAP = [(i, i ^ 1) for i in range(8)]
CORE_PAIRS = [[i, i + 1] for i in range(0, 8, 2)]
ONWARD = [(i, (i + (2 if i % 2 == 0 else 6)) % 8) for i in range(8)]
BACK = [(i, (i + (6 if i % 2 == 0 else 2)) % 8) for i in range(8)]


def piece_rows(piece):
    return min(ROWS, HEAD_DIM - ROWS * piece)


def call(kernel, outs, args, scalars=0, scratch=(), flops=0, moved=0, space=pltpu.VMEM, out_space=None):
    specs = [pl.BlockSpec(memory_space=pltpu.SMEM)] * scalars
    specs += [pl.BlockSpec(memory_space=space)] * (len(args) - scalars)
    if space is pltpu.HBM:
        args = args[:scalars] + tuple(pltpu.with_memory_space_constraint(x, space) for x in args[scalars:])
    shapes = [(out_space or jax.ShapeDtypeStruct)(shape, dtype) for shape, dtype in outs]
    return pl.pallas_call(
        kernel,
        out_shape=shapes,
        in_specs=specs,
        out_specs=[pl.BlockSpec(memory_space=out_space or pltpu.VMEM)] * len(outs),
        scratch_shapes=list(scratch),
        compiler_params=pltpu.CompilerParams(vmem_limit_bytes=VMEM_LIMIT),
        cost_estimate=pl.CostEstimate(flops=flops, bytes_accessed=moved, transcendentals=0),
    )(*args)


def event_sums(log_ref, boundary_ref):
    rate = log_ref[...] + surge_log_factor * boundary_ref[...].astype(F32)
    row = lax.broadcasted_iota(jnp.int32, (EVENTS, EVENTS), 0)
    column = lax.broadcasted_iota(jnp.int32, (EVENTS, EVENTS), 1)
    lower = (column <= row).astype(F32)
    upper = (row <= column).astype(F32)
    columns = lax.dot_general(
        lower, rate, (((1,), (1,)), ((), ())), precision=lax.Precision.HIGHEST, preferred_element_type=F32
    )
    return rate, columns, upper


def factors(side, columns):
    ends = columns[EVENTS - 1 : EVENTS, :]
    toward_end = jnp.exp(ends - columns)
    from_start = jnp.exp(columns)
    sent = jnp.where(side == 0, toward_end, from_start)
    kept = jnp.where(side == 0, from_start, toward_end)
    return ends, sent, kept


def halves(wide):
    high = wide.astype(BF16)
    low = (wide - high.astype(F32)).astype(BF16)
    return high, low


def terms_kernel(
    side_ref,
    key_hbm,
    value_hbm,
    log_hbm,
    boundary_hbm,
    sent_ref,
    kept_ref,
    decay_ref,
    key_ref,
    value_ref,
    log_ref,
    boundary_ref,
    sems,
):
    copies = [
        pltpu.make_async_copy(log_hbm, log_ref, sems.at[0]),
        pltpu.make_async_copy(boundary_hbm, boundary_ref, sems.at[1]),
        pltpu.make_async_copy(key_hbm, key_ref, sems.at[2]),
        pltpu.make_async_copy(value_hbm, value_ref, sems.at[3]),
    ]
    for copy in copies:
        copy.start()
    for copy in copies[:2]:
        copy.wait()
    _, columns, _ = event_sums(log_ref, boundary_ref)
    ends, sent, kept = factors(side_ref[0], columns)
    decay = jnp.exp(ends)
    for copy in copies[2:]:
        copy.wait()
    sent_ref[STATE_ROWS:, :] = jnp.zeros((SENT_ROWS - STATE_ROWS, HEAD_DIM), F32)
    for head in range(HEADS_DEV):
        lanes = slice(head * HEAD_DIM, (head + 1) * HEAD_DIM)
        value = value_ref[:, lanes].astype(F32)
        sides = halves(value * sent[:, head : head + 1]) + halves(value * kept[:, head : head + 1])
        product = lax.dot_general(
            key_ref[:, lanes],
            jnp.concatenate(sides, axis=1),
            (((0,), (0,)), ((), ())),
            preferred_element_type=F32,
        )
        sent_ref[lanes, :] = product[:, :128] + product[:, 128:256]
        kept_ref[lanes, :] = product[:, 256:384] + product[:, 384:]
        whole_row = jnp.broadcast_to(decay[:, head : head + 1], (1, HEAD_DIM))
        decay_ref[head : head + 1, :] = whole_row
        sent_ref[STATE_ROWS + head : STATE_ROWS + head + 1, :] = whole_row


def combine_kernel(side_ref, kept_ref, both_ref, decay_ref, out_ref):
    other = 1 - side_ref[0]
    for head in range(HEADS_DEV):
        decay = decay_ref[head : head + 1, :]
        rows = slice(head * HEAD_DIM, (head + 1) * HEAD_DIM)
        state = kept_ref[rows, :] + decay * both_ref[other, rows, :]
        last = STATE_ROWS + head
        decay = decay * both_ref[other, last : last + 1, :]
        for piece in range(PIECES):
            count, first = piece_rows(piece), head * HEAD_ROWS + piece * CHUNK
            part = [state[ROWS * piece : ROWS * piece + count]]
            if count < ROWS:
                part.append(jnp.zeros((ROWS - count, HEAD_DIM), F32))
            out_ref[first : first + CHUNK, :] = jnp.concatenate(part + [decay], axis=0)


def scan_kernel(side_ref, term_ref, out_ref):
    def run(pairs):
        state = jnp.zeros((CHUNK, HEAD_DIM), F32)
        for pair in pairs:
            slot = SLOTS[pair]
            out_ref[slot * ROWS : (slot + 1) * ROWS, :] = state[:ROWS]
            term = term_ref[slot * CHUNK : (slot + 1) * CHUNK, :]
            state = term[ROWS:, :] * state + term

    @pl.when(side_ref[0] == 1)
    def _():
        run(range(PAIRS))

    @pl.when(side_ref[0] == 0)
    def _():
        run(range(PAIRS - 1, -1, -1))


def state_rows(head):
    return slice(head * PIECES * ROWS, head * PIECES * ROWS + HEAD_DIM)


def times_state(query, state):
    product = jnp.dot(query, jnp.concatenate(halves(state), axis=1), preferred_element_type=F32)
    return product[:, :128] + product[:, 128:]


def inner_kernel(
    side_ref, query_ref, key_ref, value_ref, log_ref, boundary_ref, both_ref, own_ref, total_ref, factor_ref
):
    rate, columns, upper = event_sums(log_ref, boundary_ref)
    rows_cum = lax.dot_general(
        rate, upper, (((1,), (0,)), ((), ())), precision=lax.Precision.HIGHEST, preferred_element_type=F32
    )
    side = side_ref[0]
    _, own, other = factors(side, columns)
    for head in range(HEADS_DEV):
        lanes = slice(head * HEAD_DIM, (head + 1) * HEAD_DIM)
        query = query_ref[:, lanes]
        logits = lax.dot_general(
            query, key_ref[:, lanes], (((1,), (1,)), ((), ())), preferred_element_type=F32
        )
        weight = jnp.exp(-jnp.abs(columns[:, head : head + 1] - rows_cum[head : head + 1, :]))
        probs = (logits * weight).astype(BF16)
        intra = jnp.dot(probs, value_ref[:, lanes], preferred_element_type=F32)
        last = STATE_ROWS + head
        got_decay = both_ref[1 - side, last : last + 1, :]
        state = both_ref[1 - side, lanes, :] + got_decay * own_ref[state_rows(head), :]
        total_ref[:, lanes] = intra + own[:, head : head + 1] * times_state(query, state)
        factor_ref[:, lanes] = jnp.broadcast_to(other[:, head : head + 1], (EVENTS, HEAD_DIM))


def stage_kernel(w_hbm, staged_ref, sems):
    copies = [
        pltpu.make_async_copy(w_hbm.at[:, pl.ds(block * COLS, COLS)], staged_ref.at[block], sems.at[block])
        for block in range(D // COLS)
    ]
    for copy in copies:
        copy.start()
    for copy in copies:
        copy.wait()


def block_of(place, far, core):
    return 2 * (((place >> 1) + far) & 3) + core


def first_kernel(
    place_ref,
    query_ref,
    total_ref,
    factor_ref,
    other_ref,
    gain_ref,
    w_ref,
    normed_ref,
    opposite_send_ref,
    opposite_ref,
):
    for head in range(HEADS_DEV):
        lanes = slice(head * HEAD_DIM, (head + 1) * HEAD_DIM)
        total = total_ref[:, lanes] + factor_ref[:, lanes] * times_state(
            query_ref[:, lanes], other_ref[state_rows(head), :]
        )
        average = jnp.mean(total * total, axis=1, keepdims=True)
        scaled = total * lax.rsqrt(average + 1e-06) * gain_ref[:, lanes]
        normed_ref[:, lanes] = scaled.astype(BF16)
    place = place_ref[0]
    core = place & 1
    normed = normed_ref[...]
    for out_ref, whose in ((opposite_send_ref, 1 - core), (opposite_ref, core)):
        out_ref[...] = jnp.dot(normed, w_ref[block_of(place, 2, whose)], preferred_element_type=F32)


def behind_kernel(place_ref, normed_ref, w_ref, send_ref, mine_ref):
    place = place_ref[0]
    core = place & 1
    normed = normed_ref[...]
    for out_ref, whose in ((send_ref, 1 - core), (mine_ref, core)):
        out_ref[...] = jnp.dot(normed, w_ref[block_of(place, 3 - 2 * whose, whose)], preferred_element_type=F32)


def rest_kernel(place_ref, normed_ref, w_ref, send_ref, mine_ref):
    place = place_ref[0]
    core = place & 1
    normed = normed_ref[...]
    for out_ref, whose in ((send_ref, 1 - core), (mine_ref, core)):
        for slot, far in enumerate((1 + 2 * whose, 0)):
            out_ref[slot] = jnp.dot(normed, w_ref[block_of(place, far, whose)], preferred_element_type=F32)


def core_sum_kernel(place_ref, mine_ref, both_ref, out_ref):
    out_ref[...] = mine_ref[...] + both_ref[1 - (place_ref[0] & 1)]


def ahead_kernel(mine_ref, got_ref, more_ref, out_ref):
    out_ref[...] = mine_ref[0] + got_ref[0] + more_ref[...]


def own_kernel(mine_ref, got_ref, more_ref, out_ref):
    out_ref[...] = mine_ref[1] + got_ref[1] + more_ref[...]


def final_kernel(one_ref, two_ref, out_ref):
    out_ref[...] = (one_ref[...] + two_ref[...]).astype(BF16)


def exchange_pieces(packed, shape):
    pieces = packed.reshape((PAIRS,) + shape + (HEAD_DIM,))
    pieces = lax.all_to_all(pieces, "ctx", 0, 0, axis_index_groups=SIDE_GROUPS)
    return pieces.reshape(packed.shape)


def body(queries, keys, values, state_retention_log, boundary, gain, w_out):
    side = (lax.axis_index("ctx") & 1).reshape(1)
    place = lax.axis_index("tp").reshape(1)
    boundary = boundary.reshape(1, EVENTS)
    gain = gain.reshape(1, 512)
    packed = ((PACKED, HEAD_DIM), F32)
    state = ((STATE_ROWS, HEAD_DIM), F32)

    sent, kept, decay = call(
        terms_kernel,
        [((SENT_ROWS, HEAD_DIM), F32), state, ((HEADS_DEV, HEAD_DIM), F32)],
        (side, keys, values, state_retention_log, boundary),
        scalars=1,
        scratch=[
            pltpu.VMEM((EVENTS, 512), BF16),
            pltpu.VMEM((EVENTS, 512), BF16),
            pltpu.VMEM((HEADS_DEV, EVENTS), F32),
            pltpu.VMEM((1, EVENTS), jnp.int32),
            pltpu.SemaphoreType.DMA((4,)),
        ],
        flops=70_000_000,
        moved=900_000,
        space=pltpu.HBM,
        out_space=pltpu.VMEM,
    )
    both = lax.all_gather(sent, "ctx", axis_index_groups=SIDE_PAIRS)
    (pair_terms,) = call(
        combine_kernel, [packed], (side, kept, both, decay), scalars=1, flops=200_000, moved=1_100_000
    )
    slices = exchange_pieces(pair_terms, (3, 4))
    returned = ((PAIRS * ROWS, HEAD_DIM), F32)
    (states,) = call(scan_kernel, [returned], (side, slices), scalars=1, flops=200_000, moved=600_000)
    own = exchange_pieces(states, (ROWS, 1))
    own, w_late = lax.optimization_barrier((own, w_out))
    other = lax.ppermute(own, "ctx", SIDE_SWAP)
    (staged,) = call(
        stage_kernel,
        [((D // COLS, 512, COLS), BF16)],
        (w_late,),
        scratch=[pltpu.SemaphoreType.DMA((D // COLS,))],
        moved=12_600_000,
        space=pltpu.HBM,
        out_space=pltpu.VMEM,
    )
    other, staged = lax.optimization_barrier((other, staged))
    inner = ((EVENTS, 512), F32)
    total, factor = call(
        inner_kernel,
        [inner, inner],
        (side, queries, keys, values, state_retention_log, boundary, both, own),
        scalars=1,
        flops=100_000_000,
        moved=1_500_000,
    )
    block = ((EVENTS, COLS), F32)
    two_blocks = ((2, EVENTS, COLS), F32)
    normed, opposite_send, opposite_mine = call(
        first_kernel,
        [((EVENTS, 512), BF16), block, block],
        (place, queries, total, factor, other, gain, staged),
        scalars=1,
        flops=230_000_000,
        moved=4_000_000,
    )

    def core_sum(mine, both):
        return call(core_sum_kernel, [block], (place, mine, both), scalars=1)[0]

    opposite_both = lax.all_gather(opposite_send, "tp", axis_index_groups=CORE_PAIRS)
    opposite = core_sum(opposite_mine, opposite_both)
    opposite, normed = lax.optimization_barrier((opposite, normed))
    ahead_got = lax.ppermute(opposite, "tp", ONWARD)
    behind_send, behind_mine = call(
        behind_kernel, [block, block], (place, normed, staged), scalars=1, flops=200_000_000, moved=2_500_000
    )
    behind_both = lax.all_gather(behind_send, "tp", axis_index_groups=CORE_PAIRS)
    behind = core_sum(behind_mine, behind_both)
    one = lax.ppermute(behind, "tp", BACK)
    two_blocks = ((2, EVENTS, COLS), F32)
    rest_send, rest_mine = call(rest_kernel, [two_blocks, two_blocks], (place, normed, staged), scalars=1)
    rest_got = lax.ppermute(rest_send, "tp", CORE_SWAP)
    (passed,) = call(ahead_kernel, [block], (rest_mine, rest_got, ahead_got))
    two = lax.ppermute(passed, "tp", ONWARD)
    (own_and_one,) = call(own_kernel, [block], (rest_mine, rest_got, one), moved=1_600_000)
    (out,) = call(final_kernel, [((EVENTS, COLS), BF16)], (own_and_one, two), moved=1_000_000)
    return out


def solution(mesh):
    in_specs = (
        P("ctx", "tp"),
        P("ctx", "tp"),
        P("ctx", "tp"),
        P("tp", "ctx"),
        P("ctx"),
        P("tp"),
        P("tp", None),
    )
    out_specs = P("ctx", "tp")
    return jax.shard_map(body, mesh=mesh, in_specs=in_specs, out_specs=out_specs, check_vma=False)
```

```python
import math

import jax
import jax.numpy as jnp
from jax import lax
from jax.experimental import pallas as pl
from jax.experimental.pallas import tpu as pltpu
from jax.sharding import PartitionSpec as P

HEAD_DIM = 128
EVENTS = 128
HEADS_DEV = 4
D = 6144
COLS = 768
PAIRS = 48
PIECES = PAIRS // HEADS_DEV
ROWS = 11
CHUNK = ROWS + 1
HEAD_ROWS = PIECES * CHUNK
PACKED = PAIRS * CHUNK
STATE_ROWS = HEADS_DEV * HEAD_DIM
SENT_ROWS = STATE_ROWS + 8

surge_log_factor = math.log(0.6)
F32 = jnp.float32
BF16 = jnp.bfloat16
VMEM_LIMIT = 24 * 1024 * 1024

SLOTS = [4 * z + x for x in range(4) for z in range(PAIRS // 4)]
SIDE_GROUPS = [[2 * SLOTS.index(slot) + side for slot in range(PAIRS)] for side in range(2)]
SIDE_SWAP = [(i, i ^ 1) for i in range(2 * PAIRS)]
SIDE_PAIRS = [[i, i + 1] for i in range(0, 2 * PAIRS, 2)]
CORE_SWAP = [(i, i ^ 1) for i in range(8)]
CORE_PAIRS = [[i, i + 1] for i in range(0, 8, 2)]
ONWARD = [(i, (i + (2 if i % 2 == 0 else 6)) % 8) for i in range(8)]
BACK = [(i, (i + (6 if i % 2 == 0 else 2)) % 8) for i in range(8)]


def piece_rows(piece):
    return min(ROWS, HEAD_DIM - ROWS * piece)


def call(kernel, outs, args, scalars=0, scratch=(), flops=0, moved=0, space=pltpu.VMEM, out_space=None):
    specs = [pl.BlockSpec(memory_space=pltpu.SMEM)] * scalars
    specs += [pl.BlockSpec(memory_space=space)] * (len(args) - scalars)
    if space is pltpu.HBM:
        args = args[:scalars] + tuple(pltpu.with_memory_space_constraint(x, space) for x in args[scalars:])
    shapes = [(out_space or jax.ShapeDtypeStruct)(shape, dtype) for shape, dtype in outs]
    return pl.pallas_call(
        kernel,
        out_shape=shapes,
        in_specs=specs,
        out_specs=[pl.BlockSpec(memory_space=out_space or pltpu.VMEM)] * len(outs),
        scratch_shapes=list(scratch),
        compiler_params=pltpu.CompilerParams(vmem_limit_bytes=VMEM_LIMIT),
        cost_estimate=pl.CostEstimate(flops=flops, bytes_accessed=moved, transcendentals=0),
    )(*args)


def event_sums(log_ref, boundary_ref):
    rate = log_ref[...] + surge_log_factor * boundary_ref[...].astype(F32)
    row = lax.broadcasted_iota(jnp.int32, (EVENTS, EVENTS), 0)
    column = lax.broadcasted_iota(jnp.int32, (EVENTS, EVENTS), 1)
    lower = (column <= row).astype(F32)
    upper = (row <= column).astype(F32)
    columns = lax.dot_general(
        lower, rate, (((1,), (1,)), ((), ())), precision=lax.Precision.HIGHEST, preferred_element_type=F32
    )
    return rate, columns, upper


def factors(side, columns):
    ends = columns[EVENTS - 1 : EVENTS, :]
    toward_end = jnp.exp(ends - columns)
    from_start = jnp.exp(columns)
    sent = jnp.where(side == 0, toward_end, from_start)
    kept = jnp.where(side == 0, from_start, toward_end)
    return ends, sent, kept


def halves(wide):
    high = wide.astype(BF16)
    low = (wide - high.astype(F32)).astype(BF16)
    return high, low


def terms_kernel(
    side_ref,
    key_hbm,
    value_hbm,
    log_hbm,
    boundary_hbm,
    sent_ref,
    kept_ref,
    decay_ref,
    key_ref,
    value_ref,
    log_ref,
    boundary_ref,
    sems,
):
    copies = [
        pltpu.make_async_copy(log_hbm, log_ref, sems.at[0]),
        pltpu.make_async_copy(boundary_hbm, boundary_ref, sems.at[1]),
        pltpu.make_async_copy(key_hbm, key_ref, sems.at[2]),
        pltpu.make_async_copy(value_hbm, value_ref, sems.at[3]),
    ]
    for copy in copies:
        copy.start()
    for copy in copies[:2]:
        copy.wait()
    _, columns, _ = event_sums(log_ref, boundary_ref)
    ends, sent, kept = factors(side_ref[0], columns)
    decay = jnp.exp(ends)
    for copy in copies[2:]:
        copy.wait()
    sent_ref[STATE_ROWS:, :] = jnp.zeros((SENT_ROWS - STATE_ROWS, HEAD_DIM), F32)
    for head in range(HEADS_DEV):
        lanes = slice(head * HEAD_DIM, (head + 1) * HEAD_DIM)
        value = value_ref[:, lanes].astype(F32)
        sides = halves(value * sent[:, head : head + 1]) + halves(value * kept[:, head : head + 1])
        product = lax.dot_general(
            key_ref[:, lanes],
            jnp.concatenate(sides, axis=1),
            (((0,), (0,)), ((), ())),
            preferred_element_type=F32,
        )
        sent_ref[lanes, :] = product[:, :128] + product[:, 128:256]
        kept_ref[lanes, :] = product[:, 256:384] + product[:, 384:]
        whole_row = jnp.broadcast_to(decay[:, head : head + 1], (1, HEAD_DIM))
        decay_ref[head : head + 1, :] = whole_row
        sent_ref[STATE_ROWS + head : STATE_ROWS + head + 1, :] = whole_row


def combine_kernel(side_ref, kept_ref, both_ref, decay_ref, out_ref):
    other = 1 - side_ref[0]
    for head in range(HEADS_DEV):
        decay = decay_ref[head : head + 1, :]
        rows = slice(head * HEAD_DIM, (head + 1) * HEAD_DIM)
        state = kept_ref[rows, :] + decay * both_ref[other, rows, :]
        last = STATE_ROWS + head
        decay = decay * both_ref[other, last : last + 1, :]
        for piece in range(PIECES):
            count, first = piece_rows(piece), head * HEAD_ROWS + piece * CHUNK
            part = [state[ROWS * piece : ROWS * piece + count]]
            if count < ROWS:
                part.append(jnp.zeros((ROWS - count, HEAD_DIM), F32))
            out_ref[first : first + CHUNK, :] = jnp.concatenate(part + [decay], axis=0)


def scan_kernel(side_ref, term_ref, out_ref):
    def run(pairs):
        state = jnp.zeros((CHUNK, HEAD_DIM), F32)
        for pair in pairs:
            slot = SLOTS[pair]
            out_ref[slot * ROWS : (slot + 1) * ROWS, :] = state[:ROWS]
            term = term_ref[slot * CHUNK : (slot + 1) * CHUNK, :]
            state = term[ROWS:, :] * state + term

    @pl.when(side_ref[0] == 1)
    def _():
        run(range(PAIRS))

    @pl.when(side_ref[0] == 0)
    def _():
        run(range(PAIRS - 1, -1, -1))


def state_rows(head):
    return slice(head * PIECES * ROWS, head * PIECES * ROWS + HEAD_DIM)


def times_state(query, state):
    product = jnp.dot(query, jnp.concatenate(halves(state), axis=1), preferred_element_type=F32)
    return product[:, :128] + product[:, 128:]


def inner_kernel(
    side_ref, query_ref, key_ref, value_ref, log_ref, boundary_ref, both_ref, own_ref, total_ref, factor_ref
):
    rate, columns, upper = event_sums(log_ref, boundary_ref)
    rows_cum = lax.dot_general(
        rate, upper, (((1,), (0,)), ((), ())), precision=lax.Precision.HIGHEST, preferred_element_type=F32
    )
    side = side_ref[0]
    _, own, other = factors(side, columns)
    for head in range(HEADS_DEV):
        lanes = slice(head * HEAD_DIM, (head + 1) * HEAD_DIM)
        query = query_ref[:, lanes]
        logits = lax.dot_general(
            query, key_ref[:, lanes], (((1,), (1,)), ((), ())), preferred_element_type=F32
        )
        weight = jnp.exp(-jnp.abs(columns[:, head : head + 1] - rows_cum[head : head + 1, :]))
        probs = (logits * weight).astype(BF16)
        intra = jnp.dot(probs, value_ref[:, lanes], preferred_element_type=F32)
        last = STATE_ROWS + head
        got_decay = both_ref[1 - side, last : last + 1, :]
        state = both_ref[1 - side, lanes, :] + got_decay * own_ref[state_rows(head), :]
        total_ref[:, lanes] = intra + own[:, head : head + 1] * times_state(query, state)
        factor_ref[:, lanes] = jnp.broadcast_to(other[:, head : head + 1], (EVENTS, HEAD_DIM))


def stage_kernel(w_hbm, staged_ref, sems):
    copies = [
        pltpu.make_async_copy(w_hbm.at[:, pl.ds(block * COLS, COLS)], staged_ref.at[block], sems.at[block])
        for block in range(D // COLS)
    ]
    for copy in copies:
        copy.start()
    for copy in copies:
        copy.wait()


def block_of(place, far, core):
    return 2 * (((place >> 1) + far) & 3) + core


def first_kernel(
    place_ref,
    query_ref,
    total_ref,
    factor_ref,
    other_ref,
    gain_ref,
    w_ref,
    normed_ref,
    opposite_send_ref,
    opposite_ref,
):
    for head in range(HEADS_DEV):
        lanes = slice(head * HEAD_DIM, (head + 1) * HEAD_DIM)
        total = total_ref[:, lanes] + factor_ref[:, lanes] * times_state(
            query_ref[:, lanes], other_ref[state_rows(head), :]
        )
        average = jnp.mean(total * total, axis=1, keepdims=True)
        scaled = total * lax.rsqrt(average + 1e-06) * gain_ref[:, lanes]
        normed_ref[:, lanes] = scaled.astype(BF16)
    place = place_ref[0]
    core = place & 1
    normed = normed_ref[...]
    for out_ref, whose in ((opposite_send_ref, 1 - core), (opposite_ref, core)):
        out_ref[...] = jnp.dot(normed, w_ref[block_of(place, 2, whose)], preferred_element_type=F32)


def behind_kernel(place_ref, normed_ref, w_ref, send_ref, mine_ref):
    place = place_ref[0]
    core = place & 1
    normed = normed_ref[...]
    for out_ref, whose in ((send_ref, 1 - core), (mine_ref, core)):
        out_ref[...] = jnp.dot(normed, w_ref[block_of(place, 3 - 2 * whose, whose)], preferred_element_type=F32)


def rest_kernel(place_ref, normed_ref, w_ref, ahead_send_ref, ahead_ref, own_send_ref, own_ref):
    place = place_ref[0]
    core = place & 1
    normed = normed_ref[...]
    for out_ref, far, whose in (
        (ahead_send_ref, 3 - 2 * core, 1 - core),
        (ahead_ref, 1 + 2 * core, core),
        (own_send_ref, 0, 1 - core),
        (own_ref, 0, core),
    ):
        out_ref[...] = jnp.dot(normed, w_ref[block_of(place, far, whose)], preferred_element_type=F32)


def core_sum_kernel(place_ref, mine_ref, both_ref, out_ref):
    out_ref[...] = mine_ref[...] + both_ref[1 - (place_ref[0] & 1)]


def three_kernel(place_ref, mine_ref, both_ref, more_ref, out_ref):
    out_ref[...] = mine_ref[...] + both_ref[1 - (place_ref[0] & 1)] + more_ref[...]


def final_kernel(one_ref, two_ref, out_ref):
    out_ref[...] = (one_ref[...] + two_ref[...]).astype(BF16)


def exchange_pieces(packed, shape):
    pieces = packed.reshape((PAIRS,) + shape + (HEAD_DIM,))
    pieces = lax.all_to_all(pieces, "ctx", 0, 0, axis_index_groups=SIDE_GROUPS)
    return pieces.reshape(packed.shape)


def body(queries, keys, values, state_retention_log, boundary, gain, w_out):
    side = (lax.axis_index("ctx") & 1).reshape(1)
    place = lax.axis_index("tp").reshape(1)
    boundary = boundary.reshape(1, EVENTS)
    gain = gain.reshape(1, 512)
    packed = ((PACKED, HEAD_DIM), F32)
    state = ((STATE_ROWS, HEAD_DIM), F32)

    sent, kept, decay = call(
        terms_kernel,
        [((SENT_ROWS, HEAD_DIM), F32), state, ((HEADS_DEV, HEAD_DIM), F32)],
        (side, keys, values, state_retention_log, boundary),
        scalars=1,
        scratch=[
            pltpu.VMEM((EVENTS, 512), BF16),
            pltpu.VMEM((EVENTS, 512), BF16),
            pltpu.VMEM((HEADS_DEV, EVENTS), F32),
            pltpu.VMEM((1, EVENTS), jnp.int32),
            pltpu.SemaphoreType.DMA((4,)),
        ],
        flops=70_000_000,
        moved=900_000,
        space=pltpu.HBM,
        out_space=pltpu.VMEM,
    )
    both = lax.all_gather(sent, "ctx", axis_index_groups=SIDE_PAIRS)
    (pair_terms,) = call(
        combine_kernel, [packed], (side, kept, both, decay), scalars=1, flops=200_000, moved=1_100_000
    )
    slices = exchange_pieces(pair_terms, (3, 4))
    returned = ((PAIRS * ROWS, HEAD_DIM), F32)
    (states,) = call(scan_kernel, [returned], (side, slices), scalars=1, flops=200_000, moved=600_000)
    own = exchange_pieces(states, (ROWS, 1))
    own, w_late = lax.optimization_barrier((own, w_out))
    other = lax.ppermute(own, "ctx", SIDE_SWAP)
    (staged,) = call(
        stage_kernel,
        [((D // COLS, 512, COLS), BF16)],
        (w_late,),
        scratch=[pltpu.SemaphoreType.DMA((D // COLS,))],
        moved=12_600_000,
        space=pltpu.HBM,
        out_space=pltpu.VMEM,
    )
    other, staged = lax.optimization_barrier((other, staged))
    inner = ((EVENTS, 512), F32)
    total, factor = call(
        inner_kernel,
        [inner, inner],
        (side, queries, keys, values, state_retention_log, boundary, both, own),
        scalars=1,
        flops=100_000_000,
        moved=1_500_000,
    )
    block = ((EVENTS, COLS), F32)
    two_blocks = ((2, EVENTS, COLS), F32)
    normed, opposite_send, opposite_mine = call(
        first_kernel,
        [((EVENTS, 512), BF16), block, block],
        (place, queries, total, factor, other, gain, staged),
        scalars=1,
        flops=230_000_000,
        moved=4_000_000,
    )

    def core_sum(mine, both):
        return call(core_sum_kernel, [block], (place, mine, both), scalars=1)[0]

    opposite_both = lax.all_gather(opposite_send, "tp", axis_index_groups=CORE_PAIRS)
    opposite = core_sum(opposite_mine, opposite_both)
    opposite, normed = lax.optimization_barrier((opposite, normed))
    ahead_got = lax.ppermute(opposite, "tp", ONWARD)
    behind_send, behind_mine = call(
        behind_kernel, [block, block], (place, normed, staged), scalars=1, flops=200_000_000, moved=2_500_000
    )
    behind_both = lax.all_gather(behind_send, "tp", axis_index_groups=CORE_PAIRS)
    behind_both, normed = lax.optimization_barrier((behind_both, normed))
    behind = core_sum(behind_mine, behind_both)
    ahead_send, ahead_mine, own_send, own_mine = call(
        rest_kernel, [block] * 4, (place, normed, staged), scalars=1, flops=400_000_000, moved=5_000_000
    )
    ahead_both = lax.all_gather(ahead_send, "tp", axis_index_groups=CORE_PAIRS)
    own_both = lax.all_gather(own_send, "tp", axis_index_groups=CORE_PAIRS)
    behind, ahead_both = lax.optimization_barrier((behind, ahead_both))
    one = lax.ppermute(behind, "tp", BACK)
    (passed,) = call(three_kernel, [block], (place, ahead_mine, ahead_both, ahead_got), scalars=1)
    two = lax.ppermute(passed, "tp", ONWARD)
    (own_and_one,) = call(three_kernel, [block], (place, own_mine, own_both, one), scalars=1, moved=1_600_000)
    (out,) = call(final_kernel, [((EVENTS, COLS), BF16)], (own_and_one, two), moved=1_000_000)
    return out


def solution(mesh):
    in_specs = (
        P("ctx", "tp"),
        P("ctx", "tp"),
        P("ctx", "tp"),
        P("tp", "ctx"),
        P("ctx"),
        P("tp"),
        P("tp", None),
    )
    out_specs = P("ctx", "tp")
    return jax.shard_map(body, mesh=mesh, in_specs=in_specs, out_specs=out_specs, check_vma=False)
```
